128 devices in a mesh: dp: 4 (over z), section: 2 (over core), seq: 16 (over x, y).
Axes of the slice: x: 4, y: 4, z: 4, core: 2. Of those that a mesh axis runs over, the one named last changes fastest.
Arguments:
- inputs: bfloat16 [2, 4, 2048, 1024], P(None, 'dp', 'seq'), may hold values from -6 to 6
- out_grad: bfloat16 [2, 4, 2048, 1024], P(None, 'dp', 'seq'), may hold values from -6 to 6
- norm_gain: bfloat16 [2, 1024], P('section', ('dp', 'seq')), may hold values from 0.5 to 1.5
- w_in: bfloat16 [2, 1024, 4384], P('section', ('dp', 'seq')), may hold values from -0.1875 to 0.1875
- conv_w: bfloat16 [2, 4, 2304], P('section', None, ('dp', 'seq')), may hold values from -3 to 3
- conv_b: bfloat16 [2, 2304], P('section', ('dp', 'seq')), may hold values from -3 to 3
- dt_bias: float32 [2, 32], P('section'), may hold values from -7 to -3
- a_log: float32 [2, 32], P('section'), may hold values from -1 to 2
- d_skip: float32 [2, 32], P('section'), may hold values from 0.25 to 1
- gnorm_gain: bfloat16 [2, 2048], P('section', ('dp', 'seq')), may hold values from 0.5 to 1.5
- w_out: bfloat16 [2, 2048, 1024], P('section', ('dp', 'seq')), may hold values from -0.125 to 0.125
Outputs:
- outputs: bfloat16 [2, 4, 2048, 1024], P(None, 'dp', 'seq', 'section')
- in_grad: float32 [2, 4, 2048, 1024], P(None, 'dp', 'seq', 'section')
- grad_norm_gain: float32 [2, 1024], P('section', ('dp', 'seq'))
- grad_w_in: float32 [2, 1024, 4384], P('section', ('dp', 'seq'))
- grad_conv_w: float32 [2, 4, 2304], P('section', None, ('dp', 'seq'))
- grad_conv_b: float32 [2, 2304], P('section', ('dp', 'seq'))
- grad_dt_bias: float32 [2, 32], P('section')
- grad_a_log: float32 [2, 32], P('section')
- grad_d_skip: float32 [2, 32], P('section')
- grad_gnorm_gain: float32 [2, 2048], P('section', ('dp', 'seq'))
- grad_w_out: float32 [2, 2048, 1024], P('section', ('dp', 'seq'))
The draws below stay inside these ranges and needn't reach their ends.
All inputs are finite; a program needn't handle non-finite values.
Results may differ from the reference program's by a relative error of at most 0.035.
Values may be sent and summed in bfloat16 or wider, within the bound.
No kernel may reach another device: no remote copies, remote signals or barrier semaphores. Data moves between devices by JAX's collectives and lax.ppermute only.
A program may use at most 256 MiB of HBM per device.

```python
import jax
import jax.numpy as jnp
from jax import lax

D = 1024
DIN = 2048
HEADS = 32
STATE = 128
KW = 4
STRETCH = 256
MICRO = 2
LEN = 2048
SEQS = 4
LAYERS = 2
EIN = 4384
CONV_CH = 2304


def block_levels(rng, extent, split, least, top_value):
    level, own = 1.0, jax.random.fold_in(rng, 6)
    for position, shards_of in split:
        draws = jnp.exp(jax.random.uniform(jax.random.fold_in(own, position), (shards_of,), jnp.float32, least / len(split), top_value / len(split)))
        level = level * jnp.repeat(draws, extent[position] // shards_of).reshape([-1 if axis == position else 1 for axis in range(len(extent))])
    return level


def normal_values(rng, shape, spread, most, cuts=(), held_as=jnp.bfloat16):
    entries = jax.random.normal(rng, shape, jnp.float32) * spread
    if len(cuts) > 0:
        entries = block_levels(rng, shape, cuts, -0.22, 0.18) * entries
    return jnp.clip(entries, min=-most, max=most).astype(held_as)


def setup_inputs(seed: int = 0) -> dict:
    key_of = jax.random.split(jax.random.key(seed), 12)
    return {
        "inputs": normal_values(key_of[0], (MICRO, SEQS, LEN, D), 1.0, 6.0, ((1, 4), (2, 16))),
        "out_grad": normal_values(key_of[1], (MICRO, SEQS, LEN, D), 1.0, 6.0, ((1, 4), (2, 16))),
        "norm_gain": jnp.clip(1.0 + 0.1 * jax.random.normal(key_of[2], (LAYERS, D), jnp.float32), 0.5, 1.5).astype(jnp.bfloat16),
        "w_in": normal_values(key_of[3], (LAYERS, D, EIN), D ** -0.5, 0.1875, ((0, 2), (1, 64))),
        "conv_w": normal_values(key_of[4], (LAYERS, KW, CONV_CH), KW ** -0.5, 3.0, ((0, 2), (2, 64))),
        "conv_b": normal_values(key_of[5], (LAYERS, CONV_CH), 0.5, 3.0, ((0, 2), (1, 64))),
        "dt_bias": jnp.clip(-7.0 + 4.0 * jax.random.uniform(key_of[6], (LAYERS, HEADS), jnp.float32) ** block_levels(key_of[6], (LAYERS, HEADS), ((0, 2),), -0.2, 0.2), -7.0, -3.0),
        "a_log": jnp.clip(-1.0 + 3.0 * jax.random.uniform(key_of[7], (LAYERS, HEADS), jnp.float32) ** block_levels(key_of[7], (LAYERS, HEADS), ((0, 2),), -0.2, 0.2), -1.0, 2.0),
        "d_skip": jnp.clip(0.25 + 0.75 * jax.random.uniform(key_of[8], (LAYERS, HEADS), jnp.float32) ** block_levels(key_of[8], (LAYERS, HEADS), ((0, 2),), -0.2, 0.2), 0.25, 1.0),
        "gnorm_gain": jnp.clip(1.0 + 0.1 * jax.random.normal(key_of[9], (LAYERS, DIN), jnp.float32), 0.5, 1.5).astype(jnp.bfloat16),
        "w_out": normal_values(key_of[10], (LAYERS, DIN, D), DIN ** -0.5, 0.125, ((0, 2), (1, 64))),
    }


@jax.custom_vjp
def low(v):
    return lax.optimization_barrier(v.astype(jnp.bfloat16)).astype(jnp.float32)

@jax.custom_vjp
def low_back(v):
    return v

def low_keep(v):
    return (low(v), None)

def low_pass(kept, grad):
    return (grad,)

def back_keep(v):
    return (v, None)

def back_low(kept, grad):
    return (low(grad),)
low.defvjp(low_keep, low_pass)
low_back.defvjp(back_keep, back_low)
epsilon = 1e-05
highest = lax.Precision.HIGHEST

def causal_conv(values, kernel, offsets):
    taps = kernel.shape[0]
    length = values.shape[0]
    padded = jnp.pad(values, ((taps - 1, 0), (0, 0)))
    summed = offsets[None, :] + kernel[0][None, :] * padded[0:length]
    for tap_index in range(1, taps):
        summed = summed + kernel[tap_index][None, :] * padded[tap_index:tap_index + length]
    return summed

def state_space(inputs_x, delta, rate, keys_b, queries_c, block):
    length, heads, width = inputs_x.shape
    states = keys_b.shape[1]
    blocks = length // block
    values = inputs_x.reshape(blocks, block, heads, width)
    deltas = delta.reshape(blocks, block, heads)
    keys = keys_b.reshape(blocks, block, states)
    queries = queries_c.reshape(blocks, block, states)
    cumulative = jnp.cumsum(deltas * rate[None, None, :], axis=1)
    scores = jnp.einsum('cln,csn->cls', queries, keys, precision=highest)
    row_ids = lax.broadcasted_iota(jnp.int32, (block, block), 0)
    column_ids = lax.broadcasted_iota(jnp.int32, (block, block), 1)
    causal = (row_ids >= column_ids)[None, :, :, None]
    log_gaps = cumulative[:, :, None, :] - cumulative[:, None, :, :]
    decays = jnp.where(causal, jnp.exp(jnp.where(causal, log_gaps, 0.0)), 0.0)
    mixing = scores[:, :, :, None] * decays * deltas[:, None, :, :]
    within = jnp.einsum('clsh,cshp->clhp', mixing, values, precision=highest)
    to_end = jnp.exp(cumulative[:, -1:, :] - cumulative) * deltas
    block_states = jnp.einsum('csn,cshp->chnp', keys, to_end[:, :, :, None] * values, precision=highest)
    totals = jnp.exp(cumulative[:, -1, :])

    def carry_step(carried, pieces):
        factor, added = pieces
        return (factor[:, None, None] * carried + added, carried)
    initial = jnp.zeros((heads, states, width), inputs_x.dtype)
    _, entering = lax.scan(carry_step, initial, (totals, block_states))
    across = jnp.einsum('cln,chnp->clhp', queries, entering, precision=highest) * jnp.exp(cumulative)[:, :, :, None]
    return (within + across).reshape(length, heads, width)

def mixer(x_raw, dt_raw, bc_raw, x_kernel, x_offset, bc_kernel, bc_offset, bias, log_rate, skip):
    length = x_raw.shape[0]
    heads = dt_raw.shape[1]
    x_conv = jax.nn.silu(causal_conv(x_raw, x_kernel, x_offset))
    bc_conv = jax.nn.silu(causal_conv(bc_raw, bc_kernel, bc_offset))
    states = bc_conv.shape[1] // 2
    delta = jax.nn.softplus(dt_raw + bias[None, :])
    rate = -jnp.exp(log_rate)
    inputs_x = x_conv.reshape(length, heads, -1)
    result = state_space(inputs_x, delta, rate, bc_conv[:, :states], bc_conv[:, states:], STRETCH)
    result = result + skip[None, :, None] * inputs_x
    return result.reshape(length, -1)

def pre_norm(stream, gain):
    inverse_rms = lax.rsqrt(lax.optimization_barrier(jnp.mean(stream * stream, axis=-1, keepdims=True)) + epsilon)
    return stream * inverse_rms * gain[None, :]

def post_norm(mixed, gate_part, gain):
    gated = mixed * jax.nn.silu(gate_part)
    inverse_rms = lax.rsqrt(lax.optimization_barrier(jnp.mean(gated * gated, axis=-1, keepdims=True)) + epsilon)
    return gated * inverse_rms * gain[None, :]

def layer(stream, norm_gain, w_in, conv_w, conv_b, dt_bias, a_log, d_skip, gnorm_gain, w_out):
    hidden = low(pre_norm(stream, norm_gain))
    projected = low_back(low(jnp.dot(hidden, w_in, precision=highest, preferred_element_type=jnp.float32)))
    gate_part = projected[:, :DIN]
    x_raw = projected[:, DIN:2 * DIN]
    bc_raw = projected[:, 2 * DIN:2 * DIN + 2 * STATE]
    dt_raw = projected[:, 2 * DIN + 2 * STATE:]
    mixed = mixer(x_raw, dt_raw, bc_raw, conv_w[:, :DIN], conv_b[:DIN], conv_w[:, DIN:], conv_b[DIN:], dt_bias, a_log, d_skip)
    mixed = low_back(low(mixed))
    normed = low(post_norm(mixed, gate_part, gnorm_gain))
    branch = low_back(jnp.dot(normed, w_out, precision=highest, preferred_element_type=jnp.float32))
    return stream + branch

def reference(inputs, out_grad, norm_gain, w_in, conv_w, conv_b, dt_bias, a_log, d_skip, gnorm_gain, w_out):
    params = tuple((tensor.astype(jnp.float32) for tensor in (norm_gain, w_in, conv_w, conv_b, dt_bias, a_log, d_skip, gnorm_gain, w_out)))
    sequences = inputs.astype(jnp.float32).reshape(MICRO * SEQS, LEN, D)
    cotangent = out_grad.astype(jnp.float32).reshape(MICRO * SEQS, LEN, D)

    def forward(weight_set, batch):

        def whole(sequence):
            for layer_index in range(LAYERS):
                sequence = layer(sequence, *[tensor[layer_index] for tensor in weight_set])
            return sequence
        return lax.map(jax.checkpoint(whole), batch)
    result, pullback = jax.vjp(forward, params, sequences)
    weight_grads, input_grads = pullback(cotangent)
    return (result.reshape(MICRO, SEQS, LEN, D).astype(jnp.bfloat16), input_grads.reshape(MICRO, SEQS, LEN, D), weight_grads[0], weight_grads[1], weight_grads[2], weight_grads[3], weight_grads[4], weight_grads[5], weight_grads[6], weight_grads[7], weight_grads[8])
```

```python
import jax
import jax.numpy as jnp
from jax import lax
from jax.experimental import pallas as pl
from jax.experimental.pallas import tpu as pltpu
from jax.sharding import PartitionSpec as P

DIN = 2048
HEADS = 32
STATE = 128
KW = 4
EIN = 4384
EINP = 4480
CONV_CH = 2304
DT_COL = 2 * DIN + 2 * STATE
T = 128
PAIRS = 16
PAY = STATE + 16

f32 = jnp.float32
bf16 = jnp.bfloat16
epsilon = 1e-05
highest = lax.Precision.HIGHEST
both = ("dp", "seq")


def dot(a, b, precision=None):
    return jnp.dot(a, b, preferred_element_type=f32, precision=precision)


def dot_nt(a, b):
    return lax.dot_general(a, b, (((1,), (1,)), ((), ())), preferred_element_type=f32)


def dot_tn(a, b):
    return lax.dot_general(a, b, (((0,), (0,)), ((), ())), preferred_element_type=f32)


def low_half():
    return lax.broadcasted_iota(jnp.int32, (1, T), 1) < 64


def lower_triangle():
    rows = lax.broadcasted_iota(jnp.int32, (T, T), 0)
    columns = lax.broadcasted_iota(jnp.int32, (T, T), 1)
    return rows >= columns


def sigmoid(v):
    return 1.0 / (1.0 + jnp.exp(-v))


def silu_and_slope(v):
    s = sigmoid(v)
    return v * s, s * (1.0 + v * (1.0 - s))


def spread(table, j):
    return jnp.where(low_half(), table[:, 2 * j : 2 * j + 1], table[:, 2 * j + 1 : 2 * j + 2])


def block(j):
    return slice(j * T, (j + 1) * T)


def conv_block(padded, taps, j):
    total = taps[KW : KW + 1, block(j)] + taps[0:1, block(j)] * padded[13 : 13 + T, block(j)]
    for k in range(1, KW):
        total = total + taps[k : k + 1, block(j)] * padded[13 + k : 13 + k + T, block(j)]
    return total


def load_padded(padded, projected, halo):
    padded[0:16, :] = halo[...].astype(f32)
    padded[16 : 16 + T, :] = projected[:, DIN:DT_COL].astype(f32)


def put_payload(payload, j, state, totals):
    payload[j, 0:STATE, :] = state.astype(bf16)
    factor = spread(totals, j)
    high = factor.astype(bf16).astype(f32)
    rest = factor - high
    row = lax.broadcasted_iota(jnp.int32, (16, T), 0)
    extra = jnp.where(row == 0, high, jnp.where(row == 1, rest, 0.0))
    payload[j, STATE:PAY, :] = extra.astype(bf16)


def front_kernel(projected, halo, taps, heads, xs, bc, delta, cum, payload, padded):
    load_padded(padded, projected, halo)
    lane = lax.broadcasted_iota(jnp.int32, (1, T), 1)
    raw = projected[:, DT_COL:EINP].astype(f32) + heads[0:1, :]
    soft = jnp.maximum(raw, 0.0) + jnp.log1p(jnp.exp(-jnp.abs(raw)))
    steps = jnp.where(lane < HEADS, soft, 0.0)
    delta[...] = steps
    logs = steps * -jnp.exp(heads[1:2, :])
    sums = dot(lower_triangle().astype(f32), logs, highest)
    cum[...] = sums
    last = sums[T - 1 : T, :]
    weight = jnp.exp(last - sums) * steps
    totals = jnp.exp(last)
    b_pre = conv_block(padded, taps, PAIRS)
    c_pre = conv_block(padded, taps, PAIRS + 1)
    keys = b_pre * sigmoid(b_pre)
    bc[:, 0:STATE] = keys.astype(bf16)
    bc[:, STATE:] = (c_pre * sigmoid(c_pre)).astype(bf16)
    keys_t = keys.T.astype(bf16)
    for j in range(PAIRS):
        pre = conv_block(padded, taps, j)
        x = pre * sigmoid(pre)
        xs[:, block(j)] = x
        put_payload(payload, j, dot(keys_t, (spread(weight, j) * x).astype(bf16)), totals)


def scan_kernel(backward, payload, entering):
    carried = jnp.zeros((STATE, T), f32)
    order = range(PAIRS - 1, -1, -1) if backward else range(PAIRS)
    for k in order:
        entering[k] = carried.astype(bf16)
        extra = payload[k, STATE:PAY, :].astype(f32)
        factor = extra[0:1, :] + extra[1:2, :]
        carried = factor * carried + payload[k, 0:STATE, :].astype(f32)


def decay(cum, cum_t, h, causal):
    return jnp.where(causal, jnp.exp(cum[:, h : h + 1] - cum_t[h : h + 1, :]), 0.0)


def halves(v):
    return jnp.concatenate(
        [jnp.where(low_half(), v, 0.0), jnp.where(low_half(), 0.0, v)], axis=0
    ).astype(bf16)


def within_kernel(xs, bc, delta, cum, heads, local):
    causal = lower_triangle()
    cums = cum[...]
    cum_t = cums.T
    steps = delta[...]
    skips = heads[2:3, :]
    scores = dot_nt(bc[:, STATE:], bc[:, 0:STATE])
    for j in range(PAIRS):
        x = xs[:, block(j)]
        mixing = jnp.concatenate(
            [scores * decay(cums, cum_t, 2 * j + i, causal) for i in range(2)], axis=1
        ).astype(bf16)
        local[:, block(j)] = dot(mixing, halves(spread(steps, j) * x)) + spread(skips, j) * x


def finish_kernel(local, bc, cum, entering, projected, gain, mixed, normed, gated):
    growth = jnp.exp(cum[...])
    queries = bc[:, STATE:]
    squares = jnp.zeros((T, T), f32)
    for j in range(PAIRS):
        whole = local[:, block(j)] + spread(growth, j) * dot(queries, entering[j])
        rounded = whole.astype(bf16)
        mixed[:, block(j)] = rounded
        gate = projected[:, block(j)].astype(f32)
        u = rounded.astype(f32) * (gate * sigmoid(gate))
        gated[:, block(j)] = u
        squares = squares + u * u
    scale = lax.rsqrt(jnp.sum(squares, axis=1, keepdims=True) / DIN + epsilon)
    for j in range(PAIRS):
        normed[:, block(j)] = (gated[:, block(j)] * scale * gain[0:1, block(j)]).astype(bf16)


def top_kernel(
    upstream, mixed, projected, gain, bc, cum, d_mixed, d_gate, d_gain, payload, gated
):
    squares = jnp.zeros((T, T), f32)
    products = jnp.zeros((T, T), f32)
    for j in range(PAIRS):
        gate = projected[:, block(j)].astype(f32)
        u = mixed[:, block(j)].astype(f32) * (gate * sigmoid(gate))
        gated[:, block(j)] = u
        squares = squares + u * u
        products = products + upstream[:, block(j)] * gain[0:1, block(j)] * u
    scale = lax.rsqrt(jnp.sum(squares, axis=1, keepdims=True) / DIN + epsilon)
    pull = scale * scale * scale * (jnp.sum(products, axis=1, keepdims=True) / DIN)
    cums = cum[...]
    growth = jnp.exp(cums)
    totals = growth[T - 1 : T, :]
    queries_t = bc[:, STATE:].astype(f32).T.astype(bf16)
    for j in range(PAIRS):
        gate = projected[:, block(j)].astype(f32)
        act, slope = silu_and_slope(gate)
        u = gated[:, block(j)]
        up = upstream[:, block(j)]
        d_gain[:, block(j)] = jnp.broadcast_to(
            jnp.sum(up * u * scale, axis=0, keepdims=True), (8, T)
        )
        du = up * gain[0:1, block(j)] * scale - u * pull
        dm = (du * act).astype(bf16)
        d_mixed[:, block(j)] = dm
        d_gate[:, block(j)] = (du * mixed[:, block(j)].astype(f32) * slope).astype(bf16)
        put_payload(
            payload, j, dot(queries_t, (spread(growth, j) * dm.astype(f32)).astype(bf16)), totals
        )


def inner_kernel(xs, bc, delta, cum, d_mixed, entering, d_scaled, d_bc, d_cum, rows, columns):
    causal = lower_triangle()
    cums = cum[...]
    cum_t = cums.T
    steps = delta[...]
    growth = jnp.exp(cums)
    keys = bc[:, 0:STATE]
    queries = bc[:, STATE:]
    scores = dot_nt(queries, keys)
    rows[...] = jnp.zeros((T, T), f32)
    columns[...] = jnp.zeros((T, T), f32)
    d_scores = jnp.zeros((T, T), f32)
    d_queries = jnp.zeros((T, STATE), f32)
    for j in range(PAIRS):
        dy_low = d_mixed[:, block(j)]
        dy = dy_low.astype(f32)
        scaled = halves(spread(steps, j) * xs[:, block(j)])
        d_mixing = dot_nt(dy_low, scaled)
        grown = spread(growth, j) * dy
        across = grown * dot(queries, entering[j])
        d_queries = d_queries + dot_nt(grown.astype(bf16), entering[j])
        mixings = []
        for i in range(2):
            h = 2 * j + i
            fall = decay(cums, cum_t, h, causal)
            d_part = d_mixing[:, i * T : (i + 1) * T] * fall
            d_scores = d_scores + d_part
            mixings.append(scores * fall)
            logs = d_part * scores
            own = jnp.where(low_half(), across, 0.0) if i == 0 else jnp.where(low_half(), 0.0, across)
            rows[:, h : h + 1] = jnp.sum(logs + own, axis=1, keepdims=True)
            columns[h : h + 1, :] = jnp.sum(logs, axis=0, keepdims=True)
        d_scaled[:, block(j)] = dot_tn(
            jnp.concatenate(mixings, axis=0).astype(bf16), halves(dy)
        )
    d_low = d_scores.astype(bf16)
    d_bc[:, 0:STATE] = dot_tn(d_low, queries)
    d_bc[:, STATE:] = d_queries + dot(d_low, keys)
    d_cum[...] = rows[...] - columns[...].T


def outer_kernel(
    projected, halo, taps, heads, xs, bc, delta, cum, d_mixed, d_scaled, d_bc, d_cum, entering,
    leaving, d_conv, d_dt, d_taps, d_heads, padded, falls, direct, rest,
):
    load_padded(padded, projected, halo)
    lane = lax.broadcasted_iota(jnp.int32, (1, T), 1)
    cums = cum[...]
    steps = delta[...]
    last = cums[T - 1 : T, :]
    weight = jnp.exp(last - cums)
    totals = jnp.exp(last)
    skips = heads[2:3, :]
    keys = bc[:, 0:STATE]
    falls[...] = jnp.zeros((T, T), f32)
    direct[...] = jnp.zeros((T, T), f32)
    rest[...] = jnp.zeros((8, T), f32)
    low = low_half()

    def conv_back(j, grad):
        pre = conv_block(padded, taps, j)
        d_pre = grad * silu_and_slope(pre)[1]
        d_conv[:, block(j)] = d_pre
        for k in range(KW):
            d_taps[k : k + 1, block(j)] = jnp.sum(
                d_pre * padded[13 + k : 13 + k + T, block(j)], axis=0, keepdims=True
            )
        d_taps[KW : KW + 1, block(j)] = jnp.sum(d_pre, axis=0, keepdims=True)

    d_taps[KW + 1 : 8, :] = jnp.zeros((8 - KW - 1, CONV_CH), f32)
    d_keys = d_bc[:, 0:STATE]
    for j in range(PAIRS):
        x = xs[:, block(j)]
        dy = d_mixed[:, block(j)].astype(f32)
        step = spread(steps, j)
        fall = spread(weight, j)
        weighted = fall * (step * x)
        back = dot(keys, leaving[j])
        d_keys = d_keys + dot_nt(weighted.astype(bf16), leaving[j])
        ds = d_scaled[:, block(j)] + fall * back
        flow = weighted * back
        touch = ds * x
        kept = jnp.sum(leaving[j].astype(f32) * entering[j].astype(f32), axis=0, keepdims=True)
        kept = kept * spread(totals, j)
        skipped = jnp.sum(dy * x, axis=0, keepdims=True)
        for i in range(2):
            h = 2 * j + i
            pick = (lambda v: jnp.where(low, v, 0.0)) if i == 0 else (lambda v: jnp.where(low, 0.0, v))
            falls[:, h : h + 1] = jnp.sum(pick(flow), axis=1, keepdims=True)
            direct[:, h : h + 1] = jnp.sum(pick(touch), axis=1, keepdims=True)
            rest[0:1, h : h + 1] = jnp.sum(pick(kept), axis=1, keepdims=True)
            rest[1:2, h : h + 1] = jnp.sum(pick(skipped), axis=1, keepdims=True)
        conv_back(j, step * ds + spread(skips, j) * dy)
    conv_back(PAIRS, d_keys)
    conv_back(PAIRS + 1, d_bc[:, STATE:])
    flows = falls[...]
    gained = rest[0:1, :] + jnp.sum(flows, axis=0, keepdims=True)
    row = lax.broadcasted_iota(jnp.int32, (T, T), 0)
    d_sums = d_cum[...] - flows + jnp.where(row == T - 1, gained, 0.0)
    upper = lower_triangle().astype(f32).T
    d_logs = dot(upper, d_sums, highest)
    rate = -jnp.exp(heads[1:2, :])
    d_delta = direct[...] + d_logs * rate
    slope = sigmoid(projected[:, DT_COL:EINP].astype(f32) + heads[0:1, :])
    grad = jnp.where(lane < HEADS, d_delta * slope, 0.0)
    d_dt[...] = grad
    d_heads[...] = jnp.zeros((8, T), f32)
    d_heads[0:1, :] = jnp.sum(grad, axis=0, keepdims=True)
    d_heads[1:2, :] = jnp.sum(d_logs * steps, axis=0, keepdims=True) * rate
    d_heads[2:3, :] = rest[1:2, :]


def bottom_kernel(d_conv, halo, taps, d_gate, d_dt, d_projected, padded):
    padded[0:T, :] = d_conv[...]
    padded[T : T + 8, :] = halo[...]
    d_projected[:, 0:DIN] = d_gate[...]
    for j in range(CONV_CH // T):
        total = taps[KW - 1 : KW, block(j)] * padded[0:T, block(j)]
        for k in range(KW - 1):
            shift = KW - 1 - k
            total = total + taps[k : k + 1, block(j)] * padded[shift : shift + T, block(j)]
        d_projected[:, DIN + j * T : DIN + (j + 1) * T] = total.astype(bf16)
    d_projected[:, DT_COL:EINP] = d_dt[...].astype(bf16)


def call(kernel, outs, scratch, name, *args):
    return pl.pallas_call(
        kernel,
        out_shape=[jax.ShapeDtypeStruct(shape, dtype) for shape, dtype in outs],
        scratch_shapes=[pltpu.VMEM(shape, f32) for shape in scratch],
        compiler_params=pltpu.CompilerParams(vmem_limit_bytes=40 * 2**20),
        name=name,
    )(*args)


def swap(value):
    return lax.ppermute(value, "section", [(0, 1), (1, 0)])


def turned(value, axis, steps):
    if axis == "z":
        return lax.ppermute(value, "dp", [(i, (i + steps) % 4) for i in range(4)])
    pairs = []
    for i in range(16):
        x, y = divmod(i, 4)
        if axis == "x":
            pairs.append((i, (x + steps) % 4 * 4 + y))
        else:
            pairs.append((i, x * 4 + (y + steps) % 4))
    return lax.ppermute(value, "seq", pairs)


def coordinate(axis):
    if axis == "z":
        return lax.axis_index("dp")
    seq = lax.axis_index("seq")
    return seq // 4 if axis == "x" else seq % 4


def summed_over(value, order):
    names = ["z", "x", "y"]
    for axis in order:
        at = names.index(axis)
        names.pop(at)
        me = coordinate(axis)

        def piece(steps):
            return lax.dynamic_index_in_dim(value, (me + steps) % 4, at, keepdims=False)

        total = piece(0).astype(f32)
        for steps in (1, -1, 2):
            total = total + turned(piece(steps), axis, steps).astype(f32)
        value = total.astype(bf16)
    return value


def reduced(grad, rows, cuts):
    columns = grad.shape[1]
    shaped = grad.reshape(64, 2, rows // 2, columns)
    section = lax.axis_index("section")
    mine = lax.dynamic_index_in_dim(shaped, section, 1, keepdims=False)
    theirs = lax.dynamic_index_in_dim(shaped, 1 - section, 1, keepdims=False)
    total = (mine.astype(f32) + swap(theirs).astype(f32)).astype(bf16)
    total = total.reshape(4, 4, 4, rows // 2, columns)
    pieces = []
    for order, (start, stop) in zip(("zxy", "xyz", "yzx"), cuts):
        pieces.append(summed_over(total[..., start:stop], order))
    return jnp.concatenate(pieces, axis=-1)


def own_layer(halves_of, first):
    keep = jnp.where(first, halves_of[0], halves_of[1])
    give = jnp.where(first, halves_of[1], halves_of[0])
    came = swap(give.astype(f32))
    keep = keep.astype(f32)
    return jnp.where(
        first, jnp.concatenate([keep, came], axis=0), jnp.concatenate([came, keep], axis=0)
    )


def exchange(payload, backward):
    moved = lax.all_to_all(payload, "seq", split_axis=0, concat_axis=0, tiled=True)
    (entering,) = call(
        lambda *refs: scan_kernel(backward, *refs),
        [((PAIRS, STATE, T), bf16)],
        [],
        "scan_back" if backward else "scan",
        moved,
    )
    return lax.all_to_all(entering, "seq", split_axis=0, concat_axis=0, tiled=True)


def forward_layer(stream, w):
    inverse = lax.rsqrt(jnp.mean(stream * stream, axis=-1, keepdims=True) + epsilon)
    hidden = (stream * inverse * w["norm"]).astype(bf16)
    projected = dot(hidden, w["w_in"]).astype(bf16)
    halo = lax.ppermute(
        projected[T - 16 :, DIN:DT_COL], "seq", [(i, i + 1) for i in range(15)]
    )
    xs, bc, delta, cum, payload = call(
        front_kernel,
        [((T, DIN), f32), ((T, 2 * STATE), bf16), ((T, T), f32), ((T, T), f32), ((PAIRS, PAY, T), bf16)],
        [(T + 16, CONV_CH)],
        "front",
        projected,
        halo,
        w["taps"],
        w["heads"],
    )
    entering = exchange(payload, False)
    (local,) = call(within_kernel, [((T, DIN), f32)], [], "within", xs, bc, delta, cum, w["heads"])
    mixed, normed = call(
        finish_kernel,
        [((T, DIN), bf16), ((T, DIN), bf16)],
        [(T, DIN)],
        "finish",
        local,
        bc,
        cum,
        entering,
        projected,
        w["gnorm"],
    )
    result = stream + dot(normed, w["w_out"])
    return (stream, hidden, projected, halo, xs, bc, delta, cum, entering, mixed, normed), result


def backward_layer(kept, upstream, w):
    stream, hidden, projected, halo, xs, bc, delta, cum, entering, mixed, normed = kept
    upstream_low = upstream.astype(bf16)
    d_normed = dot_nt(upstream_low, w["w_out"])
    grad_out = dot_tn(normed, upstream_low).astype(bf16)
    d_mixed, d_gate, d_gain, payload = call(
        top_kernel,
        [((T, DIN), bf16), ((T, DIN), bf16), ((8, DIN), f32), ((PAIRS, PAY, T), bf16)],
        [(T, DIN)],
        "top",
        d_normed,
        mixed,
        projected,
        w["gnorm"],
        bc,
        cum,
    )
    leaving = exchange(payload, True)
    d_scaled, d_bc, d_cum = call(
        inner_kernel,
        [((T, DIN), f32), ((T, 2 * STATE), f32), ((T, T), f32)],
        [(T, T), (T, T)],
        "inner",
        xs,
        bc,
        delta,
        cum,
        d_mixed,
        entering,
    )
    d_conv, d_dt, d_taps, d_heads = call(
        outer_kernel,
        [((T, CONV_CH), f32), ((T, T), f32), ((8, CONV_CH), f32), ((8, T), f32)],
        [(T + 16, CONV_CH), (T, T), (T, T), (8, T)],
        "outer",
        projected,
        halo,
        w["taps"],
        w["heads"],
        xs,
        bc,
        delta,
        cum,
        d_mixed,
        d_scaled,
        d_bc,
        d_cum,
        entering,
        leaving,
    )
    halo_back = lax.ppermute(d_conv[0:8], "seq", [(i + 1, i) for i in range(15)])
    (d_projected,) = call(
        bottom_kernel,
        [((T, EINP), bf16)],
        [(T + 8, CONV_CH)],
        "bottom",
        d_conv,
        halo_back,
        w["taps"],
        d_gate,
        d_dt,
    )
    grad_in = dot_tn(hidden, d_projected).astype(bf16)
    d_hidden = dot_nt(d_projected, w["w_in"])
    inverse = lax.rsqrt(jnp.mean(stream * stream, axis=-1, keepdims=True) + epsilon)
    grad_norm = jnp.sum(d_hidden * stream * inverse, axis=0)
    scaled = d_hidden * w["norm"]
    pull = inverse * inverse * inverse * jnp.mean(scaled * stream, axis=-1, keepdims=True)
    result = upstream + scaled * inverse - stream * pull
    small = pack_small(grad_norm, d_taps, d_gain[0], d_heads)
    return result, grad_in, grad_out, small


def pack_small(grad_norm, d_taps, d_gain, d_heads):
    def padded(v):
        return jnp.pad(v, ((0, 0), (0, T - v.shape[1])))

    rows = [padded(d_taps[k].reshape(64, 36)) for k in range(KW + 1)]
    rows.append(padded(grad_norm.reshape(64, 16)))
    rows.append(padded(d_gain.reshape(64, 32)))
    heads = d_heads[0:3, 0:HEADS].reshape(1, 3 * HEADS)
    rows.append(jnp.broadcast_to(padded(heads), (64, T)))
    return jnp.stack(rows, axis=1)


def gathered_weights(norm_gain, w_in, conv_w, conv_b, dt_bias, a_log, d_skip, gnorm_gain, w_out):
    def tail(v):
        return jnp.pad(v, ((0, 0), (0, T - v.shape[1])))

    small = jnp.concatenate(
        [tail(conv_w[0]), tail(conv_b), tail(norm_gain), tail(gnorm_gain), jnp.zeros((9, T), bf16)],
        axis=0,
    )
    payload = jnp.concatenate(
        [jnp.pad(w_in[0], ((0, 0), (0, EINP - EIN))), w_out[0, 0:16], w_out[0, 16:32], small], axis=1
    )
    whole = lax.all_gather(payload, ("section", "dp", "seq"), axis=0, tiled=True)
    whole = whole.reshape(2, 64, 16, payload.shape[1])
    heads = jnp.pad(jnp.concatenate([dt_bias, a_log, d_skip], axis=0), ((0, 5), (0, T - HEADS)))
    other = swap(heads)
    first = lax.axis_index("section") == 0
    layers = []
    for l in range(2):
        part = whole[l]
        out = part[:, :, EINP : EINP + 2048].reshape(64, 16, 2, 1024)
        tiny = part[:, :, EINP + 2048 :]
        taps = jnp.stack([tiny[:, k, :36].reshape(CONV_CH) for k in range(KW + 1)]).astype(f32)
        layers.append(
            {
                "w_in": part[:, :, :EINP].reshape(1024, EINP),
                "w_out": jnp.swapaxes(out, 1, 2).reshape(DIN, 1024),
                "taps": jnp.pad(taps, ((0, 8 - KW - 1), (0, 0))),
                "norm": tiny[:, 5, :16].reshape(1, 1024).astype(f32),
                "gnorm": tiny[:, 6, :32].reshape(1, DIN).astype(f32),
                "heads": jnp.where(first == (l == 0), heads, other),
            }
        )
    return layers


def shards(
    inputs, out_grad, norm_gain, w_in, conv_w, conv_b, dt_bias, a_log, d_skip, gnorm_gain, w_out
):
    section = lax.axis_index("section")
    first = section == 0
    layers = gathered_weights(
        norm_gain, w_in, conv_w, conv_b, dt_bias, a_log, d_skip, gnorm_gain, w_out
    )
    stream = lax.dynamic_index_in_dim(inputs, section, 0, keepdims=False)[0].astype(f32)
    g = lax.dynamic_index_in_dim(out_grad, section, 0, keepdims=False)[0].astype(f32)
    kept = []
    for l in range(2):
        saved, stream = forward_layer(stream, layers[l])
        kept.append(saved)
    outputs = stream.astype(bf16)
    in_halves, out_halves, smalls = [None, None], [None, None], [None, None]
    for l in (1, 0):
        g, grad_in, grad_out, smalls[l] = backward_layer(kept[l], g, layers[l])
        out_halves[l] = reduced(grad_out, 32, ((0, 384), (384, 768), (768, 1024)))
        in_halves[l] = reduced(grad_in, 16, ((0, 1536), (1536, 3072), (3072, EINP)))
    grad_w_in = own_layer(in_halves, first)[:, :EIN]
    grad_w_out = own_layer(out_halves, first)
    small = jnp.where(first, smalls[0], smalls[1]) + swap(jnp.where(first, smalls[1], smalls[0]))
    small = jnp.sum(lax.all_to_all(small, both, split_axis=0, concat_axis=0, tiled=True), axis=0)

    half = outputs.shape[1] // 2

    def by_features(value):
        low, high = value[:, :half], value[:, half:]
        came = swap(jnp.where(first, high, low).astype(bf16)).astype(value.dtype)
        keep = jnp.where(first, low, high)
        return jnp.where(first, jnp.stack([keep, came]), jnp.stack([came, keep]))[:, None]

    return (
        by_features(outputs),
        by_features(g),
        small[5:6, :16],
        grad_w_in[None],
        small[None, 0:KW, :36],
        small[KW : KW + 1, :36],
        small[7:8, 0:HEADS],
        small[7:8, HEADS : 2 * HEADS],
        small[7:8, 2 * HEADS : 3 * HEADS],
        small[6:7, :32],
        grad_w_out[None],
    )


def solution(mesh):
    in_specs = (
        P(None, "dp", "seq", None),
        P(None, "dp", "seq", None),
        P("section", both),
        P("section", both, None),
        P("section", None, both),
        P("section", both),
        P("section", None),
        P("section", None),
        P("section", None),
        P("section", both),
        P("section", both, None),
    )
    out_specs = (
        P(None, "dp", "seq", "section"),
        P(None, "dp", "seq", "section"),
        P("section", both),
        P("section", both, None),
        P("section", None, both),
        P("section", both),
        P("section", None),
        P("section", None),
        P("section", None),
        P("section", both),
        P("section", both, None),
    )
    return jax.shard_map(shards, mesh=mesh, in_specs=in_specs, out_specs=out_specs, check_vma=False)
```

```python
import jax
import jax.numpy as jnp
from jax import lax
from jax.experimental import pallas as pl
from jax.experimental.pallas import tpu as pltpu
from jax.sharding import PartitionSpec as P

DIN = 2048
HEADS = 32
STATE = 128
KW = 4
EIN = 4384
EINP = 4480
CONV_CH = 2304
DT_COL = 2 * DIN + 2 * STATE
T = 128
D = 1024
TILE = 896
CUT = 2304
PAIRS = 16
PAY = STATE + 16

f32 = jnp.float32
bf16 = jnp.bfloat16
epsilon = 1e-05
highest = lax.Precision.HIGHEST
both = ("dp", "seq")


def dot(a, b, precision=None):
    return jnp.dot(a, b, preferred_element_type=f32, precision=precision)


def dot_nt(a, b):
    return lax.dot_general(a, b, (((1,), (1,)), ((), ())), preferred_element_type=f32)


def dot_tn(a, b):
    return lax.dot_general(a, b, (((0,), (0,)), ((), ())), preferred_element_type=f32)


def low_half():
    return lax.broadcasted_iota(jnp.int32, (1, T), 1) < 64


def lower_triangle():
    rows = lax.broadcasted_iota(jnp.int32, (T, T), 0)
    columns = lax.broadcasted_iota(jnp.int32, (T, T), 1)
    return rows >= columns


def sigmoid(v):
    return 1.0 / (1.0 + jnp.exp(-v))


def silu_and_slope(v):
    s = sigmoid(v)
    return v * s, s * (1.0 + v * (1.0 - s))


def spread(table, j):
    return jnp.where(low_half(), table[:, 2 * j : 2 * j + 1], table[:, 2 * j + 1 : 2 * j + 2])


def block(j):
    return slice(j * T, (j + 1) * T)


def conv_block(padded, taps, j):
    total = taps[KW : KW + 1, block(j)] + taps[0:1, block(j)] * padded[13 : 13 + T, block(j)]
    for k in range(1, KW):
        total = total + taps[k : k + 1, block(j)] * padded[13 + k : 13 + k + T, block(j)]
    return total


def load_padded(padded, projected, halo):
    padded[0:16, :] = halo[...].astype(f32)
    padded[16 : 16 + T, :] = projected[:, DIN:DT_COL].astype(f32)


def put_payload(payload, j, state, totals):
    payload[j, 0:STATE, :] = state.astype(bf16)
    factor = spread(totals, j)
    high = factor.astype(bf16).astype(f32)
    rest = factor - high
    row = lax.broadcasted_iota(jnp.int32, (16, T), 0)
    extra = jnp.where(row == 0, high, jnp.where(row == 1, rest, 0.0))
    payload[j, STATE:PAY, :] = extra.astype(bf16)


def front_kernel(projected, halo, taps, heads, xs, bc, delta, cum, payload, padded):
    load_padded(padded, projected, halo)
    lane = lax.broadcasted_iota(jnp.int32, (1, T), 1)
    raw = projected[:, DT_COL:EINP].astype(f32) + heads[0:1, :]
    soft = jnp.maximum(raw, 0.0) + jnp.log1p(jnp.exp(-jnp.abs(raw)))
    steps = jnp.where(lane < HEADS, soft, 0.0)
    delta[...] = steps
    logs = steps * -jnp.exp(heads[1:2, :])
    sums = dot(lower_triangle().astype(f32), logs, highest)
    cum[...] = sums
    last = sums[T - 1 : T, :]
    weight = jnp.exp(last - sums) * steps
    totals = jnp.exp(last)
    b_pre = conv_block(padded, taps, PAIRS)
    c_pre = conv_block(padded, taps, PAIRS + 1)
    keys = b_pre * sigmoid(b_pre)
    bc[:, 0:STATE] = keys.astype(bf16)
    bc[:, STATE:] = (c_pre * sigmoid(c_pre)).astype(bf16)
    keys_t = keys.T.astype(bf16)
    for j in range(PAIRS):
        pre = conv_block(padded, taps, j)
        x = pre * sigmoid(pre)
        xs[:, block(j)] = x
        put_payload(payload, j, dot(keys_t, (spread(weight, j) * x).astype(bf16)), totals)


def scan_kernel(backward, payload, entering):
    carried = jnp.zeros((STATE, T), f32)
    order = range(PAIRS - 1, -1, -1) if backward else range(PAIRS)
    for k in order:
        entering[k] = carried.astype(bf16)
        extra = payload[k, STATE:PAY, :].astype(f32)
        factor = extra[0:1, :] + extra[1:2, :]
        carried = factor * carried + payload[k, 0:STATE, :].astype(f32)


def decay(cum, cum_t, h, causal):
    return jnp.where(causal, jnp.exp(cum[:, h : h + 1] - cum_t[h : h + 1, :]), 0.0)


def halves(v):
    return jnp.concatenate(
        [jnp.where(low_half(), v, 0.0), jnp.where(low_half(), 0.0, v)], axis=0
    ).astype(bf16)


def within_kernel(xs, bc, delta, cum, heads, local):
    causal = lower_triangle()
    cums = cum[...]
    cum_t = cums.T
    steps = delta[...]
    skips = heads[2:3, :]
    scores = dot_nt(bc[:, STATE:], bc[:, 0:STATE])
    for j in range(PAIRS):
        x = xs[:, block(j)]
        mixing = jnp.concatenate(
            [scores * decay(cums, cum_t, 2 * j + i, causal) for i in range(2)], axis=1
        ).astype(bf16)
        local[:, block(j)] = dot(mixing, halves(spread(steps, j) * x)) + spread(skips, j) * x


def project_kernel(stream, gain, weight, hidden, projected):
    @pl.when(pl.program_id(0) == 0)
    def _():
        values = stream[...]
        inverse = lax.rsqrt(jnp.sum(values * values, axis=1, keepdims=True) / D + epsilon)
        hidden[...] = (values * inverse * gain[...]).astype(bf16)

    projected[...] = dot(hidden[...], weight[...]).astype(bf16)


def finish_kernel(
    local, bc, cum, entering, projected, gain, stream, weight, mixed, normed, result, gated
):
    @pl.when(pl.program_id(0) == 0)
    def _():
        growth = jnp.exp(cum[...])
        queries = bc[:, STATE:]
        squares = jnp.zeros((T, T), f32)
        for j in range(PAIRS):
            whole = local[:, block(j)] + spread(growth, j) * dot(queries, entering[j])
            rounded = whole.astype(bf16)
            mixed[:, block(j)] = rounded
            gate = projected[:, block(j)].astype(f32)
            u = rounded.astype(f32) * (gate * sigmoid(gate))
            gated[:, block(j)] = u
            squares = squares + u * u
        scale = lax.rsqrt(jnp.sum(squares, axis=1, keepdims=True) / DIN + epsilon)
        for j in range(PAIRS):
            normed[:, block(j)] = (gated[:, block(j)] * scale * gain[0:1, block(j)]).astype(bf16)

    result[...] = stream[...] + dot(normed[...], weight[...])


def top_kernel(
    upstream, weight, mixed, projected, gain, bc, cum, d_mixed, d_gate, d_gain, payload, d_normed,
    gated,
):
    step = pl.program_id(0)
    d_normed[step] = dot_nt(upstream[...], weight[...])

    def part(j):
        return d_normed[j // 4, :, block(j % 4)]

    @pl.when(step == 3)
    def _():
        squares = jnp.zeros((T, T), f32)
        products = jnp.zeros((T, T), f32)
        for j in range(PAIRS):
            gate = projected[:, block(j)].astype(f32)
            u = mixed[:, block(j)].astype(f32) * (gate * sigmoid(gate))
            gated[:, block(j)] = u
            squares = squares + u * u
            products = products + part(j) * gain[0:1, block(j)] * u
        scale = lax.rsqrt(jnp.sum(squares, axis=1, keepdims=True) / DIN + epsilon)
        pull = scale * scale * scale * (jnp.sum(products, axis=1, keepdims=True) / DIN)
        cums = cum[...]
        growth = jnp.exp(cums)
        totals = growth[T - 1 : T, :]
        queries_t = bc[:, STATE:].astype(f32).T.astype(bf16)
        for j in range(PAIRS):
            gate = projected[:, block(j)].astype(f32)
            act, slope = silu_and_slope(gate)
            u = gated[:, block(j)]
            up = part(j)
            d_gain[:, block(j)] = jnp.broadcast_to(
                jnp.sum(up * u * scale, axis=0, keepdims=True), (8, T)
            )
            du = up * gain[0:1, block(j)] * scale - u * pull
            dm = (du * act).astype(bf16)
            d_mixed[:, block(j)] = dm
            d_gate[:, block(j)] = (du * mixed[:, block(j)].astype(f32) * slope).astype(bf16)
            put_payload(
                payload, j, dot(queries_t, (spread(growth, j) * dm.astype(f32)).astype(bf16)), totals
            )


def inner_kernel(xs, bc, delta, cum, d_mixed, entering, d_scaled, d_bc, d_cum, rows, columns):
    causal = lower_triangle()
    cums = cum[...]
    cum_t = cums.T
    steps = delta[...]
    growth = jnp.exp(cums)
    keys = bc[:, 0:STATE]
    queries = bc[:, STATE:]
    scores = dot_nt(queries, keys)
    rows[...] = jnp.zeros((T, T), f32)
    columns[...] = jnp.zeros((T, T), f32)
    d_scores = jnp.zeros((T, T), f32)
    d_queries = jnp.zeros((T, STATE), f32)
    for j in range(PAIRS):
        dy_low = d_mixed[:, block(j)]
        dy = dy_low.astype(f32)
        scaled = halves(spread(steps, j) * xs[:, block(j)])
        d_mixing = dot_nt(dy_low, scaled)
        grown = spread(growth, j) * dy
        across = grown * dot(queries, entering[j])
        d_queries = d_queries + dot_nt(grown.astype(bf16), entering[j])
        mixings = []
        for i in range(2):
            h = 2 * j + i
            fall = decay(cums, cum_t, h, causal)
            d_part = d_mixing[:, i * T : (i + 1) * T] * fall
            d_scores = d_scores + d_part
            mixings.append(scores * fall)
            logs = d_part * scores
            own = jnp.where(low_half(), across, 0.0) if i == 0 else jnp.where(low_half(), 0.0, across)
            rows[:, h : h + 1] = jnp.sum(logs + own, axis=1, keepdims=True)
            columns[h : h + 1, :] = jnp.sum(logs, axis=0, keepdims=True)
        d_scaled[:, block(j)] = dot_tn(
            jnp.concatenate(mixings, axis=0).astype(bf16), halves(dy)
        )
    d_low = d_scores.astype(bf16)
    d_bc[:, 0:STATE] = dot_tn(d_low, queries)
    d_bc[:, STATE:] = d_queries + dot(d_low, keys)
    d_cum[...] = rows[...] - columns[...].T


def outer_kernel(
    projected, halo, taps, heads, xs, bc, delta, cum, d_mixed, d_scaled, d_bc, d_cum, entering,
    leaving, d_conv, d_dt, d_taps, d_heads, padded, falls, direct, rest,
):
    load_padded(padded, projected, halo)
    lane = lax.broadcasted_iota(jnp.int32, (1, T), 1)
    cums = cum[...]
    steps = delta[...]
    last = cums[T - 1 : T, :]
    weight = jnp.exp(last - cums)
    totals = jnp.exp(last)
    skips = heads[2:3, :]
    keys = bc[:, 0:STATE]
    falls[...] = jnp.zeros((T, T), f32)
    direct[...] = jnp.zeros((T, T), f32)
    rest[...] = jnp.zeros((8, T), f32)
    low = low_half()

    def conv_back(j, grad):
        pre = conv_block(padded, taps, j)
        d_pre = grad * silu_and_slope(pre)[1]
        d_conv[:, block(j)] = d_pre
        for k in range(KW):
            d_taps[k : k + 1, block(j)] = jnp.sum(
                d_pre * padded[13 + k : 13 + k + T, block(j)], axis=0, keepdims=True
            )
        d_taps[KW : KW + 1, block(j)] = jnp.sum(d_pre, axis=0, keepdims=True)

    d_taps[KW + 1 : 8, :] = jnp.zeros((8 - KW - 1, CONV_CH), f32)
    d_keys = d_bc[:, 0:STATE]
    for j in range(PAIRS):
        x = xs[:, block(j)]
        dy = d_mixed[:, block(j)].astype(f32)
        step = spread(steps, j)
        fall = spread(weight, j)
        weighted = fall * (step * x)
        back = dot(keys, leaving[j])
        d_keys = d_keys + dot_nt(weighted.astype(bf16), leaving[j])
        ds = d_scaled[:, block(j)] + fall * back
        flow = weighted * back
        touch = ds * x
        kept = jnp.sum(leaving[j].astype(f32) * entering[j].astype(f32), axis=0, keepdims=True)
        kept = kept * spread(totals, j)
        skipped = jnp.sum(dy * x, axis=0, keepdims=True)
        for i in range(2):
            h = 2 * j + i
            pick = (lambda v: jnp.where(low, v, 0.0)) if i == 0 else (lambda v: jnp.where(low, 0.0, v))
            falls[:, h : h + 1] = jnp.sum(pick(flow), axis=1, keepdims=True)
            direct[:, h : h + 1] = jnp.sum(pick(touch), axis=1, keepdims=True)
            rest[0:1, h : h + 1] = jnp.sum(pick(kept), axis=1, keepdims=True)
            rest[1:2, h : h + 1] = jnp.sum(pick(skipped), axis=1, keepdims=True)
        conv_back(j, step * ds + spread(skips, j) * dy)
    conv_back(PAIRS, d_keys)
    conv_back(PAIRS + 1, d_bc[:, STATE:])
    flows = falls[...]
    gained = rest[0:1, :] + jnp.sum(flows, axis=0, keepdims=True)
    row = lax.broadcasted_iota(jnp.int32, (T, T), 0)
    d_sums = d_cum[...] - flows + jnp.where(row == T - 1, gained, 0.0)
    upper = lower_triangle().astype(f32).T
    d_logs = dot(upper, d_sums, highest)
    rate = -jnp.exp(heads[1:2, :])
    d_delta = direct[...] + d_logs * rate
    slope = sigmoid(projected[:, DT_COL:EINP].astype(f32) + heads[0:1, :])
    grad = jnp.where(lane < HEADS, d_delta * slope, 0.0)
    d_dt[...] = grad
    d_heads[...] = jnp.zeros((8, T), f32)
    d_heads[0:1, :] = jnp.sum(grad, axis=0, keepdims=True)
    d_heads[1:2, :] = jnp.sum(d_logs * steps, axis=0, keepdims=True) * rate
    d_heads[2:3, :] = rest[1:2, :]


def bottom_kernel(
    d_conv, halo, taps, d_gate, d_dt, weight, stream, norm, upstream, d_projected, result, d_norm,
    padded, total,
):
    step = pl.program_id(0)

    @pl.when(step == 0)
    def _():
        padded[0:T, :] = d_conv[...]
        padded[T : T + 8, :] = halo[...]
        d_projected[:, 0:DIN] = d_gate[...]
        for j in range(CONV_CH // T):
            value = taps[KW - 1 : KW, block(j)] * padded[0:T, block(j)]
            for k in range(KW - 1):
                shift = KW - 1 - k
                value = value + taps[k : k + 1, block(j)] * padded[shift : shift + T, block(j)]
            d_projected[:, DIN + j * T : DIN + (j + 1) * T] = value.astype(bf16)
        d_projected[:, DT_COL:EINP] = d_dt[...].astype(bf16)
        total[...] = jnp.zeros((T, D), f32)

    columns = pl.ds(pl.multiple_of(step * TILE, T), TILE)
    total[...] += dot_nt(d_projected[:, columns], weight[...])

    @pl.when(step == EINP // TILE - 1)
    def _():
        values = stream[...]
        d_hidden = total[...]
        inverse = lax.rsqrt(jnp.sum(values * values, axis=1, keepdims=True) / D + epsilon)
        d_norm[...] = jnp.broadcast_to(
            jnp.sum(d_hidden * values * inverse, axis=0, keepdims=True), (8, D)
        )
        scaled = d_hidden * norm[...]
        mean = jnp.sum(scaled * values, axis=1, keepdims=True) / D
        pull = inverse * inverse * inverse * mean
        result[...] = upstream[...] + scaled * inverse - values * pull


def dropping(kernel, count, extra):
    return lambda *refs: kernel(*refs[:count], *refs[count + extra :])


def call(kernel, outs, scratch, name, micros, *args, after=()):
    return pl.pallas_call(
        dropping(kernel, len(args), len(after)),
        out_shape=[jax.ShapeDtypeStruct(shape, dtype) for shape, dtype in outs],
        scratch_shapes=[pltpu.VMEM(shape, f32) for shape in scratch],
        compiler_params=pltpu.CompilerParams(vmem_limit_bytes=40 * 2**20),
        in_specs=[pl.BlockSpec(memory_space=pltpu.VMEM)] * len(args)
        + [pl.BlockSpec(memory_space=pl.ANY)] * len(after),
        cost_estimate=cost(micros),
        name=name,
    )(*args, *after)


def cost(micros):
    return pl.CostEstimate(flops=0, transcendentals=0, bytes_accessed=int(micros * 3.5e6))


def whole(array):
    rank = len(array.shape)
    return pl.BlockSpec(array.shape, lambda n: (0,) * rank)


def call_tiled(kernel, steps, args, specs, outs, scratch, name, micros, after=()):
    shapes = [jax.ShapeDtypeStruct(shape, dtype) for shape, dtype, _ in outs]
    return pl.pallas_call(
        dropping(kernel, len(args), len(after)),
        grid=(steps,),
        in_specs=[whole(v) if spec is None else spec for v, spec in zip(args, specs)]
        + [pl.BlockSpec(memory_space=pl.ANY) for _ in after],
        out_specs=[whole(v) if o[2] is None else o[2] for v, o in zip(shapes, outs)],
        out_shape=shapes,
        scratch_shapes=[pltpu.VMEM(shape, f32) for shape in scratch],
        compiler_params=pltpu.CompilerParams(vmem_limit_bytes=44 * 2**20),
        cost_estimate=cost(micros),
        name=name,
    )(*args, *after)


def swap(value):
    return lax.ppermute(value, "section", [(0, 1), (1, 0)])


def to_owners(value):
    came = lax.all_to_all(value, "seq", split_axis=0, concat_axis=0, tiled=True)
    return jnp.sum(came.astype(f32), axis=0)


def to_layers(value):
    me = lax.axis_index("dp")

    def piece(steps):
        return lax.dynamic_index_in_dim(value, (me + steps) % 4, 0, keepdims=False)

    total = piece(0).astype(f32)
    for steps in (1, -1, 2):
        moved = lax.ppermute(piece(steps), "dp", [(i, (i + steps) % 4) for i in range(4)])
        total = total + moved.astype(f32)
    return total


def seq_first(value):
    return to_layers(to_owners(jnp.swapaxes(value, 0, 1)).astype(bf16))


def dp_first(value):
    return to_owners(to_layers(value).astype(bf16))


def in_chip(grad, rows):
    columns = grad.shape[1]
    shaped = grad.reshape(64, 2, rows // 2, columns)
    section = lax.axis_index("section")
    mine = lax.dynamic_index_in_dim(shaped, section, 1, keepdims=False)
    theirs = lax.dynamic_index_in_dim(shaped, 1 - section, 1, keepdims=False)
    total = (mine.astype(f32) + swap(theirs).astype(f32)).astype(bf16)
    return total.reshape(4, 16, rows // 2, columns)


def reduced_in(total):
    return jnp.concatenate([dp_first(total[..., :CUT]), seq_first(total[..., CUT:])], axis=-1)


def own_layer(halves_of, first):
    keep = jnp.where(first, halves_of[0], halves_of[1])
    give = jnp.where(first, halves_of[1], halves_of[0])
    came = swap(give.astype(f32))
    keep = keep.astype(f32)
    return jnp.where(
        first, jnp.concatenate([keep, came], axis=0), jnp.concatenate([came, keep], axis=0)
    )


def exchange(payload, backward):
    moved = lax.all_to_all(payload, "seq", split_axis=0, concat_axis=0, tiled=True)
    (entering,) = call(
        lambda *refs: scan_kernel(backward, *refs),
        [((PAIRS, STATE, T), bf16)],
        [],
        "scan_back" if backward else "scan",
        2,
        moved,
    )
    return lax.all_to_all(entering, "seq", split_axis=0, concat_axis=0, tiled=True)


def forward_layer(stream, w):
    l = w["layer"]
    hidden, projected = call_tiled(
        project_kernel,
        EINP // TILE,
        (stream, w["norm"], w["w_in"]),
        (None, None, pl.BlockSpec((D, TILE), lambda n: (l, n))),
        [((T, D), bf16, None), ((T, EINP), bf16, pl.BlockSpec((T, TILE), lambda n: (0, n)))],
        [],
        "project",
        4,
    )
    halo = lax.ppermute(
        projected[T - 16 :, DIN:DT_COL], "seq", [(i, i + 1) for i in range(15)]
    )
    xs, bc, delta, cum, payload = call(
        front_kernel,
        [((T, DIN), f32), ((T, 2 * STATE), bf16), ((T, T), f32), ((T, T), f32), ((PAIRS, PAY, T), bf16)],
        [(T + 16, CONV_CH)],
        "front",
        2,
        projected,
        halo,
        w["taps"],
        w["heads"],
    )
    entering = exchange(payload, False)
    (local,) = call(within_kernel, [((T, DIN), f32)], [], "within", 2, xs, bc, delta, cum, w["heads"])
    narrow = pl.BlockSpec((T, 512), lambda n: (0, n))
    mixed, normed, result = call_tiled(
        finish_kernel,
        2,
        (local, bc, cum, entering, projected, w["gnorm"], stream, w["w_out"]),
        (None,) * 6 + (narrow, pl.BlockSpec((DIN, 512), lambda n: (l, n))),
        [((T, DIN), bf16, None), ((T, DIN), bf16, None), ((T, D), f32, narrow)],
        [(T, DIN)],
        "finish",
        5,
    )
    return (stream, hidden, projected, halo, xs, bc, delta, cum, entering, mixed, normed), result


def backward_layer(kept, upstream, w, earlier=None):
    stream, hidden, projected, halo, xs, bc, delta, cum, entering, mixed, normed = kept
    upstream_low = upstream.astype(bf16)
    l = w["layer"]
    d_mixed, d_gate, d_gain, payload = call_tiled(
        top_kernel,
        4,
        (upstream_low, w["w_out"], mixed, projected, w["gnorm"], bc, cum),
        (None, pl.BlockSpec((512, D), lambda n: (4 * l + n, 0))) + (None,) * 5,
        [
            ((T, DIN), bf16, None),
            ((T, DIN), bf16, None),
            ((8, DIN), f32, None),
            ((PAIRS, PAY, T), bf16, None),
        ],
        [(4, T, 512), (T, DIN)],
        "top",
        5,
    )
    grad_out = dot_tn(normed, upstream_low).astype(bf16)
    leaving = exchange(payload, True)
    out_total = in_chip(grad_out, 32)
    grad_out = to_layers(out_total).astype(bf16)
    ordered = (grad_out,)
    if earlier is not None:
        leaving, earlier = lax.optimization_barrier((leaving, earlier))
        ordered = (grad_out, earlier)
    d_scaled, d_bc, d_cum = call(
        inner_kernel,
        [((T, DIN), f32), ((T, 2 * STATE), f32), ((T, T), f32)],
        [(T, T), (T, T)],
        "inner",
        8,
        xs,
        bc,
        delta,
        cum,
        d_mixed,
        entering,
    )
    d_conv, d_dt, d_taps, d_heads = call(
        outer_kernel,
        [((T, CONV_CH), f32), ((T, T), f32), ((8, CONV_CH), f32), ((8, T), f32)],
        [(T + 16, CONV_CH), (T, T), (T, T), (8, T)],
        "outer",
        5,
        projected,
        halo,
        w["taps"],
        w["heads"],
        xs,
        bc,
        delta,
        cum,
        d_mixed,
        d_scaled,
        d_bc,
        d_cum,
        entering,
        leaving,
        after=(out_total,),
    )
    halo_back = lax.ppermute(d_conv[0:8], "seq", [(i + 1, i) for i in range(15)])
    d_projected, result, d_norm = call_tiled(
        bottom_kernel,
        EINP // TILE,
        (d_conv, halo_back, w["taps"], d_gate, d_dt, w["w_in"], stream, w["norm"], upstream),
        (None,) * 5 + (pl.BlockSpec((D, TILE), lambda n: (l, n)),) + (None,) * 3,
        [((T, EINP), bf16, None), ((T, D), f32, None), ((8, D), f32, None)],
        [(T + 8, CONV_CH), (T, D)],
        "bottom",
        6,
        ordered,
    )
    grad_in = dot_tn(hidden, d_projected).astype(bf16)
    small = pack_small(d_norm[0], d_taps, d_gain[0], d_heads)
    return result, grad_in, grad_out, small, earlier


def pack_small(grad_norm, d_taps, d_gain, d_heads):
    def padded(v):
        return jnp.pad(v, ((0, 0), (0, T - v.shape[1])))

    rows = [padded(d_taps[k].reshape(64, 36)) for k in range(KW + 1)]
    rows.append(padded(grad_norm.reshape(64, 16)))
    rows.append(padded(d_gain.reshape(64, 32)))
    heads = d_heads[0:3, 0:HEADS].reshape(1, 3 * HEADS)
    rows.append(jnp.broadcast_to(padded(heads), (64, T)))
    return jnp.stack(rows, axis=1)


def gathered_weights(norm_gain, w_in, conv_w, conv_b, dt_bias, a_log, d_skip, gnorm_gain, w_out):
    def tail(v):
        return jnp.pad(v, ((0, 0), (0, T - v.shape[1])))

    small = jnp.concatenate(
        [tail(conv_w[0]), tail(conv_b), tail(norm_gain), tail(gnorm_gain), jnp.zeros((9, T), bf16)],
        axis=0,
    )
    payload = jnp.concatenate([jnp.pad(w_in[0], ((0, 0), (0, EINP - EIN))), small], axis=1)
    everywhere = ("section", "dp", "seq")
    all_in = lax.all_gather(payload, everywhere, axis=0, tiled=True)
    all_out = lax.all_gather(w_out[0], everywhere, axis=0, tiled=True)
    tiny = all_in[:, EINP:].reshape(2, 64, 16, T)
    heads = jnp.pad(jnp.concatenate([dt_bias, a_log, d_skip], axis=0), ((0, 5), (0, T - HEADS)))
    other = swap(heads)
    first = lax.axis_index("section") == 0
    layers = []
    for l in range(2):
        part = tiny[l]
        taps = jnp.stack([part[:, k, :36].reshape(CONV_CH) for k in range(KW + 1)]).astype(f32)
        layers.append(
            {
                "layer": l,
                "w_in": all_in,
                "w_out": all_out,
                "taps": jnp.pad(taps, ((0, 8 - KW - 1), (0, 0))),
                "norm": part[:, 5, :16].reshape(1, 1024).astype(f32),
                "gnorm": part[:, 6, :32].reshape(1, DIN).astype(f32),
                "heads": jnp.where(first == (l == 0), heads, other),
            }
        )
    return layers


def shards(
    inputs, out_grad, norm_gain, w_in, conv_w, conv_b, dt_bias, a_log, d_skip, gnorm_gain, w_out
):
    section = lax.axis_index("section")
    first = section == 0
    layers = gathered_weights(
        norm_gain, w_in, conv_w, conv_b, dt_bias, a_log, d_skip, gnorm_gain, w_out
    )
    stream = lax.dynamic_index_in_dim(inputs, section, 0, keepdims=False)[0].astype(f32)
    g = lax.dynamic_index_in_dim(out_grad, section, 0, keepdims=False)[0].astype(f32)
    kept = []
    for l in range(2):
        saved, stream = forward_layer(stream, layers[l])
        kept.append(saved)
    outputs = stream.astype(bf16)
    g, grad_in, out_1, small_1, _ = backward_layer(kept[1], g, layers[1])
    in_1 = to_layers(in_chip(grad_in, 16)).astype(bf16)
    g, grad_in, out_0, small_0, in_1 = backward_layer(kept[0], g, layers[0], in_1)
    in_1 = to_owners(in_1)
    outs = to_owners(jnp.concatenate([out_0, out_1], axis=1))
    in_1, small_0, small_1 = lax.optimization_barrier((in_1, small_0, small_1))
    smalls = (small_0, small_1)
    in_halves = (reduced_in(in_chip(grad_in, 16)), in_1)
    out_halves = (outs[0:16], outs[16:32])
    grad_w_in = own_layer(in_halves, first)[:, :EIN]
    grad_w_out = own_layer(out_halves, first)
    small = jnp.where(first, smalls[0], smalls[1]) + swap(jnp.where(first, smalls[1], smalls[0]))
    small = jnp.sum(lax.all_to_all(small, both, split_axis=0, concat_axis=0, tiled=True), axis=0)

    half = outputs.shape[1] // 2

    def by_features(value):
        low, high = value[:, :half], value[:, half:]
        came = swap(jnp.where(first, high, low).astype(bf16)).astype(value.dtype)
        keep = jnp.where(first, low, high)
        return jnp.where(first, jnp.stack([keep, came]), jnp.stack([came, keep]))[:, None]

    return (
        by_features(outputs),
        by_features(g),
        small[5:6, :16],
        grad_w_in[None],
        small[None, 0:KW, :36],
        small[KW : KW + 1, :36],
        small[7:8, 0:HEADS],
        small[7:8, HEADS : 2 * HEADS],
        small[7:8, 2 * HEADS : 3 * HEADS],
        small[6:7, :32],
        grad_w_out[None],
    )


def solution(mesh):
    in_specs = (
        P(None, "dp", "seq", None),
        P(None, "dp", "seq", None),
        P("section", both),
        P("section", both, None),
        P("section", None, both),
        P("section", both),
        P("section", None),
        P("section", None),
        P("section", None),
        P("section", both),
        P("section", both, None),
    )
    out_specs = (
        P(None, "dp", "seq", "section"),
        P(None, "dp", "seq", "section"),
        P("section", both),
        P("section", both, None),
        P("section", None, both),
        P("section", both),
        P("section", None),
        P("section", None),
        P("section", None),
        P("section", both),
        P("section", both, None),
    )
    return jax.shard_map(shards, mesh=mesh, in_specs=in_specs, out_specs=out_specs, check_vma=False)
```

```python
import jax
import jax.numpy as jnp
from jax import lax
from jax.experimental import pallas as pl
from jax.experimental.pallas import tpu as pltpu
from jax.sharding import PartitionSpec as P

DIN = 2048
HEADS = 32
STATE = 128
KW = 4
EIN = 4384
EINP = 4480
CONV_CH = 2304
DT_COL = 2 * DIN + 2 * STATE
T = 128
D = 1024
TILE = 896
PAIRS = 16
PAY = STATE + 16

f32 = jnp.float32
bf16 = jnp.bfloat16
epsilon = 1e-05
highest = lax.Precision.HIGHEST
both = ("dp", "seq")


def dot(a, b, precision=None):
    return jnp.dot(a, b, preferred_element_type=f32, precision=precision)


def dot_nt(a, b):
    return lax.dot_general(a, b, (((1,), (1,)), ((), ())), preferred_element_type=f32)


def dot_tn(a, b):
    return lax.dot_general(a, b, (((0,), (0,)), ((), ())), preferred_element_type=f32)


def low_half():
    return lax.broadcasted_iota(jnp.int32, (1, T), 1) < 64


def lower_triangle():
    rows = lax.broadcasted_iota(jnp.int32, (T, T), 0)
    columns = lax.broadcasted_iota(jnp.int32, (T, T), 1)
    return rows >= columns


def sigmoid(v):
    return 1.0 / (1.0 + jnp.exp(-v))


def silu_and_slope(v):
    s = sigmoid(v)
    return v * s, s * (1.0 + v * (1.0 - s))


def spread(table, j):
    return jnp.where(low_half(), table[:, 2 * j : 2 * j + 1], table[:, 2 * j + 1 : 2 * j + 2])


def block(j):
    return slice(j * T, (j + 1) * T)


def conv_block(padded, taps, j):
    total = taps[KW : KW + 1, block(j)] + taps[0:1, block(j)] * padded[13 : 13 + T, block(j)]
    for k in range(1, KW):
        total = total + taps[k : k + 1, block(j)] * padded[13 + k : 13 + k + T, block(j)]
    return total


def load_padded(padded, projected, halo):
    padded[0:16, :] = halo[...].astype(f32)
    padded[16 : 16 + T, :] = projected[:, DIN:DT_COL].astype(f32)


def put_payload(payload, j, state, totals):
    payload[j, 0:STATE, :] = state.astype(bf16)
    factor = spread(totals, j)
    high = factor.astype(bf16).astype(f32)
    rest = factor - high
    row = lax.broadcasted_iota(jnp.int32, (16, T), 0)
    extra = jnp.where(row == 0, high, jnp.where(row == 1, rest, 0.0))
    payload[j, STATE:PAY, :] = extra.astype(bf16)


def front_kernel(projected, halo, taps, heads, xs, bc, delta, cum, payload, padded):
    load_padded(padded, projected, halo)
    lane = lax.broadcasted_iota(jnp.int32, (1, T), 1)
    raw = projected[:, DT_COL:EINP].astype(f32) + heads[0:1, :]
    soft = jnp.maximum(raw, 0.0) + jnp.log1p(jnp.exp(-jnp.abs(raw)))
    steps = jnp.where(lane < HEADS, soft, 0.0)
    delta[...] = steps
    logs = steps * -jnp.exp(heads[1:2, :])
    sums = dot(lower_triangle().astype(f32), logs, highest)
    cum[...] = sums
    last = sums[T - 1 : T, :]
    weight = jnp.exp(last - sums) * steps
    totals = jnp.exp(last)
    b_pre = conv_block(padded, taps, PAIRS)
    c_pre = conv_block(padded, taps, PAIRS + 1)
    keys = b_pre * sigmoid(b_pre)
    bc[:, 0:STATE] = keys.astype(bf16)
    bc[:, STATE:] = (c_pre * sigmoid(c_pre)).astype(bf16)
    keys_t = keys.T.astype(bf16)
    for j in range(PAIRS):
        pre = conv_block(padded, taps, j)
        x = pre * sigmoid(pre)
        xs[:, block(j)] = x
        put_payload(payload, j, dot(keys_t, (spread(weight, j) * x).astype(bf16)), totals)


def scan_kernel(backward, payload, entering):
    carried = jnp.zeros((STATE, T), f32)
    order = range(PAIRS - 1, -1, -1) if backward else range(PAIRS)
    for k in order:
        entering[k] = carried.astype(bf16)
        extra = payload[k, STATE:PAY, :].astype(f32)
        factor = extra[0:1, :] + extra[1:2, :]
        carried = factor * carried + payload[k, 0:STATE, :].astype(f32)


def decay(cum, cum_t, h, causal):
    return jnp.where(causal, jnp.exp(cum[:, h : h + 1] - cum_t[h : h + 1, :]), 0.0)


def halves(v):
    return jnp.concatenate(
        [jnp.where(low_half(), v, 0.0), jnp.where(low_half(), 0.0, v)], axis=0
    ).astype(bf16)


def within_kernel(xs, bc, delta, cum, heads, local):
    causal = lower_triangle()
    cums = cum[...]
    cum_t = cums.T
    steps = delta[...]
    skips = heads[2:3, :]
    scores = dot_nt(bc[:, STATE:], bc[:, 0:STATE])
    for j in range(PAIRS):
        x = xs[:, block(j)]
        mixing = jnp.concatenate(
            [scores * decay(cums, cum_t, 2 * j + i, causal) for i in range(2)], axis=1
        ).astype(bf16)
        local[:, block(j)] = dot(mixing, halves(spread(steps, j) * x)) + spread(skips, j) * x


def project_kernel(stream, gain, weight, hidden, projected):
    @pl.when(pl.program_id(0) == 0)
    def _():
        values = stream[...]
        inverse = lax.rsqrt(jnp.sum(values * values, axis=1, keepdims=True) / D + epsilon)
        hidden[...] = (values * inverse * gain[...]).astype(bf16)

    projected[...] = dot(hidden[...], weight[...]).astype(bf16)


def finish_kernel(
    local, bc, cum, entering, projected, gain, stream, weight, mixed, normed, result, gated
):
    @pl.when(pl.program_id(0) == 0)
    def _():
        growth = jnp.exp(cum[...])
        queries = bc[:, STATE:]
        squares = jnp.zeros((T, T), f32)
        for j in range(PAIRS):
            whole = local[:, block(j)] + spread(growth, j) * dot(queries, entering[j])
            rounded = whole.astype(bf16)
            mixed[:, block(j)] = rounded
            gate = projected[:, block(j)].astype(f32)
            u = rounded.astype(f32) * (gate * sigmoid(gate))
            gated[:, block(j)] = u
            squares = squares + u * u
        scale = lax.rsqrt(jnp.sum(squares, axis=1, keepdims=True) / DIN + epsilon)
        for j in range(PAIRS):
            normed[:, block(j)] = (gated[:, block(j)] * scale * gain[0:1, block(j)]).astype(bf16)

    result[...] = stream[...] + dot(normed[...], weight[...])


def top_kernel(
    upstream, weight, mixed, projected, gain, bc, cum, d_mixed, d_gate, d_gain, payload, d_normed,
    gated,
):
    step = pl.program_id(0)
    d_normed[step] = dot_nt(upstream[...], weight[...])

    def part(j):
        return d_normed[j // 4, :, block(j % 4)]

    @pl.when(step == 3)
    def _():
        squares = jnp.zeros((T, T), f32)
        products = jnp.zeros((T, T), f32)
        for j in range(PAIRS):
            gate = projected[:, block(j)].astype(f32)
            u = mixed[:, block(j)].astype(f32) * (gate * sigmoid(gate))
            gated[:, block(j)] = u
            squares = squares + u * u
            products = products + part(j) * gain[0:1, block(j)] * u
        scale = lax.rsqrt(jnp.sum(squares, axis=1, keepdims=True) / DIN + epsilon)
        pull = scale * scale * scale * (jnp.sum(products, axis=1, keepdims=True) / DIN)
        cums = cum[...]
        growth = jnp.exp(cums)
        totals = growth[T - 1 : T, :]
        queries_t = bc[:, STATE:].astype(f32).T.astype(bf16)
        for j in range(PAIRS):
            gate = projected[:, block(j)].astype(f32)
            act, slope = silu_and_slope(gate)
            u = gated[:, block(j)]
            up = part(j)
            d_gain[:, block(j)] = jnp.broadcast_to(
                jnp.sum(up * u * scale, axis=0, keepdims=True), (8, T)
            )
            du = up * gain[0:1, block(j)] * scale - u * pull
            dm = (du * act).astype(bf16)
            d_mixed[:, block(j)] = dm
            d_gate[:, block(j)] = (du * mixed[:, block(j)].astype(f32) * slope).astype(bf16)
            put_payload(
                payload, j, dot(queries_t, (spread(growth, j) * dm.astype(f32)).astype(bf16)), totals
            )


def inner_kernel(xs, bc, delta, cum, d_mixed, entering, d_scaled, d_bc, d_cum, rows, columns):
    causal = lower_triangle()
    cums = cum[...]
    cum_t = cums.T
    steps = delta[...]
    growth = jnp.exp(cums)
    keys = bc[:, 0:STATE]
    queries = bc[:, STATE:]
    scores = dot_nt(queries, keys)
    rows[...] = jnp.zeros((T, T), f32)
    columns[...] = jnp.zeros((T, T), f32)
    d_scores = jnp.zeros((T, T), f32)
    d_queries = jnp.zeros((T, STATE), f32)
    for j in range(PAIRS):
        dy_low = d_mixed[:, block(j)]
        dy = dy_low.astype(f32)
        scaled = halves(spread(steps, j) * xs[:, block(j)])
        d_mixing = dot_nt(dy_low, scaled)
        grown = spread(growth, j) * dy
        across = grown * dot(queries, entering[j])
        d_queries = d_queries + dot_nt(grown.astype(bf16), entering[j])
        mixings = []
        for i in range(2):
            h = 2 * j + i
            fall = decay(cums, cum_t, h, causal)
            d_part = d_mixing[:, i * T : (i + 1) * T] * fall
            d_scores = d_scores + d_part
            mixings.append(scores * fall)
            logs = d_part * scores
            own = jnp.where(low_half(), across, 0.0) if i == 0 else jnp.where(low_half(), 0.0, across)
            rows[:, h : h + 1] = jnp.sum(logs + own, axis=1, keepdims=True)
            columns[h : h + 1, :] = jnp.sum(logs, axis=0, keepdims=True)
        d_scaled[:, block(j)] = dot_tn(
            jnp.concatenate(mixings, axis=0).astype(bf16), halves(dy)
        )
    d_low = d_scores.astype(bf16)
    d_bc[:, 0:STATE] = dot_tn(d_low, queries)
    d_bc[:, STATE:] = d_queries + dot(d_low, keys)
    d_cum[...] = rows[...] - columns[...].T


def outer_kernel(
    projected, halo, taps, heads, xs, bc, delta, cum, d_mixed, d_scaled, d_bc, d_cum, entering,
    leaving, d_conv, d_dt, d_taps, d_heads, padded, falls, direct, rest,
):
    load_padded(padded, projected, halo)
    lane = lax.broadcasted_iota(jnp.int32, (1, T), 1)
    cums = cum[...]
    steps = delta[...]
    last = cums[T - 1 : T, :]
    weight = jnp.exp(last - cums)
    totals = jnp.exp(last)
    skips = heads[2:3, :]
    keys = bc[:, 0:STATE]
    falls[...] = jnp.zeros((T, T), f32)
    direct[...] = jnp.zeros((T, T), f32)
    rest[...] = jnp.zeros((8, T), f32)
    low = low_half()

    def conv_back(j, grad):
        pre = conv_block(padded, taps, j)
        d_pre = grad * silu_and_slope(pre)[1]
        d_conv[:, block(j)] = d_pre
        for k in range(KW):
            d_taps[k : k + 1, block(j)] = jnp.sum(
                d_pre * padded[13 + k : 13 + k + T, block(j)], axis=0, keepdims=True
            )
        d_taps[KW : KW + 1, block(j)] = jnp.sum(d_pre, axis=0, keepdims=True)

    d_taps[KW + 1 : 8, :] = jnp.zeros((8 - KW - 1, CONV_CH), f32)
    d_keys = d_bc[:, 0:STATE]
    for j in range(PAIRS):
        x = xs[:, block(j)]
        dy = d_mixed[:, block(j)].astype(f32)
        step = spread(steps, j)
        fall = spread(weight, j)
        weighted = fall * (step * x)
        back = dot(keys, leaving[j])
        d_keys = d_keys + dot_nt(weighted.astype(bf16), leaving[j])
        ds = d_scaled[:, block(j)] + fall * back
        flow = weighted * back
        touch = ds * x
        kept = jnp.sum(leaving[j].astype(f32) * entering[j].astype(f32), axis=0, keepdims=True)
        kept = kept * spread(totals, j)
        skipped = jnp.sum(dy * x, axis=0, keepdims=True)
        for i in range(2):
            h = 2 * j + i
            pick = (lambda v: jnp.where(low, v, 0.0)) if i == 0 else (lambda v: jnp.where(low, 0.0, v))
            falls[:, h : h + 1] = jnp.sum(pick(flow), axis=1, keepdims=True)
            direct[:, h : h + 1] = jnp.sum(pick(touch), axis=1, keepdims=True)
            rest[0:1, h : h + 1] = jnp.sum(pick(kept), axis=1, keepdims=True)
            rest[1:2, h : h + 1] = jnp.sum(pick(skipped), axis=1, keepdims=True)
        conv_back(j, step * ds + spread(skips, j) * dy)
    conv_back(PAIRS, d_keys)
    conv_back(PAIRS + 1, d_bc[:, STATE:])
    flows = falls[...]
    gained = rest[0:1, :] + jnp.sum(flows, axis=0, keepdims=True)
    row = lax.broadcasted_iota(jnp.int32, (T, T), 0)
    d_sums = d_cum[...] - flows + jnp.where(row == T - 1, gained, 0.0)
    upper = lower_triangle().astype(f32).T
    d_logs = dot(upper, d_sums, highest)
    rate = -jnp.exp(heads[1:2, :])
    d_delta = direct[...] + d_logs * rate
    slope = sigmoid(projected[:, DT_COL:EINP].astype(f32) + heads[0:1, :])
    grad = jnp.where(lane < HEADS, d_delta * slope, 0.0)
    d_dt[...] = grad
    d_heads[...] = jnp.zeros((8, T), f32)
    d_heads[0:1, :] = jnp.sum(grad, axis=0, keepdims=True)
    d_heads[1:2, :] = jnp.sum(d_logs * steps, axis=0, keepdims=True) * rate
    d_heads[2:3, :] = rest[1:2, :]


def bottom_kernel(
    d_conv, halo, taps, d_gate, d_dt, weight, stream, norm, upstream, d_projected, result, d_norm,
    padded, total,
):
    step = pl.program_id(0)

    @pl.when(step == 0)
    def _():
        padded[0:T, :] = d_conv[...]
        padded[T : T + 8, :] = halo[...]
        d_projected[:, 0:DIN] = d_gate[...]
        for j in range(CONV_CH // T):
            value = taps[KW - 1 : KW, block(j)] * padded[0:T, block(j)]
            for k in range(KW - 1):
                shift = KW - 1 - k
                value = value + taps[k : k + 1, block(j)] * padded[shift : shift + T, block(j)]
            d_projected[:, DIN + j * T : DIN + (j + 1) * T] = value.astype(bf16)
        d_projected[:, DT_COL:EINP] = d_dt[...].astype(bf16)
        total[...] = jnp.zeros((T, D), f32)

    columns = pl.ds(pl.multiple_of(step * TILE, T), TILE)
    total[...] += dot_nt(d_projected[:, columns], weight[...])

    @pl.when(step == EINP // TILE - 1)
    def _():
        values = stream[...]
        d_hidden = total[...]
        inverse = lax.rsqrt(jnp.sum(values * values, axis=1, keepdims=True) / D + epsilon)
        d_norm[...] = jnp.broadcast_to(
            jnp.sum(d_hidden * values * inverse, axis=0, keepdims=True), (8, D)
        )
        scaled = d_hidden * norm[...]
        mean = jnp.sum(scaled * values, axis=1, keepdims=True) / D
        pull = inverse * inverse * inverse * mean
        result[...] = upstream[...] + scaled * inverse - values * pull


def dropping(kernel, count, extra):
    return lambda *refs: kernel(*refs[:count], *refs[count + extra :])


def call(kernel, outs, scratch, name, micros, *args, after=()):
    return pl.pallas_call(
        dropping(kernel, len(args), len(after)),
        out_shape=[jax.ShapeDtypeStruct(shape, dtype) for shape, dtype in outs],
        scratch_shapes=[pltpu.VMEM(shape, f32) for shape in scratch],
        compiler_params=pltpu.CompilerParams(vmem_limit_bytes=40 * 2**20),
        in_specs=[pl.BlockSpec(memory_space=pltpu.VMEM)] * len(args)
        + [pl.BlockSpec(memory_space=pl.ANY)] * len(after),
        cost_estimate=cost(micros),
        name=name,
    )(*args, *after)


def cost(micros):
    return pl.CostEstimate(flops=0, transcendentals=0, bytes_accessed=int(micros * 3.5e6))


def whole(array):
    rank = len(array.shape)
    return pl.BlockSpec(array.shape, lambda n: (0,) * rank)


def call_tiled(kernel, steps, args, specs, outs, scratch, name, micros, after=()):
    shapes = [jax.ShapeDtypeStruct(shape, dtype) for shape, dtype, _ in outs]
    return pl.pallas_call(
        dropping(kernel, len(args), len(after)),
        grid=(steps,),
        in_specs=[whole(v) if spec is None else spec for v, spec in zip(args, specs)]
        + [pl.BlockSpec(memory_space=pl.ANY) for _ in after],
        out_specs=[whole(v) if o[2] is None else o[2] for v, o in zip(shapes, outs)],
        out_shape=shapes,
        scratch_shapes=[pltpu.VMEM(shape, f32) for shape in scratch],
        compiler_params=pltpu.CompilerParams(vmem_limit_bytes=44 * 2**20),
        cost_estimate=cost(micros),
        name=name,
    )(*args, *after)


def swap(value):
    return lax.ppermute(value, "section", [(0, 1), (1, 0)])


def to_owners(value):
    came = lax.all_to_all(value, "seq", split_axis=0, concat_axis=0, tiled=True)
    return jnp.sum(came.astype(f32), axis=0)


def to_layers(value):
    me = lax.axis_index("dp")

    def piece(steps):
        return lax.dynamic_index_in_dim(value, (me + steps) % 4, 0, keepdims=False)

    total = piece(0).astype(f32)
    for steps in (1, -1, 2):
        moved = lax.ppermute(piece(steps), "dp", [(i, (i + steps) % 4) for i in range(4)])
        total = total + moved.astype(f32)
    return total


def in_chip(grad, rows):
    columns = grad.shape[1]
    shaped = grad.reshape(64, 2, rows // 2, columns)
    section = lax.axis_index("section")
    mine = lax.dynamic_index_in_dim(shaped, section, 1, keepdims=False)
    theirs = lax.dynamic_index_in_dim(shaped, 1 - section, 1, keepdims=False)
    total = (mine.astype(f32) + swap(theirs).astype(f32)).astype(bf16)
    return total.reshape(4, 16, rows // 2, columns)


def own_layer(halves_of, first):
    keep = jnp.where(first, halves_of[0], halves_of[1])
    give = jnp.where(first, halves_of[1], halves_of[0])
    came = swap(give.astype(f32))
    keep = keep.astype(f32)
    return jnp.where(
        first, jnp.concatenate([keep, came], axis=0), jnp.concatenate([came, keep], axis=0)
    )


def exchange(payload, backward):
    moved = lax.all_to_all(payload, "seq", split_axis=0, concat_axis=0, tiled=True)
    (entering,) = call(
        lambda *refs: scan_kernel(backward, *refs),
        [((PAIRS, STATE, T), bf16)],
        [],
        "scan_back" if backward else "scan",
        2,
        moved,
    )
    return lax.all_to_all(entering, "seq", split_axis=0, concat_axis=0, tiled=True)


def forward_layer(stream, w):
    l = w["layer"]
    hidden, projected = call_tiled(
        project_kernel,
        EINP // TILE,
        (stream, w["norm"], w["w_in"]),
        (None, None, pl.BlockSpec((D, TILE), lambda n: (l, n))),
        [((T, D), bf16, None), ((T, EINP), bf16, pl.BlockSpec((T, TILE), lambda n: (0, n)))],
        [],
        "project",
        4,
    )
    halo = lax.ppermute(
        projected[T - 16 :, DIN:DT_COL], "seq", [(i, i + 1) for i in range(15)]
    )
    xs, bc, delta, cum, payload = call(
        front_kernel,
        [((T, DIN), f32), ((T, 2 * STATE), bf16), ((T, T), f32), ((T, T), f32), ((PAIRS, PAY, T), bf16)],
        [(T + 16, CONV_CH)],
        "front",
        2,
        projected,
        halo,
        w["taps"],
        w["heads"],
    )
    entering = exchange(payload, False)
    (local,) = call(within_kernel, [((T, DIN), f32)], [], "within", 2, xs, bc, delta, cum, w["heads"])
    narrow = pl.BlockSpec((T, 512), lambda n: (0, n))
    mixed, normed, result = call_tiled(
        finish_kernel,
        2,
        (local, bc, cum, entering, projected, w["gnorm"], stream, w["w_out"]),
        (None,) * 6 + (narrow, pl.BlockSpec((DIN, 512), lambda n: (l, n))),
        [((T, DIN), bf16, None), ((T, DIN), bf16, None), ((T, D), f32, narrow)],
        [(T, DIN)],
        "finish",
        5,
    )
    return (stream, hidden, projected, halo, xs, bc, delta, cum, entering, mixed, normed), result


def backward_layer(kept, upstream, w, earlier=None, outputs=()):
    stream, hidden, projected, halo, xs, bc, delta, cum, entering, mixed, normed = kept
    upstream_low = upstream.astype(bf16)
    l = w["layer"]
    d_mixed, d_gate, d_gain, payload = call_tiled(
        top_kernel,
        4,
        (upstream_low, w["w_out"], mixed, projected, w["gnorm"], bc, cum),
        (None, pl.BlockSpec((512, D), lambda n: (4 * l + n, 0))) + (None,) * 5,
        [
            ((T, DIN), bf16, None),
            ((T, DIN), bf16, None),
            ((8, DIN), f32, None),
            ((PAIRS, PAY, T), bf16, None),
        ],
        [(4, T, 512), (T, DIN)],
        "top",
        5,
    )
    grad_out = dot_tn(normed, upstream_low).astype(bf16)
    leaving = exchange(payload, True)
    out_total = in_chip(grad_out, 32)
    grad_out = to_layers(out_total).astype(bf16)
    ordered = (grad_out,)
    if earlier is not None:
        leaving, earlier = lax.optimization_barrier((leaving, earlier))
        ordered = (grad_out, earlier)
    d_scaled, d_bc, d_cum = call(
        inner_kernel,
        [((T, DIN), f32), ((T, 2 * STATE), f32), ((T, T), f32)],
        [(T, T), (T, T)],
        "inner",
        8,
        xs,
        bc,
        delta,
        cum,
        d_mixed,
        entering,
    )
    d_conv, d_dt, d_taps, d_heads = call(
        outer_kernel,
        [((T, CONV_CH), f32), ((T, T), f32), ((8, CONV_CH), f32), ((8, T), f32)],
        [(T + 16, CONV_CH), (T, T), (T, T), (8, T)],
        "outer",
        5,
        projected,
        halo,
        w["taps"],
        w["heads"],
        xs,
        bc,
        delta,
        cum,
        d_mixed,
        d_scaled,
        d_bc,
        d_cum,
        entering,
        leaving,
        after=(out_total, *outputs),
    )
    halo_back = lax.ppermute(d_conv[0:8], "seq", [(i + 1, i) for i in range(15)])
    d_projected, result, d_norm = call_tiled(
        bottom_kernel,
        EINP // TILE,
        (d_conv, halo_back, w["taps"], d_gate, d_dt, w["w_in"], stream, w["norm"], upstream),
        (None,) * 5 + (pl.BlockSpec((D, TILE), lambda n: (l, n)),) + (None,) * 3,
        [((T, EINP), bf16, None), ((T, D), f32, None), ((8, D), f32, None)],
        [(T + 8, CONV_CH), (T, D)],
        "bottom",
        6,
        ordered,
    )
    grad_in = dot_tn(hidden, d_projected).astype(bf16)
    small = pack_small(d_norm[0], d_taps, d_gain[0], d_heads)
    return result, grad_in, grad_out, small, earlier


def pack_small(grad_norm, d_taps, d_gain, d_heads):
    def padded(v):
        return jnp.pad(v, ((0, 0), (0, T - v.shape[1])))

    rows = [padded(d_taps[k].reshape(64, 36)) for k in range(KW + 1)]
    rows.append(padded(grad_norm.reshape(64, 16)))
    rows.append(padded(d_gain.reshape(64, 32)))
    heads = d_heads[0:3, 0:HEADS].reshape(1, 3 * HEADS)
    rows.append(jnp.broadcast_to(padded(heads), (64, T)))
    return jnp.stack(rows, axis=1)


def gathered_weights(norm_gain, w_in, conv_w, conv_b, dt_bias, a_log, d_skip, gnorm_gain, w_out):
    def tail(v):
        return jnp.pad(v, ((0, 0), (0, T - v.shape[1])))

    small = jnp.concatenate(
        [tail(conv_w[0]), tail(conv_b), tail(norm_gain), tail(gnorm_gain), jnp.zeros((9, T), bf16)],
        axis=0,
    )
    payload = jnp.concatenate([jnp.pad(w_in[0], ((0, 0), (0, EINP - EIN))), small], axis=1)
    everywhere = ("section", "dp", "seq")
    all_in = lax.all_gather(payload, everywhere, axis=0, tiled=True)
    all_out = lax.all_gather(w_out[0], everywhere, axis=0, tiled=True)
    tiny = all_in[:, EINP:].reshape(2, 64, 16, T)
    heads = jnp.pad(jnp.concatenate([dt_bias, a_log, d_skip], axis=0), ((0, 5), (0, T - HEADS)))
    other = swap(heads)
    first = lax.axis_index("section") == 0
    layers = []
    for l in range(2):
        part = tiny[l]
        taps = jnp.stack([part[:, k, :36].reshape(CONV_CH) for k in range(KW + 1)]).astype(f32)
        layers.append(
            {
                "layer": l,
                "w_in": all_in,
                "w_out": all_out,
                "taps": jnp.pad(taps, ((0, 8 - KW - 1), (0, 0))),
                "norm": part[:, 5, :16].reshape(1, 1024).astype(f32),
                "gnorm": part[:, 6, :32].reshape(1, DIN).astype(f32),
                "heads": jnp.where(first == (l == 0), heads, other),
            }
        )
    return layers


def shards(
    inputs, out_grad, norm_gain, w_in, conv_w, conv_b, dt_bias, a_log, d_skip, gnorm_gain, w_out
):
    section = lax.axis_index("section")
    first = section == 0
    layers = gathered_weights(
        norm_gain, w_in, conv_w, conv_b, dt_bias, a_log, d_skip, gnorm_gain, w_out
    )
    stream = lax.dynamic_index_in_dim(inputs, section, 0, keepdims=False)[0].astype(f32)
    g = lax.dynamic_index_in_dim(out_grad, section, 0, keepdims=False)[0].astype(f32)
    kept = []
    for l in range(2):
        saved, stream = forward_layer(stream, layers[l])
        kept.append(saved)
    outputs = stream.astype(bf16)
    half = outputs.shape[1] // 2

    def by_features(value):
        low, high = value[:, :half], value[:, half:]
        came = swap(jnp.where(first, high, low).astype(bf16)).astype(value.dtype)
        keep = jnp.where(first, low, high)
        return jnp.where(first, jnp.stack([keep, came]), jnp.stack([came, keep]))[:, None]

    out_part = by_features(outputs)
    g, grad_in, out_1, small_1, _ = backward_layer(
        kept[1], g, layers[1], None, (out_part,)
    )
    in_1 = to_layers(in_chip(grad_in, 16)).astype(bf16)
    g, grad_in, out_0, small_0, in_1 = backward_layer(kept[0], g, layers[0], in_1)
    in_1 = to_owners(in_1)
    total_in = in_chip(grad_in, 16)
    total_in, out_0, out_1, small_0, small_1 = lax.optimization_barrier(
        (total_in, out_0, out_1, small_0, small_1)
    )
    smalls = (small_0, small_1)
    in_halves = (to_owners(to_layers(total_in).astype(bf16)), in_1)
    outs = to_owners(jnp.concatenate([out_0, out_1], axis=1))
    out_halves = (outs[0:16], outs[16:32])
    grad_w_in = own_layer(in_halves, first)[:, :EIN]
    grad_w_out = own_layer(out_halves, first)
    small = jnp.where(first, smalls[0], smalls[1]) + swap(jnp.where(first, smalls[1], smalls[0]))
    small = jnp.sum(lax.all_to_all(small, both, split_axis=0, concat_axis=0, tiled=True), axis=0)

    return (
        out_part,
        by_features(g),
        small[5:6, :16],
        grad_w_in[None],
        small[None, 0:KW, :36],
        small[KW : KW + 1, :36],
        small[7:8, 0:HEADS],
        small[7:8, HEADS : 2 * HEADS],
        small[7:8, 2 * HEADS : 3 * HEADS],
        small[6:7, :32],
        grad_w_out[None],
    )


def solution(mesh):
    in_specs = (
        P(None, "dp", "seq", None),
        P(None, "dp", "seq", None),
        P("section", both),
        P("section", both, None),
        P("section", None, both),
        P("section", both),
        P("section", None),
        P("section", None),
        P("section", None),
        P("section", both),
        P("section", both, None),
    )
    out_specs = (
        P(None, "dp", "seq", "section"),
        P(None, "dp", "seq", "section"),
        P("section", both),
        P("section", both, None),
        P("section", None, both),
        P("section", both),
        P("section", None),
        P("section", None),
        P("section", None),
        P("section", both),
        P("section", both, None),
    )
    return jax.shard_map(shards, mesh=mesh, in_specs=in_specs, out_specs=out_specs, check_vma=False)
```

```python
import jax
import jax.numpy as jnp
from jax import lax
from jax.experimental import pallas as pl
from jax.experimental.pallas import tpu as pltpu
from jax.sharding import PartitionSpec as P

DIN = 2048
HEADS = 32
STATE = 128
KW = 4
EIN = 4384
EINP = 4480
CONV_CH = 2304
DT_COL = 2 * DIN + 2 * STATE
T = 128
D = 1024
TILE = 896
PAIRS = 16
PAY = STATE + 16

f32 = jnp.float32
bf16 = jnp.bfloat16
epsilon = 1e-05
highest = lax.Precision.HIGHEST
both = ("dp", "seq")


def dot(a, b, precision=None):
    return jnp.dot(a, b, preferred_element_type=f32, precision=precision)


def dot_nt(a, b):
    return lax.dot_general(a, b, (((1,), (1,)), ((), ())), preferred_element_type=f32)


def dot_tn(a, b):
    return lax.dot_general(a, b, (((0,), (0,)), ((), ())), preferred_element_type=f32)


def low_half():
    return lax.broadcasted_iota(jnp.int32, (1, T), 1) < 64


def lower_triangle():
    rows = lax.broadcasted_iota(jnp.int32, (T, T), 0)
    columns = lax.broadcasted_iota(jnp.int32, (T, T), 1)
    return rows >= columns


def sigmoid(v):
    return 1.0 / (1.0 + jnp.exp(-v))


def silu_and_slope(v):
    s = sigmoid(v)
    return v * s, s * (1.0 + v * (1.0 - s))


def spread(table, j):
    return jnp.where(low_half(), table[:, 2 * j : 2 * j + 1], table[:, 2 * j + 1 : 2 * j + 2])


def block(j):
    return slice(j * T, (j + 1) * T)


def conv_block(padded, taps, j):
    total = taps[KW : KW + 1, block(j)] + taps[0:1, block(j)] * padded[13 : 13 + T, block(j)]
    for k in range(1, KW):
        total = total + taps[k : k + 1, block(j)] * padded[13 + k : 13 + k + T, block(j)]
    return total


def load_padded(padded, projected, halo):
    padded[0:16, :] = halo[...].astype(f32)
    padded[16 : 16 + T, :] = projected[:, DIN:DT_COL].astype(f32)


def put_payload(payload, j, state, totals):
    payload[j, 0:STATE, :] = state.astype(bf16)
    factor = spread(totals, j)
    high = factor.astype(bf16).astype(f32)
    rest = factor - high
    row = lax.broadcasted_iota(jnp.int32, (16, T), 0)
    extra = jnp.where(row == 0, high, jnp.where(row == 1, rest, 0.0))
    payload[j, STATE:PAY, :] = extra.astype(bf16)


def front_kernel(projected, halo, taps, heads, xs, bc, delta, cum, payload, padded):
    load_padded(padded, projected, halo)
    lane = lax.broadcasted_iota(jnp.int32, (1, T), 1)
    raw = projected[:, DT_COL:EINP].astype(f32) + heads[0:1, :]
    soft = jnp.maximum(raw, 0.0) + jnp.log1p(jnp.exp(-jnp.abs(raw)))
    steps = jnp.where(lane < HEADS, soft, 0.0)
    delta[...] = steps
    logs = steps * -jnp.exp(heads[1:2, :])
    sums = dot(lower_triangle().astype(f32), logs, highest)
    cum[...] = sums
    last = sums[T - 1 : T, :]
    weight = jnp.exp(last - sums) * steps
    totals = jnp.exp(last)
    b_pre = conv_block(padded, taps, PAIRS)
    c_pre = conv_block(padded, taps, PAIRS + 1)
    keys = b_pre * sigmoid(b_pre)
    bc[:, 0:STATE] = keys.astype(bf16)
    bc[:, STATE:] = (c_pre * sigmoid(c_pre)).astype(bf16)
    keys_t = keys.T.astype(bf16)
    for j in range(PAIRS):
        pre = conv_block(padded, taps, j)
        x = pre * sigmoid(pre)
        xs[:, block(j)] = x
        put_payload(payload, j, dot(keys_t, (spread(weight, j) * x).astype(bf16)), totals)


def scan_kernel(backward, payload, entering):
    carried = jnp.zeros((STATE, T), f32)
    order = range(PAIRS - 1, -1, -1) if backward else range(PAIRS)
    for k in order:
        entering[k] = carried.astype(bf16)
        extra = payload[k, STATE:PAY, :].astype(f32)
        factor = extra[0:1, :] + extra[1:2, :]
        carried = factor * carried + payload[k, 0:STATE, :].astype(f32)


def decay(cum, cum_t, h, causal):
    return jnp.where(causal, jnp.exp(cum[:, h : h + 1] - cum_t[h : h + 1, :]), 0.0)


def halves(v):
    return jnp.concatenate(
        [jnp.where(low_half(), v, 0.0), jnp.where(low_half(), 0.0, v)], axis=0
    ).astype(bf16)


def within_kernel(xs, bc, delta, cum, heads, local):
    causal = lower_triangle()
    cums = cum[...]
    cum_t = cums.T
    steps = delta[...]
    skips = heads[2:3, :]
    scores = dot_nt(bc[:, STATE:], bc[:, 0:STATE])
    for j in range(PAIRS):
        x = xs[:, block(j)]
        mixing = jnp.concatenate(
            [scores * decay(cums, cum_t, 2 * j + i, causal) for i in range(2)], axis=1
        ).astype(bf16)
        local[:, block(j)] = dot(mixing, halves(spread(steps, j) * x)) + spread(skips, j) * x


def project_kernel(stream, gain, weight, hidden, projected):
    @pl.when(pl.program_id(0) == 0)
    def _():
        values = stream[...]
        inverse = lax.rsqrt(jnp.sum(values * values, axis=1, keepdims=True) / D + epsilon)
        hidden[...] = (values * inverse * gain[...]).astype(bf16)

    projected[...] = dot(hidden[...], weight[...]).astype(bf16)


def finish_kernel(
    local, bc, cum, entering, projected, gain, stream, weight, mixed, normed, result, gated
):
    @pl.when(pl.program_id(0) == 0)
    def _():
        growth = jnp.exp(cum[...])
        queries = bc[:, STATE:]
        squares = jnp.zeros((T, T), f32)
        for j in range(PAIRS):
            whole = local[:, block(j)] + spread(growth, j) * dot(queries, entering[j])
            rounded = whole.astype(bf16)
            mixed[:, block(j)] = rounded
            gate = projected[:, block(j)].astype(f32)
            u = rounded.astype(f32) * (gate * sigmoid(gate))
            gated[:, block(j)] = u
            squares = squares + u * u
        scale = lax.rsqrt(jnp.sum(squares, axis=1, keepdims=True) / DIN + epsilon)
        for j in range(PAIRS):
            normed[:, block(j)] = (gated[:, block(j)] * scale * gain[0:1, block(j)]).astype(bf16)

    result[...] = stream[...] + dot(normed[...], weight[...])


def top_kernel(
    upstream, weight, mixed, projected, gain, bc, cum, d_mixed, d_gate, d_gain, payload, d_normed,
    gated,
):
    step = pl.program_id(0)
    d_normed[step] = dot_nt(upstream[...], weight[...])

    def part(j):
        return d_normed[j // 4, :, block(j % 4)]

    @pl.when(step == 3)
    def _():
        squares = jnp.zeros((T, T), f32)
        products = jnp.zeros((T, T), f32)
        for j in range(PAIRS):
            gate = projected[:, block(j)].astype(f32)
            u = mixed[:, block(j)].astype(f32) * (gate * sigmoid(gate))
            gated[:, block(j)] = u
            squares = squares + u * u
            products = products + part(j) * gain[0:1, block(j)] * u
        scale = lax.rsqrt(jnp.sum(squares, axis=1, keepdims=True) / DIN + epsilon)
        pull = scale * scale * scale * (jnp.sum(products, axis=1, keepdims=True) / DIN)
        cums = cum[...]
        growth = jnp.exp(cums)
        totals = growth[T - 1 : T, :]
        queries_t = bc[:, STATE:].astype(f32).T.astype(bf16)
        for j in range(PAIRS):
            gate = projected[:, block(j)].astype(f32)
            act, slope = silu_and_slope(gate)
            u = gated[:, block(j)]
            up = part(j)
            d_gain[:, block(j)] = jnp.broadcast_to(
                jnp.sum(up * u * scale, axis=0, keepdims=True), (8, T)
            )
            du = up * gain[0:1, block(j)] * scale - u * pull
            dm = (du * act).astype(bf16)
            d_mixed[:, block(j)] = dm
            d_gate[:, block(j)] = (du * mixed[:, block(j)].astype(f32) * slope).astype(bf16)
            put_payload(
                payload, j, dot(queries_t, (spread(growth, j) * dm.astype(f32)).astype(bf16)), totals
            )


def inner_kernel(xs, bc, delta, cum, d_mixed, entering, d_scaled, d_bc, d_cum, rows, columns):
    causal = lower_triangle()
    cums = cum[...]
    cum_t = cums.T
    steps = delta[...]
    growth = jnp.exp(cums)
    keys = bc[:, 0:STATE]
    queries = bc[:, STATE:]
    scores = dot_nt(queries, keys)
    rows[...] = jnp.zeros((T, T), f32)
    columns[...] = jnp.zeros((T, T), f32)
    d_scores = jnp.zeros((T, T), f32)
    d_queries = jnp.zeros((T, STATE), f32)
    for j in range(PAIRS):
        dy_low = d_mixed[:, block(j)]
        dy = dy_low.astype(f32)
        scaled = halves(spread(steps, j) * xs[:, block(j)])
        d_mixing = dot_nt(dy_low, scaled)
        grown = spread(growth, j) * dy
        across = grown * dot(queries, entering[j])
        d_queries = d_queries + dot_nt(grown.astype(bf16), entering[j])
        mixings = []
        for i in range(2):
            h = 2 * j + i
            fall = decay(cums, cum_t, h, causal)
            d_part = d_mixing[:, i * T : (i + 1) * T] * fall
            d_scores = d_scores + d_part
            mixings.append(scores * fall)
            logs = d_part * scores
            own = jnp.where(low_half(), across, 0.0) if i == 0 else jnp.where(low_half(), 0.0, across)
            rows[:, h : h + 1] = jnp.sum(logs + own, axis=1, keepdims=True)
            columns[h : h + 1, :] = jnp.sum(logs, axis=0, keepdims=True)
        d_scaled[:, block(j)] = dot_tn(
            jnp.concatenate(mixings, axis=0).astype(bf16), halves(dy)
        )
    d_low = d_scores.astype(bf16)
    d_bc[:, 0:STATE] = dot_tn(d_low, queries)
    d_bc[:, STATE:] = d_queries + dot(d_low, keys)
    d_cum[...] = rows[...] - columns[...].T


def outer_kernel(
    projected, halo, taps, heads, xs, bc, delta, cum, d_mixed, d_scaled, d_bc, d_cum, entering,
    leaving, d_conv, d_dt, d_taps, d_heads, padded, falls, direct, rest,
):
    load_padded(padded, projected, halo)
    lane = lax.broadcasted_iota(jnp.int32, (1, T), 1)
    cums = cum[...]
    steps = delta[...]
    last = cums[T - 1 : T, :]
    weight = jnp.exp(last - cums)
    totals = jnp.exp(last)
    skips = heads[2:3, :]
    keys = bc[:, 0:STATE]
    falls[...] = jnp.zeros((T, T), f32)
    direct[...] = jnp.zeros((T, T), f32)
    rest[...] = jnp.zeros((8, T), f32)
    low = low_half()

    def conv_back(j, grad):
        pre = conv_block(padded, taps, j)
        d_pre = grad * silu_and_slope(pre)[1]
        d_conv[:, block(j)] = d_pre
        for k in range(KW):
            d_taps[k : k + 1, block(j)] = jnp.sum(
                d_pre * padded[13 + k : 13 + k + T, block(j)], axis=0, keepdims=True
            )
        d_taps[KW : KW + 1, block(j)] = jnp.sum(d_pre, axis=0, keepdims=True)

    d_taps[KW + 1 : 8, :] = jnp.zeros((8 - KW - 1, CONV_CH), f32)
    d_keys = d_bc[:, 0:STATE]
    for j in range(PAIRS):
        x = xs[:, block(j)]
        dy = d_mixed[:, block(j)].astype(f32)
        step = spread(steps, j)
        fall = spread(weight, j)
        weighted = fall * (step * x)
        back = dot(keys, leaving[j])
        d_keys = d_keys + dot_nt(weighted.astype(bf16), leaving[j])
        ds = d_scaled[:, block(j)] + fall * back
        flow = weighted * back
        touch = ds * x
        kept = jnp.sum(leaving[j].astype(f32) * entering[j].astype(f32), axis=0, keepdims=True)
        kept = kept * spread(totals, j)
        skipped = jnp.sum(dy * x, axis=0, keepdims=True)
        for i in range(2):
            h = 2 * j + i
            pick = (lambda v: jnp.where(low, v, 0.0)) if i == 0 else (lambda v: jnp.where(low, 0.0, v))
            falls[:, h : h + 1] = jnp.sum(pick(flow), axis=1, keepdims=True)
            direct[:, h : h + 1] = jnp.sum(pick(touch), axis=1, keepdims=True)
            rest[0:1, h : h + 1] = jnp.sum(pick(kept), axis=1, keepdims=True)
            rest[1:2, h : h + 1] = jnp.sum(pick(skipped), axis=1, keepdims=True)
        conv_back(j, step * ds + spread(skips, j) * dy)
    conv_back(PAIRS, d_keys)
    conv_back(PAIRS + 1, d_bc[:, STATE:])
    flows = falls[...]
    gained = rest[0:1, :] + jnp.sum(flows, axis=0, keepdims=True)
    row = lax.broadcasted_iota(jnp.int32, (T, T), 0)
    d_sums = d_cum[...] - flows + jnp.where(row == T - 1, gained, 0.0)
    upper = lower_triangle().astype(f32).T
    d_logs = dot(upper, d_sums, highest)
    rate = -jnp.exp(heads[1:2, :])
    d_delta = direct[...] + d_logs * rate
    slope = sigmoid(projected[:, DT_COL:EINP].astype(f32) + heads[0:1, :])
    grad = jnp.where(lane < HEADS, d_delta * slope, 0.0)
    d_dt[...] = grad
    d_heads[...] = jnp.zeros((8, T), f32)
    d_heads[0:1, :] = jnp.sum(grad, axis=0, keepdims=True)
    d_heads[1:2, :] = jnp.sum(d_logs * steps, axis=0, keepdims=True) * rate
    d_heads[2:3, :] = rest[1:2, :]


def bottom_kernel(
    d_conv, halo, taps, d_gate, d_dt, weight, stream, norm, upstream, d_projected, result, d_norm,
    padded, total,
):
    step = pl.program_id(0)

    @pl.when(step == 0)
    def _():
        padded[0:T, :] = d_conv[...]
        padded[T : T + 8, :] = halo[...]
        d_projected[:, 0:DIN] = d_gate[...]
        for j in range(CONV_CH // T):
            value = taps[KW - 1 : KW, block(j)] * padded[0:T, block(j)]
            for k in range(KW - 1):
                shift = KW - 1 - k
                value = value + taps[k : k + 1, block(j)] * padded[shift : shift + T, block(j)]
            d_projected[:, DIN + j * T : DIN + (j + 1) * T] = value.astype(bf16)
        d_projected[:, DT_COL:EINP] = d_dt[...].astype(bf16)
        total[...] = jnp.zeros((T, D), f32)

    columns = pl.ds(pl.multiple_of(step * TILE, T), TILE)
    total[...] += dot_nt(d_projected[:, columns], weight[...])

    @pl.when(step == EINP // TILE - 1)
    def _():
        values = stream[...]
        d_hidden = total[...]
        inverse = lax.rsqrt(jnp.sum(values * values, axis=1, keepdims=True) / D + epsilon)
        d_norm[...] = jnp.broadcast_to(
            jnp.sum(d_hidden * values * inverse, axis=0, keepdims=True), (8, D)
        )
        scaled = d_hidden * norm[...]
        mean = jnp.sum(scaled * values, axis=1, keepdims=True) / D
        pull = inverse * inverse * inverse * mean
        result[...] = upstream[...] + scaled * inverse - values * pull


def dropping(kernel, count, extra):
    return lambda *refs: kernel(*refs[:count], *refs[count + extra :])


def call(kernel, outs, scratch, name, micros, *args, after=()):
    return pl.pallas_call(
        dropping(kernel, len(args), len(after)),
        out_shape=[jax.ShapeDtypeStruct(shape, dtype) for shape, dtype in outs],
        scratch_shapes=[pltpu.VMEM(shape, f32) for shape in scratch],
        compiler_params=pltpu.CompilerParams(vmem_limit_bytes=40 * 2**20),
        in_specs=[pl.BlockSpec(memory_space=pltpu.VMEM)] * len(args)
        + [pl.BlockSpec(memory_space=pl.ANY)] * len(after),
        cost_estimate=cost(micros),
        name=name,
    )(*args, *after)


def cost(micros):
    return pl.CostEstimate(flops=0, transcendentals=0, bytes_accessed=int(micros * 3.5e6))


def whole(array):
    rank = len(array.shape)
    return pl.BlockSpec(array.shape, lambda n: (0,) * rank)


def call_tiled(kernel, steps, args, specs, outs, scratch, name, micros, after=()):
    shapes = [jax.ShapeDtypeStruct(shape, dtype) for shape, dtype, _ in outs]
    return pl.pallas_call(
        dropping(kernel, len(args), len(after)),
        grid=(steps,),
        in_specs=[whole(v) if spec is None else spec for v, spec in zip(args, specs)]
        + [pl.BlockSpec(memory_space=pl.ANY) for _ in after],
        out_specs=[whole(v) if o[2] is None else o[2] for v, o in zip(shapes, outs)],
        out_shape=shapes,
        scratch_shapes=[pltpu.VMEM(shape, f32) for shape in scratch],
        compiler_params=pltpu.CompilerParams(vmem_limit_bytes=44 * 2**20),
        cost_estimate=cost(micros),
        name=name,
    )(*args, *after)


def swap(value):
    return lax.ppermute(value, "section", [(0, 1), (1, 0)])


def to_owners(value):
    came = lax.all_to_all(value, "seq", split_axis=0, concat_axis=0, tiled=True)
    return jnp.sum(came.astype(f32), axis=0)


def to_layers(value):
    me = lax.axis_index("dp")

    def piece(steps):
        return lax.dynamic_index_in_dim(value, (me + steps) % 4, 0, keepdims=False)

    total = piece(0).astype(f32)
    for steps in (1, -1, 2):
        moved = lax.ppermute(piece(steps), "dp", [(i, (i + steps) % 4) for i in range(4)])
        total = total + moved.astype(f32)
    return total


def to_layers_in_order(value):
    me = lax.axis_index("dp")
    came = [lax.dynamic_index_in_dim(value, me, 0, keepdims=False)]
    for steps in (1, 2, 3):
        part = lax.dynamic_index_in_dim(value, (me + steps) % 4, 0, keepdims=False)
        came.append(lax.ppermute(part, "dp", [(i, (i + steps) % 4) for i in range(4)]))
    came = jnp.stack(came)
    total = lax.dynamic_index_in_dim(came, me, 0, keepdims=False)
    for source in (1, 2, 3):
        total = total + lax.dynamic_index_in_dim(came, (me - source) % 4, 0, keepdims=False)
    return total


def in_chip(grad, rows):
    columns = grad.shape[1]
    shaped = grad.reshape(64, 2, rows // 2, columns)
    section = lax.axis_index("section")
    mine = lax.dynamic_index_in_dim(shaped, section, 1, keepdims=False)
    theirs = lax.dynamic_index_in_dim(shaped, 1 - section, 1, keepdims=False)
    total = (mine.astype(f32) + swap(theirs).astype(f32)).astype(bf16)
    return total.reshape(4, 16, rows // 2, columns)


def own_layer(halves_of, first):
    keep = jnp.where(first, halves_of[0], halves_of[1])
    give = jnp.where(first, halves_of[1], halves_of[0])
    came = swap(give.astype(f32))
    keep = keep.astype(f32)
    return jnp.where(
        first, jnp.concatenate([keep, came], axis=0), jnp.concatenate([came, keep], axis=0)
    )


def exchange(payload, backward):
    moved = lax.all_to_all(payload, "seq", split_axis=0, concat_axis=0, tiled=True)
    (entering,) = call(
        lambda *refs: scan_kernel(backward, *refs),
        [((PAIRS, STATE, T), bf16)],
        [],
        "scan_back" if backward else "scan",
        2,
        moved,
    )
    return lax.all_to_all(entering, "seq", split_axis=0, concat_axis=0, tiled=True)


def forward_layer(stream, w):
    l = w["layer"]
    hidden, projected = call_tiled(
        project_kernel,
        EINP // TILE,
        (stream, w["norm"], w["w_in"]),
        (None, None, pl.BlockSpec((D, TILE), lambda n: (l, n))),
        [((T, D), bf16, None), ((T, EINP), bf16, pl.BlockSpec((T, TILE), lambda n: (0, n)))],
        [],
        "project",
        4,
    )
    halo = lax.ppermute(
        projected[T - 16 :, DIN:DT_COL], "seq", [(i, i + 1) for i in range(15)]
    )
    xs, bc, delta, cum, payload = call(
        front_kernel,
        [((T, DIN), f32), ((T, 2 * STATE), bf16), ((T, T), f32), ((T, T), f32), ((PAIRS, PAY, T), bf16)],
        [(T + 16, CONV_CH)],
        "front",
        2,
        projected,
        halo,
        w["taps"],
        w["heads"],
    )
    entering = exchange(payload, False)
    (local,) = call(within_kernel, [((T, DIN), f32)], [], "within", 2, xs, bc, delta, cum, w["heads"])
    narrow = pl.BlockSpec((T, 512), lambda n: (0, n))
    mixed, normed, result = call_tiled(
        finish_kernel,
        2,
        (local, bc, cum, entering, projected, w["gnorm"], stream, w["w_out"]),
        (None,) * 6 + (narrow, pl.BlockSpec((DIN, 512), lambda n: (l, n))),
        [((T, DIN), bf16, None), ((T, DIN), bf16, None), ((T, D), f32, narrow)],
        [(T, DIN)],
        "finish",
        5,
    )
    return (stream, hidden, projected, halo, xs, bc, delta, cum, entering, mixed, normed), result


def backward_layer(kept, upstream, w, earlier=None, outputs=()):
    stream, hidden, projected, halo, xs, bc, delta, cum, entering, mixed, normed = kept
    upstream_low = upstream.astype(bf16)
    l = w["layer"]
    d_mixed, d_gate, d_gain, payload = call_tiled(
        top_kernel,
        4,
        (upstream_low, w["w_out"], mixed, projected, w["gnorm"], bc, cum),
        (None, pl.BlockSpec((512, D), lambda n: (4 * l + n, 0))) + (None,) * 5,
        [
            ((T, DIN), bf16, None),
            ((T, DIN), bf16, None),
            ((8, DIN), f32, None),
            ((PAIRS, PAY, T), bf16, None),
        ],
        [(4, T, 512), (T, DIN)],
        "top",
        5,
    )
    grad_out = dot_tn(normed, upstream_low).astype(bf16)
    leaving = exchange(payload, True)
    out_total = in_chip(grad_out, 32)
    grad_out = to_layers(out_total).astype(bf16)
    ordered = (grad_out,)
    if earlier is not None:
        leaving, earlier = lax.optimization_barrier((leaving, earlier))
        ordered = (grad_out, earlier)
    d_scaled, d_bc, d_cum = call(
        inner_kernel,
        [((T, DIN), f32), ((T, 2 * STATE), f32), ((T, T), f32)],
        [(T, T), (T, T)],
        "inner",
        8,
        xs,
        bc,
        delta,
        cum,
        d_mixed,
        entering,
    )
    d_conv, d_dt, d_taps, d_heads = call(
        outer_kernel,
        [((T, CONV_CH), f32), ((T, T), f32), ((8, CONV_CH), f32), ((8, T), f32)],
        [(T + 16, CONV_CH), (T, T), (T, T), (8, T)],
        "outer",
        5,
        projected,
        halo,
        w["taps"],
        w["heads"],
        xs,
        bc,
        delta,
        cum,
        d_mixed,
        d_scaled,
        d_bc,
        d_cum,
        entering,
        leaving,
        after=(out_total, *outputs),
    )
    halo_back = lax.ppermute(d_conv[0:8], "seq", [(i + 1, i) for i in range(15)])
    d_projected, result, d_norm = call_tiled(
        bottom_kernel,
        EINP // TILE,
        (d_conv, halo_back, w["taps"], d_gate, d_dt, w["w_in"], stream, w["norm"], upstream),
        (None,) * 5 + (pl.BlockSpec((D, TILE), lambda n: (l, n)),) + (None,) * 3,
        [((T, EINP), bf16, None), ((T, D), f32, None), ((8, D), f32, None)],
        [(T + 8, CONV_CH), (T, D)],
        "bottom",
        6,
        ordered,
    )
    grad_in = dot_tn(hidden, d_projected).astype(bf16)
    small = pack_small(d_norm[0], d_taps, d_gain[0], d_heads)
    return result, grad_in, grad_out, small, earlier


def pack_small(grad_norm, d_taps, d_gain, d_heads):
    def padded(v):
        return jnp.pad(v, ((0, 0), (0, T - v.shape[1])))

    rows = [padded(d_taps[k].reshape(64, 36)) for k in range(KW + 1)]
    rows.append(padded(grad_norm.reshape(64, 16)))
    rows.append(padded(d_gain.reshape(64, 32)))
    heads = d_heads[0:3, 0:HEADS].reshape(1, 3 * HEADS)
    rows.append(jnp.broadcast_to(padded(heads), (64, T)))
    return jnp.stack(rows, axis=1)


def gathered_weights(norm_gain, w_in, conv_w, conv_b, dt_bias, a_log, d_skip, gnorm_gain, w_out):
    def tail(v):
        return jnp.pad(v, ((0, 0), (0, T - v.shape[1])))

    small = jnp.concatenate(
        [tail(conv_w[0]), tail(conv_b), tail(norm_gain), tail(gnorm_gain), jnp.zeros((9, T), bf16)],
        axis=0,
    )
    payload = jnp.concatenate([jnp.pad(w_in[0], ((0, 0), (0, EINP - EIN))), small], axis=1)
    everywhere = ("section", "dp", "seq")
    all_in = lax.all_gather(payload, everywhere, axis=0, tiled=True)
    all_out = lax.all_gather(w_out[0], everywhere, axis=0, tiled=True)
    tiny = all_in[:, EINP:].reshape(2, 64, 16, T)
    heads = jnp.pad(jnp.concatenate([dt_bias, a_log, d_skip], axis=0), ((0, 5), (0, T - HEADS)))
    other = swap(heads)
    first = lax.axis_index("section") == 0
    layers = []
    for l in range(2):
        part = tiny[l]
        taps = jnp.stack([part[:, k, :36].reshape(CONV_CH) for k in range(KW + 1)]).astype(f32)
        layers.append(
            {
                "layer": l,
                "w_in": all_in,
                "w_out": all_out,
                "taps": jnp.pad(taps, ((0, 8 - KW - 1), (0, 0))),
                "norm": part[:, 5, :16].reshape(1, 1024).astype(f32),
                "gnorm": part[:, 6, :32].reshape(1, DIN).astype(f32),
                "heads": jnp.where(first == (l == 0), heads, other),
            }
        )
    return layers


def shards(
    inputs, out_grad, norm_gain, w_in, conv_w, conv_b, dt_bias, a_log, d_skip, gnorm_gain, w_out
):
    section = lax.axis_index("section")
    first = section == 0
    layers = gathered_weights(
        norm_gain, w_in, conv_w, conv_b, dt_bias, a_log, d_skip, gnorm_gain, w_out
    )
    stream = lax.dynamic_index_in_dim(inputs, section, 0, keepdims=False)[0].astype(f32)
    g = lax.dynamic_index_in_dim(out_grad, section, 0, keepdims=False)[0].astype(f32)
    kept = []
    for l in range(2):
        saved, stream = forward_layer(stream, layers[l])
        kept.append(saved)
    outputs = stream.astype(bf16)
    half = outputs.shape[1] // 2

    def by_features(value):
        low, high = value[:, :half], value[:, half:]
        came = swap(jnp.where(first, high, low).astype(bf16)).astype(value.dtype)
        keep = jnp.where(first, low, high)
        return jnp.where(first, jnp.stack([keep, came]), jnp.stack([came, keep]))[:, None]

    out_part = by_features(outputs)
    g, grad_in, out_1, small_1, _ = backward_layer(
        kept[1], g, layers[1], None, (out_part,)
    )
    in_1 = to_layers(in_chip(grad_in, 16)).astype(bf16)
    g, grad_in, out_0, small_0, in_1 = backward_layer(kept[0], g, layers[0], in_1)
    in_1 = to_owners(in_1)
    total_in = in_chip(grad_in, 16)
    total_in, out_0, out_1, small_0, small_1 = lax.optimization_barrier(
        (total_in, out_0, out_1, small_0, small_1)
    )
    smalls = (small_0, small_1)
    in_halves = (to_owners(to_layers(total_in).astype(bf16)), in_1)
    outs = to_owners(jnp.concatenate([out_0, out_1], axis=1))
    out_halves = (outs[0:16], outs[16:32])
    grad_w_in = own_layer(in_halves, first)[:, :EIN]
    grad_w_out = own_layer(out_halves, first)
    small = jnp.where(first, smalls[0], smalls[1]) + swap(jnp.where(first, smalls[1], smalls[0]))
    small = to_layers_in_order(to_owners(jnp.swapaxes(small.reshape(4, 16, 8, T), 0, 1)))

    return (
        out_part,
        by_features(g),
        small[5:6, :16],
        grad_w_in[None],
        small[None, 0:KW, :36],
        small[KW : KW + 1, :36],
        small[7:8, 0:HEADS],
        small[7:8, HEADS : 2 * HEADS],
        small[7:8, 2 * HEADS : 3 * HEADS],
        small[6:7, :32],
        grad_w_out[None],
    )


def solution(mesh):
    in_specs = (
        P(None, "dp", "seq", None),
        P(None, "dp", "seq", None),
        P("section", both),
        P("section", both, None),
        P("section", None, both),
        P("section", both),
        P("section", None),
        P("section", None),
        P("section", None),
        P("section", both),
        P("section", both, None),
    )
    out_specs = (
        P(None, "dp", "seq", "section"),
        P(None, "dp", "seq", "section"),
        P("section", both),
        P("section", both, None),
        P("section", None, both),
        P("section", both),
        P("section", None),
        P("section", None),
        P("section", None),
        P("section", both),
        P("section", both, None),
    )
    return jax.shard_map(shards, mesh=mesh, in_specs=in_specs, out_specs=out_specs, check_vma=False)
```

```python
import jax
import jax.numpy as jnp
from jax import lax
from jax.experimental import pallas as pl
from jax.experimental.pallas import tpu as pltpu
from jax.sharding import PartitionSpec as P

DIN = 2048
HEADS = 32
STATE = 128
KW = 4
EIN = 4384
EINP = 4480
CONV_CH = 2304
DT_COL = 2 * DIN + 2 * STATE
T = 128
D = 1024
TILE = 512
XBC = 2560
DT = 2304
WIDE = DIN + XBC
PAIRS = 16
PAY = STATE + 16

f32 = jnp.float32
bf16 = jnp.bfloat16
epsilon = 1e-05
highest = lax.Precision.HIGHEST
both = ("dp", "seq")


def dot(a, b, precision=None):
    return jnp.dot(a, b, preferred_element_type=f32, precision=precision)


def dot_nt(a, b):
    return lax.dot_general(a, b, (((1,), (1,)), ((), ())), preferred_element_type=f32)


def dot_tn(a, b):
    return lax.dot_general(a, b, (((0,), (0,)), ((), ())), preferred_element_type=f32)


def low_half():
    return lax.broadcasted_iota(jnp.int32, (1, T), 1) < 64


def lower_triangle():
    rows = lax.broadcasted_iota(jnp.int32, (T, T), 0)
    columns = lax.broadcasted_iota(jnp.int32, (T, T), 1)
    return rows >= columns


def sigmoid(v):
    return 1.0 / (1.0 + jnp.exp(-v))


def silu_and_slope(v):
    s = sigmoid(v)
    return v * s, s * (1.0 + v * (1.0 - s))


def spread(table, j):
    return jnp.where(low_half(), table[:, 2 * j : 2 * j + 1], table[:, 2 * j + 1 : 2 * j + 2])


def block(j):
    return slice(j * T, (j + 1) * T)


def conv_block(padded, taps, j):
    total = taps[KW : KW + 1, block(j)] + taps[0:1, block(j)] * padded[13 : 13 + T, block(j)]
    for k in range(1, KW):
        total = total + taps[k : k + 1, block(j)] * padded[13 + k : 13 + k + T, block(j)]
    return total


def load_padded(padded, xbc, halo):
    padded[0:16, :] = halo[...].astype(f32)
    padded[16 : 16 + T, :] = xbc[:, 0:DT].astype(f32)


def put_payload(payload, j, state, totals):
    payload[j, 0:STATE, :] = state.astype(bf16)
    factor = spread(totals, j)
    high = factor.astype(bf16).astype(f32)
    rest = factor - high
    row = lax.broadcasted_iota(jnp.int32, (16, T), 0)
    extra = jnp.where(row == 0, high, jnp.where(row == 1, rest, 0.0))
    payload[j, STATE:PAY, :] = extra.astype(bf16)


def shuffle():
    source = lax.broadcasted_iota(jnp.int32, (256, 256), 0)
    target = lax.broadcasted_iota(jnp.int32, (256, 256), 1)
    k, i, r = source >> 5, (source >> 4) & 1, source & 15
    return jnp.where(target == i * T + k * 16 + r, 1.0, 0.0).astype(bf16)


def front_kernel(xbc, halo, taps, heads, xs, bc, delta, cum, payload, padded):
    load_padded(padded, xbc, halo)
    lane = lax.broadcasted_iota(jnp.int32, (1, T), 1)
    raw = xbc[:, DT : DT + T].astype(f32) + heads[0:1, :]
    soft = jnp.maximum(raw, 0.0) + jnp.log1p(jnp.exp(-jnp.abs(raw)))
    steps = jnp.where(lane < HEADS, soft, 0.0)
    delta[...] = steps
    logs = steps * -jnp.exp(heads[1:2, :])
    sums = dot(lower_triangle().astype(f32), logs, highest)
    cum[...] = sums
    last = sums[T - 1 : T, :]
    weight = jnp.exp(last - sums) * steps
    totals = jnp.exp(last)
    b_pre = conv_block(padded, taps, PAIRS)
    c_pre = conv_block(padded, taps, PAIRS + 1)
    keys = b_pre * sigmoid(b_pre)
    bc[:, 0:STATE] = keys.astype(bf16)
    bc[:, STATE:] = (c_pre * sigmoid(c_pre)).astype(bf16)
    keys_t = keys.T.astype(bf16)
    for j in range(PAIRS):
        pre = conv_block(padded, taps, j)
        x = pre * sigmoid(pre)
        xs[:, block(j)] = x
        put_payload(payload, j, dot(keys_t, (spread(weight, j) * x).astype(bf16)), totals)


def scan_kernel(backward, payload, entering):
    carried = jnp.zeros((STATE, T), f32)
    order = range(PAIRS - 1, -1, -1) if backward else range(PAIRS)
    for k in order:
        entering[k] = carried.astype(bf16)
        extra = payload[k, STATE:PAY, :].astype(f32)
        factor = extra[0:1, :] + extra[1:2, :]
        carried = factor * carried + payload[k, 0:STATE, :].astype(f32)


def decay(cum, cum_t, h, causal):
    return jnp.where(causal, jnp.exp(cum[:, h : h + 1] - cum_t[h : h + 1, :]), 0.0)


def halves(v):
    return jnp.concatenate(
        [jnp.where(low_half(), v, 0.0), jnp.where(low_half(), 0.0, v)], axis=0
    ).astype(bf16)


def within_kernel(xs, bc, delta, cum, heads, local):
    causal = lower_triangle()
    cums = cum[...]
    cum_t = cums.T
    steps = delta[...]
    skips = heads[2:3, :]
    scores = dot_nt(bc[:, STATE:], bc[:, 0:STATE])
    for j in range(PAIRS):
        x = xs[:, block(j)]
        mixing = jnp.concatenate(
            [scores * decay(cums, cum_t, 2 * j + i, causal) for i in range(2)], axis=1
        ).astype(bf16)
        local[:, block(j)] = dot(mixing, halves(spread(steps, j) * x)) + spread(skips, j) * x


def project_kernel(stream, gain, weight, hidden, projected):
    @pl.when(pl.program_id(0) == 0)
    def _():
        values = stream[...]
        inverse = lax.rsqrt(jnp.sum(values * values, axis=1, keepdims=True) / D + epsilon)
        hidden[...] = (values * inverse * gain[...]).astype(bf16)

    projected[...] = dot(hidden[...], weight[...]).astype(bf16)


def finish_kernel(
    local, bc, cum, entering, gates, gain, stream, weight_0, weight_1, mixed, normed, result, gated,
    shuffled,
):
    @pl.when(pl.program_id(0) == 0)
    def _():
        growth = jnp.exp(cum[...])
        queries = bc[:, STATE:]
        squares = jnp.zeros((T, T), f32)
        for j in range(PAIRS):
            whole = local[:, block(j)] + spread(growth, j) * dot(queries, entering[j])
            rounded = whole.astype(bf16)
            mixed[:, block(j)] = rounded
            gate = gates[:, block(j)].astype(f32)
            u = rounded.astype(f32) * (gate * sigmoid(gate))
            gated[:, block(j)] = u
            squares = squares + u * u
        scale = lax.rsqrt(jnp.sum(squares, axis=1, keepdims=True) / DIN + epsilon)
        for j in range(PAIRS):
            normed[:, block(j)] = (gated[:, block(j)] * scale * gain[0:1, block(j)]).astype(bf16)

        order = shuffle()
        for b in range(8):
            moved = dot(normed[:, b * 256 : (b + 1) * 256], order)
            shuffled[0, :, block(b)] = moved[:, 0:T]
            shuffled[1, :, block(b)] = moved[:, T:]

    result[...] = (
        stream[...]
        + dot(shuffled[0].astype(bf16), weight_0[...])
        + dot(shuffled[1].astype(bf16), weight_1[...])
    )


def top_kernel(
    upstream, weight, mixed, gates, gain, bc, cum, d_mixed, d_gate, d_gain, payload, d_shuffled,
    d_normed, gated,
):
    step = pl.program_id(0)
    d_shuffled[step] = dot_nt(upstream[...], weight[...])

    def part(j):
        return d_normed[:, block(j)]

    @pl.when(step == 1)
    def _():
        order = shuffle()
        for b in range(8):
            value = jnp.concatenate([d_shuffled[0, :, block(b)], d_shuffled[1, :, block(b)]], axis=1)
            high = value.astype(bf16)
            rest = (value - high.astype(f32)).astype(bf16)
            d_normed[:, b * 256 : (b + 1) * 256] = dot_nt(high, order) + dot_nt(rest, order)
        squares = jnp.zeros((T, T), f32)
        products = jnp.zeros((T, T), f32)
        for j in range(PAIRS):
            gate = gates[:, block(j)].astype(f32)
            u = mixed[:, block(j)].astype(f32) * (gate * sigmoid(gate))
            gated[:, block(j)] = u
            squares = squares + u * u
            products = products + part(j) * gain[0:1, block(j)] * u
        scale = lax.rsqrt(jnp.sum(squares, axis=1, keepdims=True) / DIN + epsilon)
        pull = scale * scale * scale * (jnp.sum(products, axis=1, keepdims=True) / DIN)
        cums = cum[...]
        growth = jnp.exp(cums)
        totals = growth[T - 1 : T, :]
        queries_t = bc[:, STATE:].astype(f32).T.astype(bf16)
        for j in range(PAIRS):
            gate = gates[:, block(j)].astype(f32)
            act, slope = silu_and_slope(gate)
            u = gated[:, block(j)]
            up = part(j)
            d_gain[:, block(j)] = jnp.broadcast_to(
                jnp.sum(up * u * scale, axis=0, keepdims=True), (8, T)
            )
            du = up * gain[0:1, block(j)] * scale - u * pull
            dm = (du * act).astype(bf16)
            d_mixed[:, block(j)] = dm
            d_gate[:, block(j)] = (du * mixed[:, block(j)].astype(f32) * slope).astype(bf16)
            put_payload(
                payload, j, dot(queries_t, (spread(growth, j) * dm.astype(f32)).astype(bf16)), totals
            )


def inner_kernel(xs, bc, delta, cum, d_mixed, entering, d_scaled, d_bc, d_cum, rows, columns):
    causal = lower_triangle()
    cums = cum[...]
    cum_t = cums.T
    steps = delta[...]
    growth = jnp.exp(cums)
    keys = bc[:, 0:STATE]
    queries = bc[:, STATE:]
    scores = dot_nt(queries, keys)
    rows[...] = jnp.zeros((T, T), f32)
    columns[...] = jnp.zeros((T, T), f32)
    d_scores = jnp.zeros((T, T), f32)
    d_queries = jnp.zeros((T, STATE), f32)
    for j in range(PAIRS):
        dy_low = d_mixed[:, block(j)]
        dy = dy_low.astype(f32)
        scaled = halves(spread(steps, j) * xs[:, block(j)])
        d_mixing = dot_nt(dy_low, scaled)
        grown = spread(growth, j) * dy
        across = grown * dot(queries, entering[j])
        d_queries = d_queries + dot_nt(grown.astype(bf16), entering[j])
        mixings = []
        for i in range(2):
            h = 2 * j + i
            fall = decay(cums, cum_t, h, causal)
            d_part = d_mixing[:, i * T : (i + 1) * T] * fall
            d_scores = d_scores + d_part
            mixings.append(scores * fall)
            logs = d_part * scores
            own = jnp.where(low_half(), across, 0.0) if i == 0 else jnp.where(low_half(), 0.0, across)
            rows[:, h : h + 1] = jnp.sum(logs + own, axis=1, keepdims=True)
            columns[h : h + 1, :] = jnp.sum(logs, axis=0, keepdims=True)
        d_scaled[:, block(j)] = dot_tn(
            jnp.concatenate(mixings, axis=0).astype(bf16), halves(dy)
        )
    d_low = d_scores.astype(bf16)
    d_bc[:, 0:STATE] = dot_tn(d_low, queries)
    d_bc[:, STATE:] = d_queries + dot(d_low, keys)
    d_cum[...] = rows[...] - columns[...].T


def outer_kernel(
    xbc, halo, taps, heads, xs, bc, delta, cum, d_mixed, d_scaled, d_bc, d_cum, entering,
    leaving, d_conv, d_dt, d_taps, d_heads, padded, falls, direct, rest,
):
    load_padded(padded, xbc, halo)
    lane = lax.broadcasted_iota(jnp.int32, (1, T), 1)
    cums = cum[...]
    steps = delta[...]
    last = cums[T - 1 : T, :]
    weight = jnp.exp(last - cums)
    totals = jnp.exp(last)
    skips = heads[2:3, :]
    keys = bc[:, 0:STATE]
    falls[...] = jnp.zeros((T, T), f32)
    direct[...] = jnp.zeros((T, T), f32)
    rest[...] = jnp.zeros((8, T), f32)
    low = low_half()

    def conv_back(j, grad):
        pre = conv_block(padded, taps, j)
        d_pre = grad * silu_and_slope(pre)[1]
        d_conv[:, block(j)] = d_pre
        for k in range(KW):
            d_taps[k : k + 1, block(j)] = jnp.sum(
                d_pre * padded[13 + k : 13 + k + T, block(j)], axis=0, keepdims=True
            )
        d_taps[KW : KW + 1, block(j)] = jnp.sum(d_pre, axis=0, keepdims=True)

    d_taps[KW + 1 : 8, :] = jnp.zeros((8 - KW - 1, CONV_CH), f32)
    d_keys = d_bc[:, 0:STATE]
    for j in range(PAIRS):
        x = xs[:, block(j)]
        dy = d_mixed[:, block(j)].astype(f32)
        step = spread(steps, j)
        fall = spread(weight, j)
        weighted = fall * (step * x)
        back = dot(keys, leaving[j])
        d_keys = d_keys + dot_nt(weighted.astype(bf16), leaving[j])
        ds = d_scaled[:, block(j)] + fall * back
        flow = weighted * back
        touch = ds * x
        kept = jnp.sum(leaving[j].astype(f32) * entering[j].astype(f32), axis=0, keepdims=True)
        kept = kept * spread(totals, j)
        skipped = jnp.sum(dy * x, axis=0, keepdims=True)
        for i in range(2):
            h = 2 * j + i
            pick = (lambda v: jnp.where(low, v, 0.0)) if i == 0 else (lambda v: jnp.where(low, 0.0, v))
            falls[:, h : h + 1] = jnp.sum(pick(flow), axis=1, keepdims=True)
            direct[:, h : h + 1] = jnp.sum(pick(touch), axis=1, keepdims=True)
            rest[0:1, h : h + 1] = jnp.sum(pick(kept), axis=1, keepdims=True)
            rest[1:2, h : h + 1] = jnp.sum(pick(skipped), axis=1, keepdims=True)
        conv_back(j, step * ds + spread(skips, j) * dy)
    conv_back(PAIRS, d_keys)
    conv_back(PAIRS + 1, d_bc[:, STATE:])
    flows = falls[...]
    gained = rest[0:1, :] + jnp.sum(flows, axis=0, keepdims=True)
    row = lax.broadcasted_iota(jnp.int32, (T, T), 0)
    d_sums = d_cum[...] - flows + jnp.where(row == T - 1, gained, 0.0)
    upper = lower_triangle().astype(f32).T
    d_logs = dot(upper, d_sums, highest)
    rate = -jnp.exp(heads[1:2, :])
    d_delta = direct[...] + d_logs * rate
    slope = sigmoid(xbc[:, DT : DT + T].astype(f32) + heads[0:1, :])
    grad = jnp.where(lane < HEADS, d_delta * slope, 0.0)
    d_dt[...] = grad
    d_heads[...] = jnp.zeros((8, T), f32)
    d_heads[0:1, :] = jnp.sum(grad, axis=0, keepdims=True)
    d_heads[1:2, :] = jnp.sum(d_logs * steps, axis=0, keepdims=True) * rate
    d_heads[2:3, :] = rest[1:2, :]


def bottom_kernel(
    d_conv, halo, taps, d_gate, d_dt, weight, stream, norm, upstream, d_projected, result, d_norm,
    padded, total,
):
    step = pl.program_id(0)

    @pl.when(step == 0)
    def _():
        padded[0:T, :] = d_conv[...]
        padded[T : T + 8, :] = halo[...]
        d_projected[:, 0:DIN] = d_gate[...]
        for j in range(CONV_CH // T):
            value = taps[KW - 1 : KW, block(j)] * padded[0:T, block(j)]
            for k in range(KW - 1):
                shift = KW - 1 - k
                value = value + taps[k : k + 1, block(j)] * padded[shift : shift + T, block(j)]
            d_projected[:, DIN + j * T : DIN + (j + 1) * T] = value.astype(bf16)
        d_projected[:, DT_COL:EINP] = d_dt[...].astype(bf16)
        d_projected[:, EINP:WIDE] = jnp.zeros((T, T), bf16)
        total[...] = jnp.zeros((T, D), f32)

    columns = pl.ds(pl.multiple_of(step * TILE, T), TILE)
    total[...] += dot_nt(d_projected[:, columns], weight[...])

    @pl.when(step == WIDE // TILE - 1)
    def _():
        values = stream[...]
        d_hidden = total[...]
        inverse = lax.rsqrt(jnp.sum(values * values, axis=1, keepdims=True) / D + epsilon)
        d_norm[...] = jnp.broadcast_to(
            jnp.sum(d_hidden * values * inverse, axis=0, keepdims=True), (8, D)
        )
        scaled = d_hidden * norm[...]
        mean = jnp.sum(scaled * values, axis=1, keepdims=True) / D
        pull = inverse * inverse * inverse * mean
        result[...] = upstream[...] + scaled * inverse - values * pull


def dropping(kernel, count, extra):
    return lambda *refs: kernel(*refs[:count], *refs[count + extra :])


def call(kernel, outs, scratch, name, micros, *args, after=()):
    return pl.pallas_call(
        dropping(kernel, len(args), len(after)),
        out_shape=[jax.ShapeDtypeStruct(shape, dtype) for shape, dtype in outs],
        scratch_shapes=[pltpu.VMEM(shape, f32) for shape in scratch],
        compiler_params=pltpu.CompilerParams(vmem_limit_bytes=40 * 2**20),
        in_specs=[pl.BlockSpec(memory_space=pltpu.VMEM)] * len(args)
        + [pl.BlockSpec(memory_space=pl.ANY)] * len(after),
        cost_estimate=cost(micros),
        name=name,
    )(*args, *after)


def cost(micros):
    return pl.CostEstimate(flops=0, transcendentals=0, bytes_accessed=int(micros * 3.5e6))


def whole(array):
    rank = len(array.shape)
    return pl.BlockSpec(array.shape, lambda n: (0,) * rank)


def call_tiled(kernel, steps, args, specs, outs, scratch, name, micros, after=()):
    shapes = [jax.ShapeDtypeStruct(shape, dtype) for shape, dtype, _ in outs]
    return pl.pallas_call(
        dropping(kernel, len(args), len(after)),
        grid=(steps,),
        in_specs=[whole(v) if spec is None else spec for v, spec in zip(args, specs)]
        + [pl.BlockSpec(memory_space=pl.ANY) for _ in after],
        out_specs=[whole(v) if o[2] is None else o[2] for v, o in zip(shapes, outs)],
        out_shape=shapes,
        scratch_shapes=[pltpu.VMEM(shape, f32) for shape in scratch],
        compiler_params=pltpu.CompilerParams(vmem_limit_bytes=44 * 2**20),
        cost_estimate=cost(micros),
        name=name,
    )(*args, *after)


def swap(value):
    return lax.ppermute(value, "section", [(0, 1), (1, 0)])


def to_owners(value):
    came = lax.all_to_all(value, "seq", split_axis=0, concat_axis=0, tiled=True)
    return jnp.sum(came.astype(f32), axis=0)


def to_layers(value):
    me = lax.axis_index("dp")

    def piece(steps):
        return lax.dynamic_index_in_dim(value, (me + steps) % 4, 0, keepdims=False)

    total = piece(0).astype(f32)
    for steps in (1, -1, 2):
        moved = lax.ppermute(piece(steps), "dp", [(i, (i + steps) % 4) for i in range(4)])
        total = total + moved.astype(f32)
    return total


def to_layers_in_order(value):
    me = lax.axis_index("dp")
    came = [lax.dynamic_index_in_dim(value, me, 0, keepdims=False)]
    for steps in (1, 2, 3):
        part = lax.dynamic_index_in_dim(value, (me + steps) % 4, 0, keepdims=False)
        came.append(lax.ppermute(part, "dp", [(i, (i + steps) % 4) for i in range(4)]))
    came = jnp.stack(came)
    total = lax.dynamic_index_in_dim(came, me, 0, keepdims=False)
    for source in (1, 2, 3):
        total = total + lax.dynamic_index_in_dim(came, (me - source) % 4, 0, keepdims=False)
    return total


def in_chip(grad, rows):
    columns = grad.shape[1]
    shaped = grad.reshape(64, 2, rows // 2, columns)
    section = lax.axis_index("section")
    mine = lax.dynamic_index_in_dim(shaped, section, 1, keepdims=False)
    theirs = lax.dynamic_index_in_dim(shaped, 1 - section, 1, keepdims=False)
    total = (mine.astype(f32) + swap(theirs).astype(f32)).astype(bf16)
    return total.reshape(4, 16, rows // 2, columns)


def own_layer(halves_of, first):
    keep = jnp.where(first, halves_of[0], halves_of[1])
    give = jnp.where(first, halves_of[1], halves_of[0])
    came = swap(give.astype(f32))
    keep = keep.astype(f32)
    return jnp.where(
        first, jnp.concatenate([keep, came], axis=0), jnp.concatenate([came, keep], axis=0)
    )


def exchange(payload, backward):
    moved = lax.all_to_all(payload, "seq", split_axis=0, concat_axis=0, tiled=True)
    (entering,) = call(
        lambda *refs: scan_kernel(backward, *refs),
        [((PAIRS, STATE, T), bf16)],
        [],
        "scan_back" if backward else "scan",
        2,
        moved,
    )
    return lax.all_to_all(entering, "seq", split_axis=0, concat_axis=0, tiled=True)


def forward_layer(stream, w):
    l = w["layer"]
    columns = DIN if w["xbc"] is not None else WIDE
    hidden, projected = call_tiled(
        project_kernel,
        columns // TILE,
        (stream, w["norm"], w["all"]),
        (None, None, pl.BlockSpec((D, TILE), lambda n: (l, 4 + n))),
        [((T, D), bf16, None), ((T, columns), bf16, pl.BlockSpec((T, TILE), lambda n: (0, n)))],
        [],
        "project",
        4,
    )
    gates = projected[:, :DIN]
    xbc = projected[:, DIN:] if w["xbc"] is None else w["xbc"]
    halo = lax.ppermute(xbc[T - 16 :, :DT], "seq", [(i, i + 1) for i in range(15)])
    xs, bc, delta, cum, payload = call(
        front_kernel,
        [((T, DIN), f32), ((T, 2 * STATE), bf16), ((T, T), f32), ((T, T), f32), ((PAIRS, PAY, T), bf16)],
        [(T + 16, CONV_CH)],
        "front",
        2,
        xbc,
        halo,
        w["taps"],
        w["heads"],
    )
    entering = exchange(payload, False)
    (local,) = call(within_kernel, [((T, DIN), f32)], [], "within", 2, xs, bc, delta, cum, w["heads"])
    narrow = pl.BlockSpec((T, 512), lambda n: (0, n))
    mixed, normed, result = call_tiled(
        finish_kernel,
        2,
        (local, bc, cum, entering, gates, w["gnorm"], stream, w["all"], w["all"]),
        (None,) * 6
        + (narrow, pl.BlockSpec((D, 512), lambda n: (l, n)), pl.BlockSpec((D, 512), lambda n: (l, 2 + n))),
        [((T, DIN), bf16, None), ((T, DIN), bf16, None), ((T, D), f32, narrow)],
        [(T, DIN), (2, T, D)],
        "finish",
        5,
    )
    return (stream, hidden, gates, xbc, halo, xs, bc, delta, cum, entering, mixed, normed), result


def backward_layer(kept, upstream, w, earlier=None, outputs=()):
    stream, hidden, gates, xbc, halo, xs, bc, delta, cum, entering, mixed, normed = kept
    upstream_low = upstream.astype(bf16)
    l = w["layer"]
    d_mixed, d_gate, d_gain, payload = call_tiled(
        top_kernel,
        2,
        (upstream_low, w["all"], mixed, gates, w["gnorm"], bc, cum),
        (None, pl.BlockSpec((D, D), lambda n: (l, n))) + (None,) * 5,
        [
            ((T, DIN), bf16, None),
            ((T, DIN), bf16, None),
            ((8, DIN), f32, None),
            ((PAIRS, PAY, T), bf16, None),
        ],
        [(2, T, D), (T, DIN), (T, DIN)],
        "top",
        5,
    )
    grad_out = dot_tn(normed, upstream_low).astype(bf16)
    leaving = exchange(payload, True)
    out_total = in_chip(grad_out, 32)
    grad_out = to_layers(out_total).astype(bf16)
    ordered = (grad_out,)
    if earlier is not None:
        leaving, earlier = lax.optimization_barrier((leaving, earlier))
        ordered = (grad_out, earlier)
    d_scaled, d_bc, d_cum = call(
        inner_kernel,
        [((T, DIN), f32), ((T, 2 * STATE), f32), ((T, T), f32)],
        [(T, T), (T, T)],
        "inner",
        8,
        xs,
        bc,
        delta,
        cum,
        d_mixed,
        entering,
    )
    d_conv, d_dt, d_taps, d_heads = call(
        outer_kernel,
        [((T, CONV_CH), f32), ((T, T), f32), ((8, CONV_CH), f32), ((8, T), f32)],
        [(T + 16, CONV_CH), (T, T), (T, T), (8, T)],
        "outer",
        5,
        xbc,
        halo,
        w["taps"],
        w["heads"],
        xs,
        bc,
        delta,
        cum,
        d_mixed,
        d_scaled,
        d_bc,
        d_cum,
        entering,
        leaving,
        after=(out_total, *outputs),
    )
    halo_back = lax.ppermute(d_conv[0:8], "seq", [(i + 1, i) for i in range(15)])
    d_projected, result, d_norm = call_tiled(
        bottom_kernel,
        WIDE // TILE,
        (d_conv, halo_back, w["taps"], d_gate, d_dt, w["all"], stream, w["norm"], upstream),
        (None,) * 5 + (pl.BlockSpec((D, TILE), lambda n: (l, 4 + n)),) + (None,) * 3,
        [((T, WIDE), bf16, None), ((T, D), f32, None), ((8, D), f32, None)],
        [(T + 8, CONV_CH), (T, D)],
        "bottom",
        6,
        ordered,
    )
    grad_in = dot_tn(hidden, d_projected[:, :EINP]).astype(bf16)
    small = pack_small(d_norm[0], d_taps, d_gain[0], d_heads)
    return result, grad_in, grad_out, small, earlier


def pack_small(grad_norm, d_taps, d_gain, d_heads):
    def padded(v):
        return jnp.pad(v, ((0, 0), (0, T - v.shape[1])))

    rows = [padded(d_taps[k].reshape(64, 36)) for k in range(KW + 1)]
    rows.append(padded(grad_norm.reshape(64, 16)))
    rows.append(padded(d_gain.reshape(64, 32)))
    heads = d_heads[0:3, 0:HEADS].reshape(1, 3 * HEADS)
    rows.append(jnp.broadcast_to(padded(heads), (64, T)))
    return jnp.stack(rows, axis=1)


def turned(value, axis, steps):
    if axis == "z":
        return lax.ppermute(value, "dp", [(i, (i + steps) % 4) for i in range(4)])
    pairs = []
    for i in range(16):
        x, y = divmod(i, 4)
        if axis == "x":
            pairs.append((i, (x + steps) % 4 * 4 + y))
        else:
            pairs.append((i, x * 4 + (y + steps) % 4))
    return lax.ppermute(value, "seq", pairs)


def gathered_along(value, axis):
    seq = lax.axis_index("seq")
    me = {"z": lax.axis_index("dp"), "x": seq // 4, "y": seq % 4}[axis]
    out = jnp.zeros((4,) + value.shape, value.dtype)
    came = [value] + [turned(value, axis, steps) for steps in (1, 2, 3)]
    for steps, part in enumerate(came):
        start = ((me - steps) % 4,) + (0,) * value.ndim
        out = lax.dynamic_update_slice(out, part[None], start)
    return out


def normalised(stream):
    return stream * lax.rsqrt(jnp.mean(stream * stream, axis=-1, keepdims=True) + epsilon)


def first_projection(stream, shard, first):
    came = lax.ppermute(shard[8:16], "section", [(0, 1)])
    half = jnp.where(first, shard[0:8], came)
    for axis in ("y", "x", "z"):
        half = gathered_along(half, axis)
    half = half.reshape(512, XBC)
    other = swap(half)
    small = jnp.where(first, half[:, XBC - T :], other[:, XBC - T :]).reshape(64, 8, T)
    parts = normalised(stream).reshape(T, 64, 2, 8)
    parts = parts[:, :, 0, :].reshape(T, 512), parts[:, :, 1, :].reshape(T, 512)
    gain = small[:, 5, :16].astype(f32)
    gains = gain[:, :8].reshape(1, 512), gain[:, 8:].reshape(1, 512)
    low, high = [(part * g).astype(bf16) for part, g in zip(parts, gains)]
    xbc = dot(jnp.where(first, low, high), half) + dot(jnp.where(first, high, low), other)
    return xbc.astype(bf16), small


def gathered_weights(
    stream, norm_gain, w_in, conv_w, conv_b, dt_bias, a_log, d_skip, gnorm_gain, w_out
):
    def tail(v):
        return jnp.pad(v, ((0, 0), (0, T - v.shape[1])))

    first = lax.axis_index("section") == 0
    small = jnp.concatenate(
        [tail(conv_w[0]), tail(conv_b), tail(norm_gain), tail(gnorm_gain), jnp.zeros((9, T), bf16)],
        axis=0,
    )
    mixer_part = jnp.concatenate([jnp.pad(w_in[0, :, DIN:], ((0, 0), (0, EINP - EIN))), small], axis=1)
    payload = jnp.concatenate([w_out[0, 0:16], w_out[0, 16:32], w_in[0, :, :DIN], mixer_part], axis=1)
    everything = lax.all_gather(payload, ("section", "dp", "seq"), axis=0, tiled=True)
    xbc, small_0 = first_projection(stream, mixer_part, first)
    small_1 = everything[D:, payload.shape[1] - T :].reshape(64, 16, T)
    heads = jnp.pad(jnp.concatenate([dt_bias, a_log, d_skip], axis=0), ((0, 5), (0, T - HEADS)))
    other = swap(heads)
    layers = []
    for l, part in enumerate((small_0, small_1)):
        taps = jnp.stack([part[:, k, :36].reshape(CONV_CH) for k in range(KW + 1)]).astype(f32)
        layers.append(
            {
                "layer": l,
                "all": everything,
                "xbc": xbc if l == 0 else None,
                "taps": jnp.pad(taps, ((0, 8 - KW - 1), (0, 0))),
                "norm": part[:, 5, :16].reshape(1, 1024).astype(f32),
                "gnorm": part[:, 6, :32].reshape(1, DIN).astype(f32),
                "heads": jnp.where(first == (l == 0), heads, other),
            }
        )
    return layers


def shards(
    inputs, out_grad, norm_gain, w_in, conv_w, conv_b, dt_bias, a_log, d_skip, gnorm_gain, w_out
):
    section = lax.axis_index("section")
    first = section == 0
    stream = lax.dynamic_index_in_dim(inputs, section, 0, keepdims=False)[0].astype(f32)
    layers = gathered_weights(
        stream, norm_gain, w_in, conv_w, conv_b, dt_bias, a_log, d_skip, gnorm_gain, w_out
    )
    g = lax.dynamic_index_in_dim(out_grad, section, 0, keepdims=False)[0].astype(f32)
    kept = []
    for l in range(2):
        saved, stream = forward_layer(stream, layers[l])
        kept.append(saved)
    outputs = stream.astype(bf16)
    half = outputs.shape[1] // 2

    def by_features(value):
        low, high = value[:, :half], value[:, half:]
        came = swap(jnp.where(first, high, low).astype(bf16)).astype(value.dtype)
        keep = jnp.where(first, low, high)
        return jnp.where(first, jnp.stack([keep, came]), jnp.stack([came, keep]))[:, None]

    out_part = by_features(outputs)
    g, grad_in, out_1, small_1, _ = backward_layer(
        kept[1], g, layers[1], None, (out_part,)
    )
    in_1 = to_layers(in_chip(grad_in, 16)).astype(bf16)
    g, grad_in, out_0, small_0, in_1 = backward_layer(kept[0], g, layers[0], in_1)
    in_1 = to_owners(in_1)
    total_in = in_chip(grad_in, 16)
    total_in, out_0, out_1 = lax.optimization_barrier((total_in, out_0, out_1))
    in_1, small_0, small_1 = lax.optimization_barrier((in_1, small_0, small_1))
    smalls = (small_0, small_1)
    in_halves = (to_owners(to_layers(total_in).astype(bf16)), in_1)
    outs = to_owners(jnp.concatenate([out_0, out_1], axis=1))
    out_halves = (outs[0:16], outs[16:32])
    grad_w_in = own_layer(in_halves, first)[:, :EIN]
    grad_w_out = own_layer(out_halves, first)
    small = jnp.where(first, smalls[0], smalls[1]) + swap(jnp.where(first, smalls[1], smalls[0]))
    small = to_layers_in_order(to_owners(jnp.swapaxes(small.reshape(4, 16, 8, T), 0, 1)))

    return (
        out_part,
        by_features(g),
        small[5:6, :16],
        grad_w_in[None],
        small[None, 0:KW, :36],
        small[KW : KW + 1, :36],
        small[7:8, 0:HEADS],
        small[7:8, HEADS : 2 * HEADS],
        small[7:8, 2 * HEADS : 3 * HEADS],
        small[6:7, :32],
        grad_w_out[None],
    )


def solution(mesh):
    in_specs = (
        P(None, "dp", "seq", None),
        P(None, "dp", "seq", None),
        P("section", both),
        P("section", both, None),
        P("section", None, both),
        P("section", both),
        P("section", None),
        P("section", None),
        P("section", None),
        P("section", both),
        P("section", both, None),
    )
    out_specs = (
        P(None, "dp", "seq", "section"),
        P(None, "dp", "seq", "section"),
        P("section", both),
        P("section", both, None),
        P("section", None, both),
        P("section", both),
        P("section", None),
        P("section", None),
        P("section", None),
        P("section", both),
        P("section", both, None),
    )
    return jax.shard_map(shards, mesh=mesh, in_specs=in_specs, out_specs=out_specs, check_vma=False)
```

```python
import jax
import jax.numpy as jnp
from jax import lax
from jax.experimental import pallas as pl
from jax.experimental.pallas import tpu as pltpu
from jax.sharding import PartitionSpec as P

DIN = 2048
HEADS = 32
STATE = 128
KW = 4
EIN = 4384
EINP = 4480
CONV_CH = 2304
DT_COL = 2 * DIN + 2 * STATE
T = 128
D = 1024
TILE = 512
XBC = 2560
DT = 2304
WIDE = DIN + XBC
PAIRS = 16
PAY = STATE + 16

f32 = jnp.float32
bf16 = jnp.bfloat16
epsilon = 1e-05
highest = lax.Precision.HIGHEST
both = ("dp", "seq")


def dot(a, b, precision=None):
    return jnp.dot(a, b, preferred_element_type=f32, precision=precision)


def dot_nt(a, b):
    return lax.dot_general(a, b, (((1,), (1,)), ((), ())), preferred_element_type=f32)


def dot_tn(a, b):
    return lax.dot_general(a, b, (((0,), (0,)), ((), ())), preferred_element_type=f32)


def low_half():
    return lax.broadcasted_iota(jnp.int32, (1, T), 1) < 64


def lower_triangle():
    rows = lax.broadcasted_iota(jnp.int32, (T, T), 0)
    columns = lax.broadcasted_iota(jnp.int32, (T, T), 1)
    return rows >= columns


def sigmoid(v):
    return 1.0 / (1.0 + jnp.exp(-v))


def silu_and_slope(v):
    s = sigmoid(v)
    return v * s, s * (1.0 + v * (1.0 - s))


def spread(table, j):
    return jnp.where(low_half(), table[:, 2 * j : 2 * j + 1], table[:, 2 * j + 1 : 2 * j + 2])


def block(j):
    return slice(j * T, (j + 1) * T)


def conv_block(padded, taps, j):
    total = taps[KW : KW + 1, block(j)] + taps[0:1, block(j)] * padded[13 : 13 + T, block(j)]
    for k in range(1, KW):
        total = total + taps[k : k + 1, block(j)] * padded[13 + k : 13 + k + T, block(j)]
    return total


def load_padded(padded, xbc, halo):
    padded[0:16, :] = halo[...].astype(f32)
    padded[16 : 16 + T, :] = xbc[:, 0:DT].astype(f32)


def put_payload(payload, j, state, totals):
    payload[j, 0:STATE, :] = state.astype(bf16)
    factor = spread(totals, j)
    high = factor.astype(bf16).astype(f32)
    rest = factor - high
    row = lax.broadcasted_iota(jnp.int32, (16, T), 0)
    extra = jnp.where(row == 0, high, jnp.where(row == 1, rest, 0.0))
    payload[j, STATE:PAY, :] = extra.astype(bf16)


def shuffle():
    source = lax.broadcasted_iota(jnp.int32, (256, 256), 0)
    target = lax.broadcasted_iota(jnp.int32, (256, 256), 1)
    k, i, r = source >> 5, (source >> 4) & 1, source & 15
    return jnp.where(target == i * T + k * 16 + r, 1.0, 0.0).astype(bf16)


def front_kernel(xbc, halo, taps, heads, xs, bc, delta, cum, payload, padded):
    load_padded(padded, xbc, halo)
    lane = lax.broadcasted_iota(jnp.int32, (1, T), 1)
    raw = xbc[:, DT : DT + T].astype(f32) + heads[0:1, :]
    soft = jnp.maximum(raw, 0.0) + jnp.log1p(jnp.exp(-jnp.abs(raw)))
    steps = jnp.where(lane < HEADS, soft, 0.0)
    delta[...] = steps
    logs = steps * -jnp.exp(heads[1:2, :])
    sums = dot(lower_triangle().astype(f32), logs, highest)
    cum[...] = sums
    last = sums[T - 1 : T, :]
    weight = jnp.exp(last - sums) * steps
    totals = jnp.exp(last)
    b_pre = conv_block(padded, taps, PAIRS)
    c_pre = conv_block(padded, taps, PAIRS + 1)
    keys = b_pre * sigmoid(b_pre)
    bc[:, 0:STATE] = keys.astype(bf16)
    bc[:, STATE:] = (c_pre * sigmoid(c_pre)).astype(bf16)
    keys_t = keys.T.astype(bf16)
    for j in range(PAIRS):
        pre = conv_block(padded, taps, j)
        x = pre * sigmoid(pre)
        xs[:, block(j)] = x
        put_payload(payload, j, dot(keys_t, (spread(weight, j) * x).astype(bf16)), totals)


def scan_kernel(backward, payload, entering):
    carried = jnp.zeros((STATE, T), f32)
    order = range(PAIRS - 1, -1, -1) if backward else range(PAIRS)
    for k in order:
        entering[k] = carried.astype(bf16)
        extra = payload[k, STATE:PAY, :].astype(f32)
        factor = extra[0:1, :] + extra[1:2, :]
        carried = factor * carried + payload[k, 0:STATE, :].astype(f32)


def decay(cum, cum_t, h, causal):
    return jnp.where(causal, jnp.exp(cum[:, h : h + 1] - cum_t[h : h + 1, :]), 0.0)


def halves(v):
    return jnp.concatenate(
        [jnp.where(low_half(), v, 0.0), jnp.where(low_half(), 0.0, v)], axis=0
    ).astype(bf16)


def within_kernel(xs, bc, delta, cum, heads, local):
    causal = lower_triangle()
    cums = cum[...]
    cum_t = cums.T
    steps = delta[...]
    skips = heads[2:3, :]
    scores = dot_nt(bc[:, STATE:], bc[:, 0:STATE])
    for j in range(PAIRS):
        x = xs[:, block(j)]
        mixing = jnp.concatenate(
            [scores * decay(cums, cum_t, 2 * j + i, causal) for i in range(2)], axis=1
        ).astype(bf16)
        local[:, block(j)] = dot(mixing, halves(spread(steps, j) * x)) + spread(skips, j) * x


def project_kernel(stream, gain, weight, hidden, projected):
    @pl.when(pl.program_id(0) == 0)
    def _():
        values = stream[...]
        inverse = lax.rsqrt(jnp.sum(values * values, axis=1, keepdims=True) / D + epsilon)
        hidden[...] = (values * inverse * gain[...]).astype(bf16)

    projected[...] = dot(hidden[...], weight[...]).astype(bf16)


def finish_kernel(
    local, bc, cum, entering, gates, gain, stream, weight_0, weight_1, mixed, normed, result, gated,
    shuffled,
):
    @pl.when(pl.program_id(0) == 0)
    def _():
        growth = jnp.exp(cum[...])
        queries = bc[:, STATE:]
        squares = jnp.zeros((T, T), f32)
        for j in range(PAIRS):
            whole = local[:, block(j)] + spread(growth, j) * dot(queries, entering[j])
            rounded = whole.astype(bf16)
            mixed[:, block(j)] = rounded
            gate = gates[:, block(j)].astype(f32)
            u = rounded.astype(f32) * (gate * sigmoid(gate))
            gated[:, block(j)] = u
            squares = squares + u * u
        scale = lax.rsqrt(jnp.sum(squares, axis=1, keepdims=True) / DIN + epsilon)
        for j in range(PAIRS):
            normed[:, block(j)] = (gated[:, block(j)] * scale * gain[0:1, block(j)]).astype(bf16)

        order = shuffle()
        for b in range(8):
            moved = dot(normed[:, b * 256 : (b + 1) * 256], order)
            shuffled[0, :, block(b)] = moved[:, 0:T]
            shuffled[1, :, block(b)] = moved[:, T:]

    result[...] = (
        stream[...]
        + dot(shuffled[0].astype(bf16), weight_0[...])
        + dot(shuffled[1].astype(bf16), weight_1[...])
    )


def top_kernel(
    upstream, weight, mixed, gates, gain, bc, cum, d_mixed, d_gate, d_gain, payload, d_shuffled,
    d_normed, gated,
):
    step = pl.program_id(0)
    d_shuffled[step] = dot_nt(upstream[...], weight[...])

    def part(j):
        return d_normed[:, block(j)]

    @pl.when(step == 1)
    def _():
        order = shuffle()
        for b in range(8):
            value = jnp.concatenate([d_shuffled[0, :, block(b)], d_shuffled[1, :, block(b)]], axis=1)
            high = value.astype(bf16)
            rest = (value - high.astype(f32)).astype(bf16)
            d_normed[:, b * 256 : (b + 1) * 256] = dot_nt(high, order) + dot_nt(rest, order)
        squares = jnp.zeros((T, T), f32)
        products = jnp.zeros((T, T), f32)
        for j in range(PAIRS):
            gate = gates[:, block(j)].astype(f32)
            u = mixed[:, block(j)].astype(f32) * (gate * sigmoid(gate))
            gated[:, block(j)] = u
            squares = squares + u * u
            products = products + part(j) * gain[0:1, block(j)] * u
        scale = lax.rsqrt(jnp.sum(squares, axis=1, keepdims=True) / DIN + epsilon)
        pull = scale * scale * scale * (jnp.sum(products, axis=1, keepdims=True) / DIN)
        cums = cum[...]
        growth = jnp.exp(cums)
        totals = growth[T - 1 : T, :]
        queries_t = bc[:, STATE:].astype(f32).T.astype(bf16)
        for j in range(PAIRS):
            gate = gates[:, block(j)].astype(f32)
            act, slope = silu_and_slope(gate)
            u = gated[:, block(j)]
            up = part(j)
            d_gain[:, block(j)] = jnp.broadcast_to(
                jnp.sum(up * u * scale, axis=0, keepdims=True), (8, T)
            )
            du = up * gain[0:1, block(j)] * scale - u * pull
            dm = (du * act).astype(bf16)
            d_mixed[:, block(j)] = dm
            d_gate[:, block(j)] = (du * mixed[:, block(j)].astype(f32) * slope).astype(bf16)
            put_payload(
                payload, j, dot(queries_t, (spread(growth, j) * dm.astype(f32)).astype(bf16)), totals
            )


def inner_kernel(xs, bc, delta, cum, d_mixed, entering, d_scaled, d_bc, d_cum, rows, columns):
    causal = lower_triangle()
    cums = cum[...]
    cum_t = cums.T
    steps = delta[...]
    growth = jnp.exp(cums)
    keys = bc[:, 0:STATE]
    queries = bc[:, STATE:]
    scores = dot_nt(queries, keys)
    rows[...] = jnp.zeros((T, T), f32)
    columns[...] = jnp.zeros((T, T), f32)
    d_scores = jnp.zeros((T, T), f32)
    d_queries = jnp.zeros((T, STATE), f32)
    for j in range(PAIRS):
        dy_low = d_mixed[:, block(j)]
        dy = dy_low.astype(f32)
        scaled = halves(spread(steps, j) * xs[:, block(j)])
        d_mixing = dot_nt(dy_low, scaled)
        grown = spread(growth, j) * dy
        across = grown * dot(queries, entering[j])
        d_queries = d_queries + dot_nt(grown.astype(bf16), entering[j])
        mixings = []
        for i in range(2):
            h = 2 * j + i
            fall = decay(cums, cum_t, h, causal)
            d_part = d_mixing[:, i * T : (i + 1) * T] * fall
            d_scores = d_scores + d_part
            mixings.append(scores * fall)
            logs = d_part * scores
            own = jnp.where(low_half(), across, 0.0) if i == 0 else jnp.where(low_half(), 0.0, across)
            rows[:, h : h + 1] = jnp.sum(logs + own, axis=1, keepdims=True)
            columns[h : h + 1, :] = jnp.sum(logs, axis=0, keepdims=True)
        d_scaled[:, block(j)] = dot_tn(
            jnp.concatenate(mixings, axis=0).astype(bf16), halves(dy)
        )
    d_low = d_scores.astype(bf16)
    d_bc[:, 0:STATE] = dot_tn(d_low, queries)
    d_bc[:, STATE:] = d_queries + dot(d_low, keys)
    d_cum[...] = rows[...] - columns[...].T


def outer_kernel(
    xbc, halo, taps, heads, xs, bc, delta, cum, d_mixed, d_scaled, d_bc, d_cum, entering,
    leaving, d_conv, d_dt, d_taps, d_heads, padded, falls, direct, rest,
):
    load_padded(padded, xbc, halo)
    lane = lax.broadcasted_iota(jnp.int32, (1, T), 1)
    cums = cum[...]
    steps = delta[...]
    last = cums[T - 1 : T, :]
    weight = jnp.exp(last - cums)
    totals = jnp.exp(last)
    skips = heads[2:3, :]
    keys = bc[:, 0:STATE]
    falls[...] = jnp.zeros((T, T), f32)
    direct[...] = jnp.zeros((T, T), f32)
    rest[...] = jnp.zeros((8, T), f32)
    low = low_half()

    def conv_back(j, grad):
        pre = conv_block(padded, taps, j)
        d_pre = grad * silu_and_slope(pre)[1]
        d_conv[:, block(j)] = d_pre
        for k in range(KW):
            d_taps[k : k + 1, block(j)] = jnp.sum(
                d_pre * padded[13 + k : 13 + k + T, block(j)], axis=0, keepdims=True
            )
        d_taps[KW : KW + 1, block(j)] = jnp.sum(d_pre, axis=0, keepdims=True)

    d_taps[KW + 1 : 8, :] = jnp.zeros((8 - KW - 1, CONV_CH), f32)
    d_keys = d_bc[:, 0:STATE]
    for j in range(PAIRS):
        x = xs[:, block(j)]
        dy = d_mixed[:, block(j)].astype(f32)
        step = spread(steps, j)
        fall = spread(weight, j)
        weighted = fall * (step * x)
        back = dot(keys, leaving[j])
        d_keys = d_keys + dot_nt(weighted.astype(bf16), leaving[j])
        ds = d_scaled[:, block(j)] + fall * back
        flow = weighted * back
        touch = ds * x
        kept = jnp.sum(leaving[j].astype(f32) * entering[j].astype(f32), axis=0, keepdims=True)
        kept = kept * spread(totals, j)
        skipped = jnp.sum(dy * x, axis=0, keepdims=True)
        for i in range(2):
            h = 2 * j + i
            pick = (lambda v: jnp.where(low, v, 0.0)) if i == 0 else (lambda v: jnp.where(low, 0.0, v))
            falls[:, h : h + 1] = jnp.sum(pick(flow), axis=1, keepdims=True)
            direct[:, h : h + 1] = jnp.sum(pick(touch), axis=1, keepdims=True)
            rest[0:1, h : h + 1] = jnp.sum(pick(kept), axis=1, keepdims=True)
            rest[1:2, h : h + 1] = jnp.sum(pick(skipped), axis=1, keepdims=True)
        conv_back(j, step * ds + spread(skips, j) * dy)
    conv_back(PAIRS, d_keys)
    conv_back(PAIRS + 1, d_bc[:, STATE:])
    flows = falls[...]
    gained = rest[0:1, :] + jnp.sum(flows, axis=0, keepdims=True)
    row = lax.broadcasted_iota(jnp.int32, (T, T), 0)
    d_sums = d_cum[...] - flows + jnp.where(row == T - 1, gained, 0.0)
    upper = lower_triangle().astype(f32).T
    d_logs = dot(upper, d_sums, highest)
    rate = -jnp.exp(heads[1:2, :])
    d_delta = direct[...] + d_logs * rate
    slope = sigmoid(xbc[:, DT : DT + T].astype(f32) + heads[0:1, :])
    grad = jnp.where(lane < HEADS, d_delta * slope, 0.0)
    d_dt[...] = grad
    d_heads[...] = jnp.zeros((8, T), f32)
    d_heads[0:1, :] = jnp.sum(grad, axis=0, keepdims=True)
    d_heads[1:2, :] = jnp.sum(d_logs * steps, axis=0, keepdims=True) * rate
    d_heads[2:3, :] = rest[1:2, :]


def bottom_kernel(
    d_conv, halo, taps, d_gate, d_dt, weight, stream, norm, upstream, d_projected, result, d_norm,
    padded, total,
):
    step = pl.program_id(0)

    @pl.when(step == 0)
    def _():
        padded[0:T, :] = d_conv[...]
        padded[T : T + 8, :] = halo[...]
        d_projected[:, 0:DIN] = d_gate[...]
        for j in range(CONV_CH // T):
            value = taps[KW - 1 : KW, block(j)] * padded[0:T, block(j)]
            for k in range(KW - 1):
                shift = KW - 1 - k
                value = value + taps[k : k + 1, block(j)] * padded[shift : shift + T, block(j)]
            d_projected[:, DIN + j * T : DIN + (j + 1) * T] = value.astype(bf16)
        d_projected[:, DT_COL:EINP] = d_dt[...].astype(bf16)
        d_projected[:, EINP:WIDE] = jnp.zeros((T, T), bf16)
        total[...] = jnp.zeros((T, D), f32)

    columns = pl.ds(pl.multiple_of(step * TILE, T), TILE)
    total[...] += dot_nt(d_projected[:, columns], weight[...])

    @pl.when(step == WIDE // TILE - 1)
    def _():
        values = stream[...]
        d_hidden = total[...]
        inverse = lax.rsqrt(jnp.sum(values * values, axis=1, keepdims=True) / D + epsilon)
        d_norm[...] = jnp.broadcast_to(
            jnp.sum(d_hidden * values * inverse, axis=0, keepdims=True), (8, D)
        )
        scaled = d_hidden * norm[...]
        mean = jnp.sum(scaled * values, axis=1, keepdims=True) / D
        pull = inverse * inverse * inverse * mean
        result[...] = upstream[...] + scaled * inverse - values * pull


def dropping(kernel, count, extra):
    return lambda *refs: kernel(*refs[:count], *refs[count + extra :])


def call(kernel, outs, scratch, name, micros, *args, after=()):
    return pl.pallas_call(
        dropping(kernel, len(args), len(after)),
        out_shape=[jax.ShapeDtypeStruct(shape, dtype) for shape, dtype in outs],
        scratch_shapes=[pltpu.VMEM(shape, f32) for shape in scratch],
        compiler_params=pltpu.CompilerParams(vmem_limit_bytes=40 * 2**20),
        in_specs=[pl.BlockSpec(memory_space=pltpu.VMEM)] * len(args)
        + [pl.BlockSpec(memory_space=pl.ANY)] * len(after),
        cost_estimate=cost(micros),
        name=name,
    )(*args, *after)


def cost(micros):
    return pl.CostEstimate(flops=0, transcendentals=0, bytes_accessed=int(micros * 3.5e6))


def whole(array):
    rank = len(array.shape)
    return pl.BlockSpec(array.shape, lambda n: (0,) * rank)


def call_tiled(kernel, steps, args, specs, outs, scratch, name, micros, after=()):
    shapes = [jax.ShapeDtypeStruct(shape, dtype) for shape, dtype, _ in outs]
    return pl.pallas_call(
        dropping(kernel, len(args), len(after)),
        grid=(steps,),
        in_specs=[whole(v) if spec is None else spec for v, spec in zip(args, specs)]
        + [pl.BlockSpec(memory_space=pl.ANY) for _ in after],
        out_specs=[whole(v) if o[2] is None else o[2] for v, o in zip(shapes, outs)],
        out_shape=shapes,
        scratch_shapes=[pltpu.VMEM(shape, f32) for shape in scratch],
        compiler_params=pltpu.CompilerParams(vmem_limit_bytes=44 * 2**20),
        cost_estimate=cost(micros),
        name=name,
    )(*args, *after)


def swap(value):
    return lax.ppermute(value, "section", [(0, 1), (1, 0)])


def to_owners(value):
    came = lax.all_to_all(value, "seq", split_axis=0, concat_axis=0, tiled=True)
    return jnp.sum(came.astype(f32), axis=0)


def to_layers(value):
    me = lax.axis_index("dp")

    def piece(steps):
        return lax.dynamic_index_in_dim(value, (me + steps) % 4, 0, keepdims=False)

    total = piece(0).astype(f32)
    for steps in (1, -1, 2):
        moved = lax.ppermute(piece(steps), "dp", [(i, (i + steps) % 4) for i in range(4)])
        total = total + moved.astype(f32)
    return total


def to_layers_in_order(value):
    me = lax.axis_index("dp")
    came = [lax.dynamic_index_in_dim(value, me, 0, keepdims=False)]
    for steps in (1, 2, 3):
        part = lax.dynamic_index_in_dim(value, (me + steps) % 4, 0, keepdims=False)
        came.append(lax.ppermute(part, "dp", [(i, (i + steps) % 4) for i in range(4)]))
    came = jnp.stack(came)
    total = lax.dynamic_index_in_dim(came, me, 0, keepdims=False)
    for source in (1, 2, 3):
        total = total + lax.dynamic_index_in_dim(came, (me - source) % 4, 0, keepdims=False)
    return total


def in_chip(grad, rows):
    columns = grad.shape[1]
    shaped = grad.reshape(64, 2, rows // 2, columns)
    section = lax.axis_index("section")
    mine = lax.dynamic_index_in_dim(shaped, section, 1, keepdims=False)
    theirs = lax.dynamic_index_in_dim(shaped, 1 - section, 1, keepdims=False)
    total = (mine.astype(f32) + swap(theirs).astype(f32)).astype(bf16)
    return total.reshape(4, 16, rows // 2, columns)


def own_layer(halves_of, first):
    keep = jnp.where(first, halves_of[0], halves_of[1])
    give = jnp.where(first, halves_of[1], halves_of[0])
    came = swap(give.astype(f32))
    keep = keep.astype(f32)
    return jnp.where(
        first, jnp.concatenate([keep, came], axis=0), jnp.concatenate([came, keep], axis=0)
    )


def exchange(payload, backward):
    moved = lax.all_to_all(payload, "seq", split_axis=0, concat_axis=0, tiled=True)
    (entering,) = call(
        lambda *refs: scan_kernel(backward, *refs),
        [((PAIRS, STATE, T), bf16)],
        [],
        "scan_back" if backward else "scan",
        2,
        moved,
    )
    return lax.all_to_all(entering, "seq", split_axis=0, concat_axis=0, tiled=True)


def forward_layer(stream, w):
    l = w["layer"]
    columns = DIN if w["xbc"] is not None else WIDE
    hidden, projected = call_tiled(
        project_kernel,
        columns // TILE,
        (stream, w["norm"], w["all"]),
        (None, None, pl.BlockSpec((D, TILE), lambda n: (l, 4 + n))),
        [((T, D), bf16, None), ((T, columns), bf16, pl.BlockSpec((T, TILE), lambda n: (0, n)))],
        [],
        "project",
        4,
    )
    gates = projected[:, :DIN]
    xbc = projected[:, DIN:] if w["xbc"] is None else w["xbc"]
    halo = lax.ppermute(xbc[T - 16 :, :DT], "seq", [(i, i + 1) for i in range(15)])
    xs, bc, delta, cum, payload = call(
        front_kernel,
        [((T, DIN), f32), ((T, 2 * STATE), bf16), ((T, T), f32), ((T, T), f32), ((PAIRS, PAY, T), bf16)],
        [(T + 16, CONV_CH)],
        "front",
        2,
        xbc,
        halo,
        w["taps"],
        w["heads"],
    )
    entering = exchange(payload, False)
    (local,) = call(within_kernel, [((T, DIN), f32)], [], "within", 2, xs, bc, delta, cum, w["heads"])
    narrow = pl.BlockSpec((T, 512), lambda n: (0, n))
    mixed, normed, result = call_tiled(
        finish_kernel,
        2,
        (local, bc, cum, entering, gates, w["gnorm"], stream, w["all"], w["all"]),
        (None,) * 6
        + (narrow, pl.BlockSpec((D, 512), lambda n: (l, n)), pl.BlockSpec((D, 512), lambda n: (l, 2 + n))),
        [((T, DIN), bf16, None), ((T, DIN), bf16, None), ((T, D), f32, narrow)],
        [(T, DIN), (2, T, D)],
        "finish",
        5,
    )
    return (stream, hidden, gates, xbc, halo, xs, bc, delta, cum, entering, mixed, normed), result


def backward_layer(kept, upstream, w, earlier=None, outputs=()):
    stream, hidden, gates, xbc, halo, xs, bc, delta, cum, entering, mixed, normed = kept
    upstream_low = upstream.astype(bf16)
    l = w["layer"]
    d_mixed, d_gate, d_gain, payload = call_tiled(
        top_kernel,
        2,
        (upstream_low, w["all"], mixed, gates, w["gnorm"], bc, cum),
        (None, pl.BlockSpec((D, D), lambda n: (l, n))) + (None,) * 5,
        [
            ((T, DIN), bf16, None),
            ((T, DIN), bf16, None),
            ((8, DIN), f32, None),
            ((PAIRS, PAY, T), bf16, None),
        ],
        [(2, T, D), (T, DIN), (T, DIN)],
        "top",
        5,
        () if earlier is None else earlier[1:],
    )
    grad_out = dot_tn(normed, upstream_low).astype(bf16)
    leaving = exchange(payload, True)
    out_total = in_chip(grad_out, 32)
    grad_out = to_layers(out_total).astype(bf16)
    ordered, grad_gate = (grad_out,), None
    if earlier is not None:
        leaving, came = lax.optimization_barrier((leaving, earlier[0]))
        came = to_owners(came)
        total_gate = in_chip(dot_tn(hidden, d_gate).astype(bf16), 16)
        ordered = (grad_out, came, total_gate)
        grad_gate = to_layers(total_gate).astype(bf16)
    d_scaled, d_bc, d_cum = call(
        inner_kernel,
        [((T, DIN), f32), ((T, 2 * STATE), f32), ((T, T), f32)],
        [(T, T), (T, T)],
        "inner",
        8,
        xs,
        bc,
        delta,
        cum,
        d_mixed,
        entering,
    )
    d_conv, d_dt, d_taps, d_heads = call(
        outer_kernel,
        [((T, CONV_CH), f32), ((T, T), f32), ((8, CONV_CH), f32), ((8, T), f32)],
        [(T + 16, CONV_CH), (T, T), (T, T), (8, T)],
        "outer",
        5,
        xbc,
        halo,
        w["taps"],
        w["heads"],
        xs,
        bc,
        delta,
        cum,
        d_mixed,
        d_scaled,
        d_bc,
        d_cum,
        entering,
        leaving,
        after=(out_total, *outputs),
    )
    halo_back = lax.ppermute(d_conv[0:8], "seq", [(i + 1, i) for i in range(15)])
    d_projected, result, d_norm = call_tiled(
        bottom_kernel,
        WIDE // TILE,
        (d_conv, halo_back, w["taps"], d_gate, d_dt, w["all"], stream, w["norm"], upstream),
        (None,) * 5 + (pl.BlockSpec((D, TILE), lambda n: (l, 4 + n)),) + (None,) * 3,
        [((T, WIDE), bf16, None), ((T, D), f32, None), ((8, D), f32, None)],
        [(T + 8, CONV_CH), (T, D)],
        "bottom",
        6,
        ordered,
    )
    start = 0 if earlier is None else DIN
    grad_in = dot_tn(hidden, d_projected[:, start:EINP]).astype(bf16)
    small = pack_small(d_norm[0], d_taps, d_gain[0], d_heads)
    if earlier is None:
        return result, grad_in, grad_out, small
    return result, grad_gate, grad_in, grad_out, small, came


def pack_small(grad_norm, d_taps, d_gain, d_heads):
    def padded(v):
        return jnp.pad(v, ((0, 0), (0, T - v.shape[1])))

    rows = [padded(d_taps[k].reshape(64, 36)) for k in range(KW + 1)]
    rows.append(padded(grad_norm.reshape(64, 16)))
    rows.append(padded(d_gain.reshape(64, 32)))
    heads = d_heads[0:3, 0:HEADS].reshape(1, 3 * HEADS)
    rows.append(jnp.broadcast_to(padded(heads), (64, T)))
    return jnp.stack(rows, axis=1)


def turned(value, axis, steps):
    if axis == "z":
        return lax.ppermute(value, "dp", [(i, (i + steps) % 4) for i in range(4)])
    pairs = []
    for i in range(16):
        x, y = divmod(i, 4)
        if axis == "x":
            pairs.append((i, (x + steps) % 4 * 4 + y))
        else:
            pairs.append((i, x * 4 + (y + steps) % 4))
    return lax.ppermute(value, "seq", pairs)


def gathered_along(value, axis):
    seq = lax.axis_index("seq")
    me = {"z": lax.axis_index("dp"), "x": seq // 4, "y": seq % 4}[axis]
    out = jnp.zeros((4,) + value.shape, value.dtype)
    came = [value] + [turned(value, axis, steps) for steps in (1, 2, 3)]
    for steps, part in enumerate(came):
        start = ((me - steps) % 4,) + (0,) * value.ndim
        out = lax.dynamic_update_slice(out, part[None], start)
    return out


def normalised(stream):
    return stream * lax.rsqrt(jnp.mean(stream * stream, axis=-1, keepdims=True) + epsilon)


def first_projection(stream, shard, first):
    came = lax.ppermute(shard[8:16], "section", [(0, 1)])
    half = jnp.where(first, shard[0:8], came)
    for axis in ("y", "x"):
        half = gathered_along(half, axis)
    parts = normalised(stream).reshape(T, 64, 2, 8)
    parts = parts[:, :, 0, :].reshape(T, 512), parts[:, :, 1, :].reshape(T, 512)
    half, parts = lax.optimization_barrier((half, parts))
    half = gathered_along(half, "z")
    half = half.reshape(512, XBC)
    other = swap(half)
    small = jnp.where(first, half[:, XBC - T :], other[:, XBC - T :]).reshape(64, 8, T)
    gain = small[:, 5, :16].astype(f32)
    gains = gain[:, :8].reshape(1, 512), gain[:, 8:].reshape(1, 512)
    low, high = [(part * g).astype(bf16) for part, g in zip(parts, gains)]
    xbc = dot(jnp.where(first, low, high), half) + dot(jnp.where(first, high, low), other)
    return xbc.astype(bf16), small


def gathered_weights(
    stream, norm_gain, w_in, conv_w, conv_b, dt_bias, a_log, d_skip, gnorm_gain, w_out
):
    def tail(v):
        return jnp.pad(v, ((0, 0), (0, T - v.shape[1])))

    first = lax.axis_index("section") == 0
    small = jnp.concatenate(
        [tail(conv_w[0]), tail(conv_b), tail(norm_gain), tail(gnorm_gain), jnp.zeros((9, T), bf16)],
        axis=0,
    )
    mixer_part = jnp.concatenate([jnp.pad(w_in[0, :, DIN:], ((0, 0), (0, EINP - EIN))), small], axis=1)
    payload = jnp.concatenate([w_out[0, 0:16], w_out[0, 16:32], w_in[0, :, :DIN], mixer_part], axis=1)
    everything = lax.all_gather(payload, ("section", "dp", "seq"), axis=0, tiled=True)
    xbc, small_0 = first_projection(stream, mixer_part, first)
    small_1 = everything[D:, payload.shape[1] - T :].reshape(64, 16, T)
    heads = jnp.pad(jnp.concatenate([dt_bias, a_log, d_skip], axis=0), ((0, 5), (0, T - HEADS)))
    other = swap(heads)
    layers = []
    for l, part in enumerate((small_0, small_1)):
        taps = jnp.stack([part[:, k, :36].reshape(CONV_CH) for k in range(KW + 1)]).astype(f32)
        layers.append(
            {
                "layer": l,
                "all": everything,
                "xbc": xbc if l == 0 else None,
                "taps": jnp.pad(taps, ((0, 8 - KW - 1), (0, 0))),
                "norm": part[:, 5, :16].reshape(1, 1024).astype(f32),
                "gnorm": part[:, 6, :32].reshape(1, DIN).astype(f32),
                "heads": jnp.where(first == (l == 0), heads, other),
            }
        )
    return layers


def shards(
    inputs, out_grad, norm_gain, w_in, conv_w, conv_b, dt_bias, a_log, d_skip, gnorm_gain, w_out
):
    section = lax.axis_index("section")
    first = section == 0
    stream = lax.dynamic_index_in_dim(inputs, section, 0, keepdims=False)[0].astype(f32)
    layers = gathered_weights(
        stream, norm_gain, w_in, conv_w, conv_b, dt_bias, a_log, d_skip, gnorm_gain, w_out
    )
    g = lax.dynamic_index_in_dim(out_grad, section, 0, keepdims=False)[0].astype(f32)
    kept = []
    for l in range(2):
        saved, stream = forward_layer(stream, layers[l])
        kept.append(saved)
    outputs = stream.astype(bf16)
    half = outputs.shape[1] // 2

    def by_features(value):
        low, high = value[:, :half], value[:, half:]
        came = swap(jnp.where(first, high, low).astype(bf16)).astype(value.dtype)
        keep = jnp.where(first, low, high)
        return jnp.where(first, jnp.stack([keep, came]), jnp.stack([came, keep]))[:, None]

    out_part = by_features(outputs)
    g, grad_in, out_1, small_1 = backward_layer(kept[1], g, layers[1], None, (out_part,))
    out_1 = to_owners(out_1)
    in_1 = to_layers(in_chip(grad_in, 16)).astype(bf16)
    g, grad_gate, grad_in, out_0, small_0, in_1 = backward_layer(
        kept[0], g, layers[0], (in_1, out_1)
    )
    total_in = in_chip(grad_in, 16)
    total_in, grad_gate, small_0, small_1 = lax.optimization_barrier(
        (total_in, grad_gate, small_0, small_1)
    )
    smalls = (small_0, small_1)
    grad_in = to_owners(to_layers(total_in).astype(bf16))
    in_halves = (jnp.concatenate([to_owners(grad_gate), grad_in], axis=-1), in_1)
    out_halves = (to_owners(out_0), out_1)
    grad_w_in = own_layer(in_halves, first)[:, :EIN]
    grad_w_out = own_layer(out_halves, first)
    small = jnp.where(first, smalls[0], smalls[1]) + swap(jnp.where(first, smalls[1], smalls[0]))
    small = to_layers_in_order(to_owners(jnp.swapaxes(small.reshape(4, 16, 8, T), 0, 1)))

    return (
        out_part,
        by_features(g),
        small[5:6, :16],
        grad_w_in[None],
        small[None, 0:KW, :36],
        small[KW : KW + 1, :36],
        small[7:8, 0:HEADS],
        small[7:8, HEADS : 2 * HEADS],
        small[7:8, 2 * HEADS : 3 * HEADS],
        small[6:7, :32],
        grad_w_out[None],
    )


def solution(mesh):
    in_specs = (
        P(None, "dp", "seq", None),
        P(None, "dp", "seq", None),
        P("section", both),
        P("section", both, None),
        P("section", None, both),
        P("section", both),
        P("section", None),
        P("section", None),
        P("section", None),
        P("section", both),
        P("section", both, None),
    )
    out_specs = (
        P(None, "dp", "seq", "section"),
        P(None, "dp", "seq", "section"),
        P("section", both),
        P("section", both, None),
        P("section", None, both),
        P("section", both),
        P("section", None),
        P("section", None),
        P("section", None),
        P("section", both),
        P("section", both, None),
    )
    return jax.shard_map(shards, mesh=mesh, in_specs=in_specs, out_specs=out_specs, check_vma=False)
```

```python
import jax
import jax.numpy as jnp
from jax import lax
from jax.experimental import pallas as pl
from jax.experimental.pallas import tpu as pltpu
from jax.sharding import PartitionSpec as P

DIN = 2048
HEADS = 32
STATE = 128
KW = 4
EIN = 4384
EINP = 4480
CONV_CH = 2304
DT_COL = 2 * DIN + 2 * STATE
T = 128
D = 1024
TILE = 512
XBC = 2560
DT = 2304
WIDE = DIN + XBC
PAIRS = 16
PAY = STATE + 16

f32 = jnp.float32
bf16 = jnp.bfloat16
epsilon = 1e-05
highest = lax.Precision.HIGHEST
both = ("dp", "seq")


def dot(a, b, precision=None):
    return jnp.dot(a, b, preferred_element_type=f32, precision=precision)


def dot_nt(a, b):
    return lax.dot_general(a, b, (((1,), (1,)), ((), ())), preferred_element_type=f32)


def dot_tn(a, b):
    return lax.dot_general(a, b, (((0,), (0,)), ((), ())), preferred_element_type=f32)


def low_half():
    return lax.broadcasted_iota(jnp.int32, (1, T), 1) < 64


def lower_triangle():
    rows = lax.broadcasted_iota(jnp.int32, (T, T), 0)
    columns = lax.broadcasted_iota(jnp.int32, (T, T), 1)
    return rows >= columns


def sigmoid(v):
    return 1.0 / (1.0 + jnp.exp(-v))


def silu_and_slope(v):
    s = sigmoid(v)
    return v * s, s * (1.0 + v * (1.0 - s))


def spread(table, j):
    return jnp.where(low_half(), table[:, 2 * j : 2 * j + 1], table[:, 2 * j + 1 : 2 * j + 2])


def block(j):
    return slice(j * T, (j + 1) * T)


def conv_block(padded, taps, j):
    total = taps[KW : KW + 1, block(j)] + taps[0:1, block(j)] * padded[13 : 13 + T, block(j)]
    for k in range(1, KW):
        total = total + taps[k : k + 1, block(j)] * padded[13 + k : 13 + k + T, block(j)]
    return total


def load_padded(padded, xbc, halo):
    padded[0:16, :] = halo[...].astype(f32)
    padded[16 : 16 + T, :] = xbc[:, 0:DT].astype(f32)


def put_payload(payload, j, state, totals):
    payload[j, 0:STATE, :] = state.astype(bf16)
    factor = spread(totals, j)
    high = factor.astype(bf16).astype(f32)
    rest = factor - high
    row = lax.broadcasted_iota(jnp.int32, (16, T), 0)
    extra = jnp.where(row == 0, high, jnp.where(row == 1, rest, 0.0))
    payload[j, STATE:PAY, :] = extra.astype(bf16)


def shuffle():
    source = lax.broadcasted_iota(jnp.int32, (256, 256), 0)
    target = lax.broadcasted_iota(jnp.int32, (256, 256), 1)
    k, i, r = source >> 5, (source >> 4) & 1, source & 15
    return jnp.where(target == i * T + k * 16 + r, 1.0, 0.0).astype(bf16)


def front_kernel(xbc, halo, taps, heads, xs, bc, delta, cum, payload, padded):
    load_padded(padded, xbc, halo)
    lane = lax.broadcasted_iota(jnp.int32, (1, T), 1)
    raw = xbc[:, DT : DT + T].astype(f32) + heads[0:1, :]
    soft = jnp.maximum(raw, 0.0) + jnp.log1p(jnp.exp(-jnp.abs(raw)))
    steps = jnp.where(lane < HEADS, soft, 0.0)
    delta[...] = steps
    logs = steps * -jnp.exp(heads[1:2, :])
    sums = dot(lower_triangle().astype(f32), logs, highest)
    cum[...] = sums
    last = sums[T - 1 : T, :]
    weight = jnp.exp(last - sums) * steps
    totals = jnp.exp(last)
    b_pre = conv_block(padded, taps, PAIRS)
    c_pre = conv_block(padded, taps, PAIRS + 1)
    keys = b_pre * sigmoid(b_pre)
    bc[:, 0:STATE] = keys.astype(bf16)
    bc[:, STATE:] = (c_pre * sigmoid(c_pre)).astype(bf16)
    keys_t = keys.T.astype(bf16)
    for j in range(PAIRS):
        pre = conv_block(padded, taps, j)
        x = pre * sigmoid(pre)
        xs[:, block(j)] = x
        put_payload(payload, j, dot(keys_t, (spread(weight, j) * x).astype(bf16)), totals)


def scan_kernel(backward, payload, entering):
    carried = jnp.zeros((STATE, T), f32)
    order = range(PAIRS - 1, -1, -1) if backward else range(PAIRS)
    for k in order:
        entering[k] = carried.astype(bf16)
        extra = payload[k, STATE:PAY, :].astype(f32)
        factor = extra[0:1, :] + extra[1:2, :]
        carried = factor * carried + payload[k, 0:STATE, :].astype(f32)


def decay(cum, cum_t, h, causal):
    return jnp.where(causal, jnp.exp(cum[:, h : h + 1] - cum_t[h : h + 1, :]), 0.0)


def halves(v):
    return jnp.concatenate(
        [jnp.where(low_half(), v, 0.0), jnp.where(low_half(), 0.0, v)], axis=0
    ).astype(bf16)


def within_kernel(xs, bc, delta, cum, heads, local):
    causal = lower_triangle()
    cums = cum[...]
    cum_t = cums.T
    steps = delta[...]
    skips = heads[2:3, :]
    scores = dot_nt(bc[:, STATE:], bc[:, 0:STATE])
    for j in range(PAIRS):
        x = xs[:, block(j)]
        mixing = jnp.concatenate(
            [scores * decay(cums, cum_t, 2 * j + i, causal) for i in range(2)], axis=1
        ).astype(bf16)
        local[:, block(j)] = dot(mixing, halves(spread(steps, j) * x)) + spread(skips, j) * x


def project_kernel(stream, gain, weight, hidden, projected):
    @pl.when(pl.program_id(0) == 0)
    def _():
        values = stream[...]
        inverse = lax.rsqrt(jnp.sum(values * values, axis=1, keepdims=True) / D + epsilon)
        hidden[...] = (values * inverse * gain[...]).astype(bf16)

    projected[...] = dot(hidden[...], weight[...]).astype(bf16)


def finish_kernel(
    local, bc, cum, entering, gates, gain, stream, weight_0, weight_1, mixed, normed, result, gated,
    shuffled,
):
    @pl.when(pl.program_id(0) == 0)
    def _():
        growth = jnp.exp(cum[...])
        queries = bc[:, STATE:]
        squares = jnp.zeros((T, T), f32)
        for j in range(PAIRS):
            whole = local[:, block(j)] + spread(growth, j) * dot(queries, entering[j])
            rounded = whole.astype(bf16)
            mixed[:, block(j)] = rounded
            gate = gates[:, block(j)].astype(f32)
            u = rounded.astype(f32) * (gate * sigmoid(gate))
            gated[:, block(j)] = u
            squares = squares + u * u
        scale = lax.rsqrt(jnp.sum(squares, axis=1, keepdims=True) / DIN + epsilon)
        for j in range(PAIRS):
            normed[:, block(j)] = (gated[:, block(j)] * scale * gain[0:1, block(j)]).astype(bf16)

        order = shuffle()
        for b in range(8):
            moved = dot(normed[:, b * 256 : (b + 1) * 256], order)
            shuffled[0, :, block(b)] = moved[:, 0:T]
            shuffled[1, :, block(b)] = moved[:, T:]

    result[...] = (
        stream[...]
        + dot(shuffled[0].astype(bf16), weight_0[...])
        + dot(shuffled[1].astype(bf16), weight_1[...])
    )


def top_kernel(
    upstream, weight, mixed, gates, gain, bc, cum, d_mixed, d_gate, d_gain, payload, d_shuffled,
    d_normed, gated,
):
    step = pl.program_id(0)
    d_shuffled[step] = dot_nt(upstream[...], weight[...])

    def part(j):
        return d_normed[:, block(j)]

    @pl.when(step == 1)
    def _():
        order = shuffle()
        for b in range(8):
            value = jnp.concatenate([d_shuffled[0, :, block(b)], d_shuffled[1, :, block(b)]], axis=1)
            high = value.astype(bf16)
            rest = (value - high.astype(f32)).astype(bf16)
            d_normed[:, b * 256 : (b + 1) * 256] = dot_nt(high, order) + dot_nt(rest, order)
        squares = jnp.zeros((T, T), f32)
        products = jnp.zeros((T, T), f32)
        for j in range(PAIRS):
            gate = gates[:, block(j)].astype(f32)
            u = mixed[:, block(j)].astype(f32) * (gate * sigmoid(gate))
            gated[:, block(j)] = u
            squares = squares + u * u
            products = products + part(j) * gain[0:1, block(j)] * u
        scale = lax.rsqrt(jnp.sum(squares, axis=1, keepdims=True) / DIN + epsilon)
        pull = scale * scale * scale * (jnp.sum(products, axis=1, keepdims=True) / DIN)
        cums = cum[...]
        growth = jnp.exp(cums)
        totals = growth[T - 1 : T, :]
        queries_t = bc[:, STATE:].astype(f32).T.astype(bf16)
        for j in range(PAIRS):
            gate = gates[:, block(j)].astype(f32)
            act, slope = silu_and_slope(gate)
            u = gated[:, block(j)]
            up = part(j)
            d_gain[:, block(j)] = jnp.broadcast_to(
                jnp.sum(up * u * scale, axis=0, keepdims=True), (8, T)
            )
            du = up * gain[0:1, block(j)] * scale - u * pull
            dm = (du * act).astype(bf16)
            d_mixed[:, block(j)] = dm
            d_gate[:, block(j)] = (du * mixed[:, block(j)].astype(f32) * slope).astype(bf16)
            put_payload(
                payload, j, dot(queries_t, (spread(growth, j) * dm.astype(f32)).astype(bf16)), totals
            )


def inner_kernel(xs, bc, delta, cum, d_mixed, entering, d_scaled, d_bc, d_cum, rows, columns):
    causal = lower_triangle()
    cums = cum[...]
    cum_t = cums.T
    steps = delta[...]
    growth = jnp.exp(cums)
    keys = bc[:, 0:STATE]
    queries = bc[:, STATE:]
    scores = dot_nt(queries, keys)
    rows[...] = jnp.zeros((T, T), f32)
    columns[...] = jnp.zeros((T, T), f32)
    d_scores = jnp.zeros((T, T), f32)
    d_queries = jnp.zeros((T, STATE), f32)
    for j in range(PAIRS):
        dy_low = d_mixed[:, block(j)]
        dy = dy_low.astype(f32)
        scaled = halves(spread(steps, j) * xs[:, block(j)])
        d_mixing = dot_nt(dy_low, scaled)
        grown = spread(growth, j) * dy
        across = grown * dot(queries, entering[j])
        d_queries = d_queries + dot_nt(grown.astype(bf16), entering[j])
        mixings = []
        for i in range(2):
            h = 2 * j + i
            fall = decay(cums, cum_t, h, causal)
            d_part = d_mixing[:, i * T : (i + 1) * T] * fall
            d_scores = d_scores + d_part
            mixings.append(scores * fall)
            logs = d_part * scores
            own = jnp.where(low_half(), across, 0.0) if i == 0 else jnp.where(low_half(), 0.0, across)
            rows[:, h : h + 1] = jnp.sum(logs + own, axis=1, keepdims=True)
            columns[h : h + 1, :] = jnp.sum(logs, axis=0, keepdims=True)
        d_scaled[:, block(j)] = dot_tn(
            jnp.concatenate(mixings, axis=0).astype(bf16), halves(dy)
        )
    d_low = d_scores.astype(bf16)
    d_bc[:, 0:STATE] = dot_tn(d_low, queries)
    d_bc[:, STATE:] = d_queries + dot(d_low, keys)
    d_cum[...] = rows[...] - columns[...].T


def outer_kernel(
    xbc, halo, taps, heads, xs, bc, delta, cum, d_mixed, d_scaled, d_bc, d_cum, entering,
    leaving, d_conv, d_dt, d_taps, d_heads, padded, falls, direct, rest,
):
    load_padded(padded, xbc, halo)
    lane = lax.broadcasted_iota(jnp.int32, (1, T), 1)
    cums = cum[...]
    steps = delta[...]
    last = cums[T - 1 : T, :]
    weight = jnp.exp(last - cums)
    totals = jnp.exp(last)
    skips = heads[2:3, :]
    keys = bc[:, 0:STATE]
    falls[...] = jnp.zeros((T, T), f32)
    direct[...] = jnp.zeros((T, T), f32)
    rest[...] = jnp.zeros((8, T), f32)
    low = low_half()

    def conv_back(j, grad):
        pre = conv_block(padded, taps, j)
        d_pre = grad * silu_and_slope(pre)[1]
        d_conv[:, block(j)] = d_pre
        for k in range(KW):
            d_taps[k : k + 1, block(j)] = jnp.sum(
                d_pre * padded[13 + k : 13 + k + T, block(j)], axis=0, keepdims=True
            )
        d_taps[KW : KW + 1, block(j)] = jnp.sum(d_pre, axis=0, keepdims=True)

    d_taps[KW + 1 : 8, :] = jnp.zeros((8 - KW - 1, CONV_CH), f32)
    d_keys = d_bc[:, 0:STATE]
    for j in range(PAIRS):
        x = xs[:, block(j)]
        dy = d_mixed[:, block(j)].astype(f32)
        step = spread(steps, j)
        fall = spread(weight, j)
        weighted = fall * (step * x)
        back = dot(keys, leaving[j])
        d_keys = d_keys + dot_nt(weighted.astype(bf16), leaving[j])
        ds = d_scaled[:, block(j)] + fall * back
        flow = weighted * back
        touch = ds * x
        kept = jnp.sum(leaving[j].astype(f32) * entering[j].astype(f32), axis=0, keepdims=True)
        kept = kept * spread(totals, j)
        skipped = jnp.sum(dy * x, axis=0, keepdims=True)
        for i in range(2):
            h = 2 * j + i
            pick = (lambda v: jnp.where(low, v, 0.0)) if i == 0 else (lambda v: jnp.where(low, 0.0, v))
            falls[:, h : h + 1] = jnp.sum(pick(flow), axis=1, keepdims=True)
            direct[:, h : h + 1] = jnp.sum(pick(touch), axis=1, keepdims=True)
            rest[0:1, h : h + 1] = jnp.sum(pick(kept), axis=1, keepdims=True)
            rest[1:2, h : h + 1] = jnp.sum(pick(skipped), axis=1, keepdims=True)
        conv_back(j, step * ds + spread(skips, j) * dy)
    conv_back(PAIRS, d_keys)
    conv_back(PAIRS + 1, d_bc[:, STATE:])
    flows = falls[...]
    gained = rest[0:1, :] + jnp.sum(flows, axis=0, keepdims=True)
    row = lax.broadcasted_iota(jnp.int32, (T, T), 0)
    d_sums = d_cum[...] - flows + jnp.where(row == T - 1, gained, 0.0)
    upper = lower_triangle().astype(f32).T
    d_logs = dot(upper, d_sums, highest)
    rate = -jnp.exp(heads[1:2, :])
    d_delta = direct[...] + d_logs * rate
    slope = sigmoid(xbc[:, DT : DT + T].astype(f32) + heads[0:1, :])
    grad = jnp.where(lane < HEADS, d_delta * slope, 0.0)
    d_dt[...] = grad
    d_heads[...] = jnp.zeros((8, T), f32)
    d_heads[0:1, :] = jnp.sum(grad, axis=0, keepdims=True)
    d_heads[1:2, :] = jnp.sum(d_logs * steps, axis=0, keepdims=True) * rate
    d_heads[2:3, :] = rest[1:2, :]


def bottom_kernel(
    d_conv, halo, taps, d_gate, d_dt, weight, stream, norm, upstream, d_projected, result, d_norm,
    padded, total,
):
    step = pl.program_id(0)

    @pl.when(step == 0)
    def _():
        padded[0:T, :] = d_conv[...]
        padded[T : T + 8, :] = halo[...]
        d_projected[:, 0:DIN] = d_gate[...]
        for j in range(CONV_CH // T):
            value = taps[KW - 1 : KW, block(j)] * padded[0:T, block(j)]
            for k in range(KW - 1):
                shift = KW - 1 - k
                value = value + taps[k : k + 1, block(j)] * padded[shift : shift + T, block(j)]
            d_projected[:, DIN + j * T : DIN + (j + 1) * T] = value.astype(bf16)
        d_projected[:, DT_COL:EINP] = d_dt[...].astype(bf16)
        d_projected[:, EINP:WIDE] = jnp.zeros((T, T), bf16)
        total[...] = jnp.zeros((T, D), f32)

    columns = pl.ds(pl.multiple_of(step * TILE, T), TILE)
    total[...] += dot_nt(d_projected[:, columns], weight[...])

    @pl.when(step == WIDE // TILE - 1)
    def _():
        values = stream[...]
        d_hidden = total[...]
        inverse = lax.rsqrt(jnp.sum(values * values, axis=1, keepdims=True) / D + epsilon)
        d_norm[...] = jnp.broadcast_to(
            jnp.sum(d_hidden * values * inverse, axis=0, keepdims=True), (8, D)
        )
        scaled = d_hidden * norm[...]
        mean = jnp.sum(scaled * values, axis=1, keepdims=True) / D
        pull = inverse * inverse * inverse * mean
        result[...] = upstream[...] + scaled * inverse - values * pull


def dropping(kernel, count, extra):
    return lambda *refs: kernel(*refs[:count], *refs[count + extra :])


def call(kernel, outs, scratch, name, micros, *args, after=()):
    return pl.pallas_call(
        dropping(kernel, len(args), len(after)),
        out_shape=[jax.ShapeDtypeStruct(shape, dtype) for shape, dtype in outs],
        scratch_shapes=[pltpu.VMEM(shape, f32) for shape in scratch],
        compiler_params=pltpu.CompilerParams(vmem_limit_bytes=40 * 2**20),
        in_specs=[pl.BlockSpec(memory_space=pltpu.VMEM)] * len(args)
        + [pl.BlockSpec(memory_space=pl.ANY)] * len(after),
        cost_estimate=cost(micros),
        name=name,
    )(*args, *after)


def cost(micros):
    return pl.CostEstimate(flops=0, transcendentals=0, bytes_accessed=int(micros * 3.5e6))


def whole(array):
    rank = len(array.shape)
    return pl.BlockSpec(array.shape, lambda n: (0,) * rank)


def call_tiled(kernel, steps, args, specs, outs, scratch, name, micros, after=()):
    shapes = [jax.ShapeDtypeStruct(shape, dtype) for shape, dtype, _ in outs]
    return pl.pallas_call(
        dropping(kernel, len(args), len(after)),
        grid=(steps,),
        in_specs=[whole(v) if spec is None else spec for v, spec in zip(args, specs)]
        + [pl.BlockSpec(memory_space=pl.ANY) for _ in after],
        out_specs=[whole(v) if o[2] is None else o[2] for v, o in zip(shapes, outs)],
        out_shape=shapes,
        scratch_shapes=[pltpu.VMEM(shape, f32) for shape in scratch],
        compiler_params=pltpu.CompilerParams(vmem_limit_bytes=44 * 2**20),
        cost_estimate=cost(micros),
        name=name,
    )(*args, *after)


def swap(value):
    return lax.ppermute(value, "section", [(0, 1), (1, 0)])


def to_owners(value):
    came = lax.all_to_all(value, "seq", split_axis=0, concat_axis=0, tiled=True)
    return jnp.sum(came.astype(f32), axis=0)


def to_layers(value):
    me = lax.axis_index("dp")

    def piece(steps):
        return lax.dynamic_index_in_dim(value, (me + steps) % 4, 0, keepdims=False)

    total = piece(0).astype(f32)
    for steps in (1, -1, 2):
        moved = lax.ppermute(piece(steps), "dp", [(i, (i + steps) % 4) for i in range(4)])
        total = total + moved.astype(f32)
    return total


def to_layers_in_order(value):
    me = lax.axis_index("dp")
    came = [lax.dynamic_index_in_dim(value, me, 0, keepdims=False)]
    for steps in (1, 2, 3):
        part = lax.dynamic_index_in_dim(value, (me + steps) % 4, 0, keepdims=False)
        came.append(lax.ppermute(part, "dp", [(i, (i + steps) % 4) for i in range(4)]))
    came = jnp.stack(came)
    total = lax.dynamic_index_in_dim(came, me, 0, keepdims=False)
    for source in (1, 2, 3):
        total = total + lax.dynamic_index_in_dim(came, (me - source) % 4, 0, keepdims=False)
    return total


def in_chip(grad, rows):
    columns = grad.shape[1]
    shaped = grad.reshape(64, 2, rows // 2, columns)
    section = lax.axis_index("section")
    mine = lax.dynamic_index_in_dim(shaped, section, 1, keepdims=False)
    theirs = lax.dynamic_index_in_dim(shaped, 1 - section, 1, keepdims=False)
    total = (mine.astype(f32) + swap(theirs).astype(f32)).astype(bf16)
    return total.reshape(4, 16, rows // 2, columns)


def own_layer(halves_of, first):
    keep = jnp.where(first, halves_of[0], halves_of[1])
    give = jnp.where(first, halves_of[1], halves_of[0])
    came = swap(give.astype(f32))
    keep = keep.astype(f32)
    return jnp.where(
        first, jnp.concatenate([keep, came], axis=0), jnp.concatenate([came, keep], axis=0)
    )


def exchange(payload, backward):
    moved = lax.all_to_all(payload, "seq", split_axis=0, concat_axis=0, tiled=True)
    (entering,) = call(
        lambda *refs: scan_kernel(backward, *refs),
        [((PAIRS, STATE, T), bf16)],
        [],
        "scan_back" if backward else "scan",
        2,
        moved,
    )
    return lax.all_to_all(entering, "seq", split_axis=0, concat_axis=0, tiled=True)


def forward_layer(stream, w):
    l = w["layer"]
    columns = DIN if w["xbc"] is not None else WIDE
    hidden, projected = call_tiled(
        project_kernel,
        columns // TILE,
        (stream, w["norm"], w["all"]),
        (None, None, pl.BlockSpec((D, TILE), lambda n: (l, 4 + n))),
        [((T, D), bf16, None), ((T, columns), bf16, pl.BlockSpec((T, TILE), lambda n: (0, n)))],
        [],
        "project",
        4,
    )
    gates = projected[:, :DIN]
    xbc = projected[:, DIN:] if w["xbc"] is None else w["xbc"]
    halo = lax.ppermute(xbc[T - 16 :, :DT], "seq", [(i, i + 1) for i in range(15)])
    xs, bc, delta, cum, payload = call(
        front_kernel,
        [((T, DIN), f32), ((T, 2 * STATE), bf16), ((T, T), f32), ((T, T), f32), ((PAIRS, PAY, T), bf16)],
        [(T + 16, CONV_CH)],
        "front",
        2,
        xbc,
        halo,
        w["taps"],
        w["heads"],
    )
    entering = exchange(payload, False)
    (local,) = call(within_kernel, [((T, DIN), f32)], [], "within", 2, xs, bc, delta, cum, w["heads"])
    narrow = pl.BlockSpec((T, 512), lambda n: (0, n))
    mixed, normed, result = call_tiled(
        finish_kernel,
        2,
        (local, bc, cum, entering, gates, w["gnorm"], stream, w["all"], w["all"]),
        (None,) * 6
        + (narrow, pl.BlockSpec((D, 512), lambda n: (l, n)), pl.BlockSpec((D, 512), lambda n: (l, 2 + n))),
        [((T, DIN), bf16, None), ((T, DIN), bf16, None), ((T, D), f32, narrow)],
        [(T, DIN), (2, T, D)],
        "finish",
        5,
    )
    return (stream, hidden, gates, xbc, halo, xs, bc, delta, cum, entering, mixed, normed), result


def backward_layer(kept, upstream, w, earlier=None, outputs=()):
    stream, hidden, gates, xbc, halo, xs, bc, delta, cum, entering, mixed, normed = kept
    upstream_low = upstream.astype(bf16)
    l = w["layer"]
    d_mixed, d_gate, d_gain, payload = call_tiled(
        top_kernel,
        2,
        (upstream_low, w["all"], mixed, gates, w["gnorm"], bc, cum),
        (None, pl.BlockSpec((D, D), lambda n: (l, n))) + (None,) * 5,
        [
            ((T, DIN), bf16, None),
            ((T, DIN), bf16, None),
            ((8, DIN), f32, None),
            ((PAIRS, PAY, T), bf16, None),
        ],
        [(2, T, D), (T, DIN), (T, DIN)],
        "top",
        5,
    )
    grad_out = dot_tn(normed, upstream_low).astype(bf16)
    leaving = exchange(payload, True)
    out_total = in_chip(grad_out, 32)
    grad_out = to_layers(out_total).astype(bf16)
    ordered = (grad_out,)
    if earlier is not None:
        leaving, earlier = lax.optimization_barrier((leaving, earlier))
        ordered = (grad_out, earlier)
    d_scaled, d_bc, d_cum = call(
        inner_kernel,
        [((T, DIN), f32), ((T, 2 * STATE), f32), ((T, T), f32)],
        [(T, T), (T, T)],
        "inner",
        8,
        xs,
        bc,
        delta,
        cum,
        d_mixed,
        entering,
    )
    d_conv, d_dt, d_taps, d_heads = call(
        outer_kernel,
        [((T, CONV_CH), f32), ((T, T), f32), ((8, CONV_CH), f32), ((8, T), f32)],
        [(T + 16, CONV_CH), (T, T), (T, T), (8, T)],
        "outer",
        5,
        xbc,
        halo,
        w["taps"],
        w["heads"],
        xs,
        bc,
        delta,
        cum,
        d_mixed,
        d_scaled,
        d_bc,
        d_cum,
        entering,
        leaving,
        after=(out_total, *outputs),
    )
    halo_back = lax.ppermute(d_conv[0:8], "seq", [(i + 1, i) for i in range(15)])
    d_projected, result, d_norm = call_tiled(
        bottom_kernel,
        WIDE // TILE,
        (d_conv, halo_back, w["taps"], d_gate, d_dt, w["all"], stream, w["norm"], upstream),
        (None,) * 5 + (pl.BlockSpec((D, TILE), lambda n: (l, 4 + n)),) + (None,) * 3,
        [((T, WIDE), bf16, None), ((T, D), f32, None), ((8, D), f32, None)],
        [(T + 8, CONV_CH), (T, D)],
        "bottom",
        6,
        ordered,
    )
    grad_in = dot_tn(hidden, d_projected[:, :EINP]).astype(bf16)
    small = pack_small(d_norm[0], d_taps, d_gain[0], d_heads)
    return result, grad_in, grad_out, small, earlier


def pack_small(grad_norm, d_taps, d_gain, d_heads):
    def padded(v):
        return jnp.pad(v, ((0, 0), (0, T - v.shape[1])))

    rows = [padded(d_taps[k].reshape(64, 36)) for k in range(KW + 1)]
    rows.append(padded(grad_norm.reshape(64, 16)))
    rows.append(padded(d_gain.reshape(64, 32)))
    heads = d_heads[0:3, 0:HEADS].reshape(1, 3 * HEADS)
    rows.append(jnp.broadcast_to(padded(heads), (64, T)))
    return jnp.stack(rows, axis=1)


def turned(value, axis, steps):
    if axis == "z":
        return lax.ppermute(value, "dp", [(i, (i + steps) % 4) for i in range(4)])
    pairs = []
    for i in range(16):
        x, y = divmod(i, 4)
        if axis == "x":
            pairs.append((i, (x + steps) % 4 * 4 + y))
        else:
            pairs.append((i, x * 4 + (y + steps) % 4))
    return lax.ppermute(value, "seq", pairs)


def gathered_along(value, axis):
    seq = lax.axis_index("seq")
    me = {"z": lax.axis_index("dp"), "x": seq // 4, "y": seq % 4}[axis]
    out = jnp.zeros((4,) + value.shape, value.dtype)
    came = [value] + [turned(value, axis, steps) for steps in (1, 2, 3)]
    for steps, part in enumerate(came):
        start = ((me - steps) % 4,) + (0,) * value.ndim
        out = lax.dynamic_update_slice(out, part[None], start)
    return out


def normalised(stream):
    return stream * lax.rsqrt(jnp.mean(stream * stream, axis=-1, keepdims=True) + epsilon)


def first_projection(stream, shard, first):
    came = lax.ppermute(shard[8:16], "section", [(0, 1)])
    half = jnp.where(first, shard[0:8], came)
    for axis in ("y", "x"):
        half = gathered_along(half, axis)
    parts = normalised(stream).reshape(T, 64, 2, 8)
    parts = parts[:, :, 0, :].reshape(T, 512), parts[:, :, 1, :].reshape(T, 512)
    half, parts = lax.optimization_barrier((half, parts))
    half = gathered_along(half, "z")
    half = half.reshape(512, XBC)
    other = swap(half)
    small = jnp.where(first, half[:, XBC - T :], other[:, XBC - T :]).reshape(64, 8, T)
    gain = small[:, 5, :16].astype(f32)
    gains = gain[:, :8].reshape(1, 512), gain[:, 8:].reshape(1, 512)
    low, high = [(part * g).astype(bf16) for part, g in zip(parts, gains)]
    xbc = dot(jnp.where(first, low, high), half) + dot(jnp.where(first, high, low), other)
    return xbc.astype(bf16), small


def gathered_weights(
    stream, norm_gain, w_in, conv_w, conv_b, dt_bias, a_log, d_skip, gnorm_gain, w_out
):
    def tail(v):
        return jnp.pad(v, ((0, 0), (0, T - v.shape[1])))

    first = lax.axis_index("section") == 0
    small = jnp.concatenate(
        [tail(conv_w[0]), tail(conv_b), tail(norm_gain), tail(gnorm_gain), jnp.zeros((9, T), bf16)],
        axis=0,
    )
    mixer_part = jnp.concatenate([jnp.pad(w_in[0, :, DIN:], ((0, 0), (0, EINP - EIN))), small], axis=1)
    payload = jnp.concatenate([w_out[0, 0:16], w_out[0, 16:32], w_in[0, :, :DIN], mixer_part], axis=1)
    everything = lax.all_gather(payload, ("section", "dp", "seq"), axis=0, tiled=True)
    xbc, small_0 = first_projection(stream, mixer_part, first)
    small_1 = everything[D:, payload.shape[1] - T :].reshape(64, 16, T)
    heads = jnp.pad(jnp.concatenate([dt_bias, a_log, d_skip], axis=0), ((0, 5), (0, T - HEADS)))
    other = swap(heads)
    layers = []
    for l, part in enumerate((small_0, small_1)):
        taps = jnp.stack([part[:, k, :36].reshape(CONV_CH) for k in range(KW + 1)]).astype(f32)
        layers.append(
            {
                "layer": l,
                "all": everything,
                "xbc": xbc if l == 0 else None,
                "taps": jnp.pad(taps, ((0, 8 - KW - 1), (0, 0))),
                "norm": part[:, 5, :16].reshape(1, 1024).astype(f32),
                "gnorm": part[:, 6, :32].reshape(1, DIN).astype(f32),
                "heads": jnp.where(first == (l == 0), heads, other),
            }
        )
    return layers


def shards(
    inputs, out_grad, norm_gain, w_in, conv_w, conv_b, dt_bias, a_log, d_skip, gnorm_gain, w_out
):
    section = lax.axis_index("section")
    first = section == 0
    stream = lax.dynamic_index_in_dim(inputs, section, 0, keepdims=False)[0].astype(f32)
    layers = gathered_weights(
        stream, norm_gain, w_in, conv_w, conv_b, dt_bias, a_log, d_skip, gnorm_gain, w_out
    )
    g = lax.dynamic_index_in_dim(out_grad, section, 0, keepdims=False)[0].astype(f32)
    kept = []
    for l in range(2):
        saved, stream = forward_layer(stream, layers[l])
        kept.append(saved)
    outputs = stream.astype(bf16)
    half = outputs.shape[1] // 2

    def by_features(value):
        low, high = value[:, :half], value[:, half:]
        came = swap(jnp.where(first, high, low).astype(bf16)).astype(value.dtype)
        keep = jnp.where(first, low, high)
        return jnp.where(first, jnp.stack([keep, came]), jnp.stack([came, keep]))[:, None]

    out_part = by_features(outputs)
    g, grad_in, out_1, small_1, _ = backward_layer(
        kept[1], g, layers[1], None, (out_part,)
    )
    in_1 = to_layers(in_chip(grad_in, 16)).astype(bf16)
    g, grad_in, out_0, small_0, in_1 = backward_layer(kept[0], g, layers[0], in_1)
    total_in = in_chip(grad_in, 16)
    total_in, in_1, out_0, out_1 = lax.optimization_barrier((total_in, in_1, out_0, out_1))
    in_1 = to_owners(in_1)
    in_1, small_0, small_1 = lax.optimization_barrier((in_1, small_0, small_1))
    smalls = (small_0, small_1)
    in_halves = (to_owners(to_layers(total_in).astype(bf16)), in_1)
    outs = to_owners(jnp.concatenate([out_0, out_1], axis=1))
    out_halves = (outs[0:16], outs[16:32])
    grad_w_in = own_layer(in_halves, first)[:, :EIN]
    grad_w_out = own_layer(out_halves, first)
    small = jnp.where(first, smalls[0], smalls[1]) + swap(jnp.where(first, smalls[1], smalls[0]))
    small = to_layers_in_order(to_owners(jnp.swapaxes(small.reshape(4, 16, 8, T), 0, 1)))

    return (
        out_part,
        by_features(g),
        small[5:6, :16],
        grad_w_in[None],
        small[None, 0:KW, :36],
        small[KW : KW + 1, :36],
        small[7:8, 0:HEADS],
        small[7:8, HEADS : 2 * HEADS],
        small[7:8, 2 * HEADS : 3 * HEADS],
        small[6:7, :32],
        grad_w_out[None],
    )


def solution(mesh):
    in_specs = (
        P(None, "dp", "seq", None),
        P(None, "dp", "seq", None),
        P("section", both),
        P("section", both, None),
        P("section", None, both),
        P("section", both),
        P("section", None),
        P("section", None),
        P("section", None),
        P("section", both),
        P("section", both, None),
    )
    out_specs = (
        P(None, "dp", "seq", "section"),
        P(None, "dp", "seq", "section"),
        P("section", both),
        P("section", both, None),
        P("section", None, both),
        P("section", both),
        P("section", None),
        P("section", None),
        P("section", None),
        P("section", both),
        P("section", both, None),
    )
    return jax.shard_map(shards, mesh=mesh, in_specs=in_specs, out_specs=out_specs, check_vma=False)
```

```python
import jax
import jax.numpy as jnp
from jax import lax
from jax.experimental import pallas as pl
from jax.experimental.pallas import tpu as pltpu
from jax.sharding import PartitionSpec as P

DIN = 2048
HEADS = 32
STATE = 128
KW = 4
EIN = 4384
EINP = 4480
CONV_CH = 2304
DT_COL = 2 * DIN + 2 * STATE
T = 128
D = 1024
TILE = 512
XBC = 2560
DT = 2304
WIDE = DIN + XBC
PAIRS = 16
PAY = STATE + 16

f32 = jnp.float32
bf16 = jnp.bfloat16
epsilon = 1e-05
highest = lax.Precision.HIGHEST
both = ("dp", "seq")


def dot(a, b, precision=None):
    return jnp.dot(a, b, preferred_element_type=f32, precision=precision)


def dot_nt(a, b):
    return lax.dot_general(a, b, (((1,), (1,)), ((), ())), preferred_element_type=f32)


def dot_tn(a, b):
    return lax.dot_general(a, b, (((0,), (0,)), ((), ())), preferred_element_type=f32)


def low_half():
    return lax.broadcasted_iota(jnp.int32, (1, T), 1) < 64


def lower_triangle():
    rows = lax.broadcasted_iota(jnp.int32, (T, T), 0)
    columns = lax.broadcasted_iota(jnp.int32, (T, T), 1)
    return rows >= columns


def sigmoid(v):
    return 1.0 / (1.0 + jnp.exp(-v))


def silu_and_slope(v):
    s = sigmoid(v)
    return v * s, s * (1.0 + v * (1.0 - s))


def spread(table, j):
    return jnp.where(low_half(), table[:, 2 * j : 2 * j + 1], table[:, 2 * j + 1 : 2 * j + 2])


def block(j):
    return slice(j * T, (j + 1) * T)


def conv_block(padded, taps, j):
    total = taps[KW : KW + 1, block(j)] + taps[0:1, block(j)] * padded[13 : 13 + T, block(j)]
    for k in range(1, KW):
        total = total + taps[k : k + 1, block(j)] * padded[13 + k : 13 + k + T, block(j)]
    return total


def load_padded(padded, xbc, halo):
    padded[0:16, :] = halo[...].astype(f32)
    padded[16 : 16 + T, :] = xbc[:, 0:DT].astype(f32)


def put_payload(payload, j, state, totals):
    payload[j, 0:STATE, :] = state.astype(bf16)
    factor = spread(totals, j)
    high = factor.astype(bf16).astype(f32)
    rest = factor - high
    row = lax.broadcasted_iota(jnp.int32, (16, T), 0)
    extra = jnp.where(row == 0, high, jnp.where(row == 1, rest, 0.0))
    payload[j, STATE:PAY, :] = extra.astype(bf16)


def shuffle():
    source = lax.broadcasted_iota(jnp.int32, (256, 256), 0)
    target = lax.broadcasted_iota(jnp.int32, (256, 256), 1)
    k, i, r = source >> 5, (source >> 4) & 1, source & 15
    return jnp.where(target == i * T + k * 16 + r, 1.0, 0.0).astype(bf16)


def front_kernel(xbc, halo, taps, heads, xs, bc, delta, cum, payload, padded):
    load_padded(padded, xbc, halo)
    lane = lax.broadcasted_iota(jnp.int32, (1, T), 1)
    raw = xbc[:, DT : DT + T].astype(f32) + heads[0:1, :]
    soft = jnp.maximum(raw, 0.0) + jnp.log1p(jnp.exp(-jnp.abs(raw)))
    steps = jnp.where(lane < HEADS, soft, 0.0)
    delta[...] = steps
    logs = steps * -jnp.exp(heads[1:2, :])
    sums = dot(lower_triangle().astype(f32), logs, highest)
    cum[...] = sums
    last = sums[T - 1 : T, :]
    weight = jnp.exp(last - sums) * steps
    totals = jnp.exp(last)
    b_pre = conv_block(padded, taps, PAIRS)
    c_pre = conv_block(padded, taps, PAIRS + 1)
    keys = b_pre * sigmoid(b_pre)
    bc[:, 0:STATE] = keys.astype(bf16)
    bc[:, STATE:] = (c_pre * sigmoid(c_pre)).astype(bf16)
    keys_t = keys.T.astype(bf16)
    for j in range(PAIRS):
        pre = conv_block(padded, taps, j)
        x = pre * sigmoid(pre)
        xs[:, block(j)] = x
        put_payload(payload, j, dot(keys_t, (spread(weight, j) * x).astype(bf16)), totals)


def scan_kernel(backward, payload, entering):
    carried = jnp.zeros((STATE, T), f32)
    order = range(PAIRS - 1, -1, -1) if backward else range(PAIRS)
    for k in order:
        entering[k] = carried.astype(bf16)
        extra = payload[k, STATE:PAY, :].astype(f32)
        factor = extra[0:1, :] + extra[1:2, :]
        carried = factor * carried + payload[k, 0:STATE, :].astype(f32)


def decay(cum, cum_t, h, causal):
    return jnp.where(causal, jnp.exp(cum[:, h : h + 1] - cum_t[h : h + 1, :]), 0.0)


def halves(v):
    return jnp.concatenate(
        [jnp.where(low_half(), v, 0.0), jnp.where(low_half(), 0.0, v)], axis=0
    ).astype(bf16)


def within_kernel(xs, bc, delta, cum, heads, local):
    causal = lower_triangle()
    cums = cum[...]
    cum_t = cums.T
    steps = delta[...]
    skips = heads[2:3, :]
    scores = dot_nt(bc[:, STATE:], bc[:, 0:STATE])
    for j in range(PAIRS):
        x = xs[:, block(j)]
        mixing = jnp.concatenate(
            [scores * decay(cums, cum_t, 2 * j + i, causal) for i in range(2)], axis=1
        ).astype(bf16)
        local[:, block(j)] = dot(mixing, halves(spread(steps, j) * x)) + spread(skips, j) * x


def project_kernel(stream, gain, weight, hidden, projected):
    @pl.when(pl.program_id(0) == 0)
    def _():
        values = stream[...]
        inverse = lax.rsqrt(jnp.sum(values * values, axis=1, keepdims=True) / D + epsilon)
        hidden[...] = (values * inverse * gain[...]).astype(bf16)

    projected[...] = dot(hidden[...], weight[...]).astype(bf16)


def finish_kernel(
    local, bc, cum, entering, gates, gain, stream, weight_0, weight_1, mixed, normed, result, gated,
    shuffled,
):
    @pl.when(pl.program_id(0) == 0)
    def _():
        growth = jnp.exp(cum[...])
        queries = bc[:, STATE:]
        squares = jnp.zeros((T, T), f32)
        for j in range(PAIRS):
            whole = local[:, block(j)] + spread(growth, j) * dot(queries, entering[j])
            rounded = whole.astype(bf16)
            mixed[:, block(j)] = rounded
            gate = gates[:, block(j)].astype(f32)
            u = rounded.astype(f32) * (gate * sigmoid(gate))
            gated[:, block(j)] = u
            squares = squares + u * u
        scale = lax.rsqrt(jnp.sum(squares, axis=1, keepdims=True) / DIN + epsilon)
        for j in range(PAIRS):
            normed[:, block(j)] = (gated[:, block(j)] * scale * gain[0:1, block(j)]).astype(bf16)

        order = shuffle()
        for b in range(8):
            moved = dot(normed[:, b * 256 : (b + 1) * 256], order)
            shuffled[0, :, block(b)] = moved[:, 0:T]
            shuffled[1, :, block(b)] = moved[:, T:]

    result[...] = (
        stream[...]
        + dot(shuffled[0].astype(bf16), weight_0[...])
        + dot(shuffled[1].astype(bf16), weight_1[...])
    )


def top_kernel(
    upstream, weight, mixed, gates, gain, bc, cum, d_mixed, d_gate, d_gain, payload, d_shuffled,
    d_normed, gated,
):
    step = pl.program_id(0)
    d_shuffled[step] = dot_nt(upstream[...], weight[...])

    def part(j):
        return d_normed[:, block(j)]

    @pl.when(step == 1)
    def _():
        order = shuffle()
        for b in range(8):
            value = jnp.concatenate([d_shuffled[0, :, block(b)], d_shuffled[1, :, block(b)]], axis=1)
            high = value.astype(bf16)
            rest = (value - high.astype(f32)).astype(bf16)
            d_normed[:, b * 256 : (b + 1) * 256] = dot_nt(high, order) + dot_nt(rest, order)
        squares = jnp.zeros((T, T), f32)
        products = jnp.zeros((T, T), f32)
        for j in range(PAIRS):
            gate = gates[:, block(j)].astype(f32)
            u = mixed[:, block(j)].astype(f32) * (gate * sigmoid(gate))
            gated[:, block(j)] = u
            squares = squares + u * u
            products = products + part(j) * gain[0:1, block(j)] * u
        scale = lax.rsqrt(jnp.sum(squares, axis=1, keepdims=True) / DIN + epsilon)
        pull = scale * scale * scale * (jnp.sum(products, axis=1, keepdims=True) / DIN)
        cums = cum[...]
        growth = jnp.exp(cums)
        totals = growth[T - 1 : T, :]
        queries_t = bc[:, STATE:].astype(f32).T.astype(bf16)
        for j in range(PAIRS):
            gate = gates[:, block(j)].astype(f32)
            act, slope = silu_and_slope(gate)
            u = gated[:, block(j)]
            up = part(j)
            d_gain[:, block(j)] = jnp.broadcast_to(
                jnp.sum(up * u * scale, axis=0, keepdims=True), (8, T)
            )
            du = up * gain[0:1, block(j)] * scale - u * pull
            dm = (du * act).astype(bf16)
            d_mixed[:, block(j)] = dm
            d_gate[:, block(j)] = (du * mixed[:, block(j)].astype(f32) * slope).astype(bf16)
            put_payload(
                payload, j, dot(queries_t, (spread(growth, j) * dm.astype(f32)).astype(bf16)), totals
            )


def inner_kernel(xs, bc, delta, cum, d_mixed, entering, d_scaled, d_bc, d_cum, rows, columns):
    causal = lower_triangle()
    cums = cum[...]
    cum_t = cums.T
    steps = delta[...]
    growth = jnp.exp(cums)
    keys = bc[:, 0:STATE]
    queries = bc[:, STATE:]
    scores = dot_nt(queries, keys)
    rows[...] = jnp.zeros((T, T), f32)
    columns[...] = jnp.zeros((T, T), f32)
    d_scores = jnp.zeros((T, T), f32)
    d_queries = jnp.zeros((T, STATE), f32)
    for j in range(PAIRS):
        dy_low = d_mixed[:, block(j)]
        dy = dy_low.astype(f32)
        scaled = halves(spread(steps, j) * xs[:, block(j)])
        d_mixing = dot_nt(dy_low, scaled)
        grown = spread(growth, j) * dy
        across = grown * dot(queries, entering[j])
        d_queries = d_queries + dot_nt(grown.astype(bf16), entering[j])
        mixings = []
        for i in range(2):
            h = 2 * j + i
            fall = decay(cums, cum_t, h, causal)
            d_part = d_mixing[:, i * T : (i + 1) * T] * fall
            d_scores = d_scores + d_part
            mixings.append(scores * fall)
            logs = d_part * scores
            own = jnp.where(low_half(), across, 0.0) if i == 0 else jnp.where(low_half(), 0.0, across)
            rows[:, h : h + 1] = jnp.sum(logs + own, axis=1, keepdims=True)
            columns[h : h + 1, :] = jnp.sum(logs, axis=0, keepdims=True)
        d_scaled[:, block(j)] = dot_tn(
            jnp.concatenate(mixings, axis=0).astype(bf16), halves(dy)
        )
    d_low = d_scores.astype(bf16)
    d_bc[:, 0:STATE] = dot_tn(d_low, queries)
    d_bc[:, STATE:] = d_queries + dot(d_low, keys)
    d_cum[...] = rows[...] - columns[...].T


def outer_kernel(
    xbc, halo, taps, heads, xs, bc, delta, cum, d_mixed, d_scaled, d_bc, d_cum, entering,
    leaving, d_conv, d_dt, d_taps, d_heads, padded, falls, direct, rest,
):
    load_padded(padded, xbc, halo)
    lane = lax.broadcasted_iota(jnp.int32, (1, T), 1)
    cums = cum[...]
    steps = delta[...]
    last = cums[T - 1 : T, :]
    weight = jnp.exp(last - cums)
    totals = jnp.exp(last)
    skips = heads[2:3, :]
    keys = bc[:, 0:STATE]
    falls[...] = jnp.zeros((T, T), f32)
    direct[...] = jnp.zeros((T, T), f32)
    rest[...] = jnp.zeros((8, T), f32)
    low = low_half()

    def conv_back(j, grad):
        pre = conv_block(padded, taps, j)
        d_pre = grad * silu_and_slope(pre)[1]
        d_conv[:, block(j)] = d_pre
        for k in range(KW):
            d_taps[k : k + 1, block(j)] = jnp.sum(
                d_pre * padded[13 + k : 13 + k + T, block(j)], axis=0, keepdims=True
            )
        d_taps[KW : KW + 1, block(j)] = jnp.sum(d_pre, axis=0, keepdims=True)

    d_taps[KW + 1 : 8, :] = jnp.zeros((8 - KW - 1, CONV_CH), f32)
    d_keys = d_bc[:, 0:STATE]
    for j in range(PAIRS):
        x = xs[:, block(j)]
        dy = d_mixed[:, block(j)].astype(f32)
        step = spread(steps, j)
        fall = spread(weight, j)
        weighted = fall * (step * x)
        back = dot(keys, leaving[j])
        d_keys = d_keys + dot_nt(weighted.astype(bf16), leaving[j])
        ds = d_scaled[:, block(j)] + fall * back
        flow = weighted * back
        touch = ds * x
        kept = jnp.sum(leaving[j].astype(f32) * entering[j].astype(f32), axis=0, keepdims=True)
        kept = kept * spread(totals, j)
        skipped = jnp.sum(dy * x, axis=0, keepdims=True)
        for i in range(2):
            h = 2 * j + i
            pick = (lambda v: jnp.where(low, v, 0.0)) if i == 0 else (lambda v: jnp.where(low, 0.0, v))
            falls[:, h : h + 1] = jnp.sum(pick(flow), axis=1, keepdims=True)
            direct[:, h : h + 1] = jnp.sum(pick(touch), axis=1, keepdims=True)
            rest[0:1, h : h + 1] = jnp.sum(pick(kept), axis=1, keepdims=True)
            rest[1:2, h : h + 1] = jnp.sum(pick(skipped), axis=1, keepdims=True)
        conv_back(j, step * ds + spread(skips, j) * dy)
    conv_back(PAIRS, d_keys)
    conv_back(PAIRS + 1, d_bc[:, STATE:])
    flows = falls[...]
    gained = rest[0:1, :] + jnp.sum(flows, axis=0, keepdims=True)
    row = lax.broadcasted_iota(jnp.int32, (T, T), 0)
    d_sums = d_cum[...] - flows + jnp.where(row == T - 1, gained, 0.0)
    upper = lower_triangle().astype(f32).T
    d_logs = dot(upper, d_sums, highest)
    rate = -jnp.exp(heads[1:2, :])
    d_delta = direct[...] + d_logs * rate
    slope = sigmoid(xbc[:, DT : DT + T].astype(f32) + heads[0:1, :])
    grad = jnp.where(lane < HEADS, d_delta * slope, 0.0)
    d_dt[...] = grad
    d_heads[...] = jnp.zeros((8, T), f32)
    d_heads[0:1, :] = jnp.sum(grad, axis=0, keepdims=True)
    d_heads[1:2, :] = jnp.sum(d_logs * steps, axis=0, keepdims=True) * rate
    d_heads[2:3, :] = rest[1:2, :]


def bottom_kernel(
    d_conv, halo, taps, d_gate, d_dt, weight, stream, norm, upstream, d_projected, result, d_norm,
    padded, total,
):
    step = pl.program_id(0)

    @pl.when(step == 0)
    def _():
        padded[0:T, :] = d_conv[...]
        padded[T : T + 8, :] = halo[...]
        d_projected[:, 0:DIN] = d_gate[...]
        for j in range(CONV_CH // T):
            value = taps[KW - 1 : KW, block(j)] * padded[0:T, block(j)]
            for k in range(KW - 1):
                shift = KW - 1 - k
                value = value + taps[k : k + 1, block(j)] * padded[shift : shift + T, block(j)]
            d_projected[:, DIN + j * T : DIN + (j + 1) * T] = value.astype(bf16)
        d_projected[:, DT_COL:EINP] = d_dt[...].astype(bf16)
        d_projected[:, EINP:WIDE] = jnp.zeros((T, T), bf16)
        total[...] = jnp.zeros((T, D), f32)

    columns = pl.ds(pl.multiple_of(step * TILE, T), TILE)
    total[...] += dot_nt(d_projected[:, columns], weight[...])

    @pl.when(step == WIDE // TILE - 1)
    def _():
        values = stream[...]
        d_hidden = total[...]
        inverse = lax.rsqrt(jnp.sum(values * values, axis=1, keepdims=True) / D + epsilon)
        d_norm[...] = jnp.broadcast_to(
            jnp.sum(d_hidden * values * inverse, axis=0, keepdims=True), (8, D)
        )
        scaled = d_hidden * norm[...]
        mean = jnp.sum(scaled * values, axis=1, keepdims=True) / D
        pull = inverse * inverse * inverse * mean
        result[...] = upstream[...] + scaled * inverse - values * pull


def dropping(kernel, count, extra):
    return lambda *refs: kernel(*refs[:count], *refs[count + extra :])


def call(kernel, outs, scratch, name, micros, *args, after=()):
    return pl.pallas_call(
        dropping(kernel, len(args), len(after)),
        out_shape=[jax.ShapeDtypeStruct(shape, dtype) for shape, dtype in outs],
        scratch_shapes=[pltpu.VMEM(shape, f32) for shape in scratch],
        compiler_params=pltpu.CompilerParams(vmem_limit_bytes=40 * 2**20),
        in_specs=[pl.BlockSpec(memory_space=pltpu.VMEM)] * len(args)
        + [pl.BlockSpec(memory_space=pl.ANY)] * len(after),
        cost_estimate=cost(micros),
        name=name,
    )(*args, *after)


def cost(micros):
    return pl.CostEstimate(flops=0, transcendentals=0, bytes_accessed=int(micros * 3.5e6))


def whole(array):
    rank = len(array.shape)
    return pl.BlockSpec(array.shape, lambda n: (0,) * rank)


def call_tiled(kernel, steps, args, specs, outs, scratch, name, micros, after=()):
    shapes = [jax.ShapeDtypeStruct(shape, dtype) for shape, dtype, _ in outs]
    return pl.pallas_call(
        dropping(kernel, len(args), len(after)),
        grid=(steps,),
        in_specs=[whole(v) if spec is None else spec for v, spec in zip(args, specs)]
        + [pl.BlockSpec(memory_space=pl.ANY) for _ in after],
        out_specs=[whole(v) if o[2] is None else o[2] for v, o in zip(shapes, outs)],
        out_shape=shapes,
        scratch_shapes=[pltpu.VMEM(shape, f32) for shape in scratch],
        compiler_params=pltpu.CompilerParams(vmem_limit_bytes=44 * 2**20),
        cost_estimate=cost(micros),
        name=name,
    )(*args, *after)


def swap(value):
    return lax.ppermute(value, "section", [(0, 1), (1, 0)])


def to_owners(value):
    came = lax.all_to_all(value, "seq", split_axis=0, concat_axis=0, tiled=True)
    return jnp.sum(came.astype(f32), axis=0)


def to_layers(value):
    me = lax.axis_index("dp")

    def piece(steps):
        return lax.dynamic_index_in_dim(value, (me + steps) % 4, 0, keepdims=False)

    total = piece(0).astype(f32)
    for steps in (1, -1, 2):
        moved = lax.ppermute(piece(steps), "dp", [(i, (i + steps) % 4) for i in range(4)])
        total = total + moved.astype(f32)
    return total


def to_layers_in_order(value):
    me = lax.axis_index("dp")
    came = [lax.dynamic_index_in_dim(value, me, 0, keepdims=False)]
    for steps in (1, 2, 3):
        part = lax.dynamic_index_in_dim(value, (me + steps) % 4, 0, keepdims=False)
        came.append(lax.ppermute(part, "dp", [(i, (i + steps) % 4) for i in range(4)]))
    came = jnp.stack(came)
    total = lax.dynamic_index_in_dim(came, me, 0, keepdims=False)
    for source in (1, 2, 3):
        total = total + lax.dynamic_index_in_dim(came, (me - source) % 4, 0, keepdims=False)
    return total


def in_chip(grad, rows):
    return chip_sum(*chip_parts(grad, rows))


def chip_parts(grad, rows):
    columns = grad.shape[1]
    shaped = grad.reshape(64, 2, rows // 2, columns)
    section = lax.axis_index("section")
    mine = lax.dynamic_index_in_dim(shaped, section, 1, keepdims=False)
    theirs = lax.dynamic_index_in_dim(shaped, 1 - section, 1, keepdims=False)
    return mine, swap(theirs)


def chip_sum(mine, came):
    total = (mine.astype(f32) + came.astype(f32)).astype(bf16)
    return total.reshape(4, 16, *mine.shape[1:])


def own_layer(halves_of, first):
    keep = jnp.where(first, halves_of[0], halves_of[1])
    give = jnp.where(first, halves_of[1], halves_of[0])
    came = swap(give.astype(f32))
    keep = keep.astype(f32)
    return jnp.where(
        first, jnp.concatenate([keep, came], axis=0), jnp.concatenate([came, keep], axis=0)
    )


def exchange(payload, backward):
    moved = lax.all_to_all(payload, "seq", split_axis=0, concat_axis=0, tiled=True)
    (entering,) = call(
        lambda *refs: scan_kernel(backward, *refs),
        [((PAIRS, STATE, T), bf16)],
        [],
        "scan_back" if backward else "scan",
        2,
        moved,
    )
    return lax.all_to_all(entering, "seq", split_axis=0, concat_axis=0, tiled=True)


def forward_layer(stream, w):
    l = w["layer"]
    columns = DIN if w["xbc"] is not None else WIDE
    hidden, projected = call_tiled(
        project_kernel,
        columns // TILE,
        (stream, w["norm"], w["all"]),
        (None, None, pl.BlockSpec((D, TILE), lambda n: (l, 4 + n))),
        [((T, D), bf16, None), ((T, columns), bf16, pl.BlockSpec((T, TILE), lambda n: (0, n)))],
        [],
        "project",
        4,
    )
    gates = projected[:, :DIN]
    xbc = projected[:, DIN:] if w["xbc"] is None else w["xbc"]
    halo = lax.ppermute(xbc[T - 16 :, :DT], "seq", [(i, i + 1) for i in range(15)])
    xs, bc, delta, cum, payload = call(
        front_kernel,
        [((T, DIN), f32), ((T, 2 * STATE), bf16), ((T, T), f32), ((T, T), f32), ((PAIRS, PAY, T), bf16)],
        [(T + 16, CONV_CH)],
        "front",
        2,
        xbc,
        halo,
        w["taps"],
        w["heads"],
    )
    entering = exchange(payload, False)
    (local,) = call(within_kernel, [((T, DIN), f32)], [], "within", 2, xs, bc, delta, cum, w["heads"])
    narrow = pl.BlockSpec((T, 512), lambda n: (0, n))
    mixed, normed, result = call_tiled(
        finish_kernel,
        2,
        (local, bc, cum, entering, gates, w["gnorm"], stream, w["all"], w["all"]),
        (None,) * 6
        + (narrow, pl.BlockSpec((D, 512), lambda n: (l, n)), pl.BlockSpec((D, 512), lambda n: (l, 2 + n))),
        [((T, DIN), bf16, None), ((T, DIN), bf16, None), ((T, D), f32, narrow)],
        [(T, DIN), (2, T, D)],
        "finish",
        5,
    )
    return (stream, hidden, gates, xbc, halo, xs, bc, delta, cum, entering, mixed, normed), result


def backward_layer(kept, upstream, w, earlier=None, outputs=()):
    stream, hidden, gates, xbc, halo, xs, bc, delta, cum, entering, mixed, normed = kept
    upstream_low = upstream.astype(bf16)
    l = w["layer"]
    d_mixed, d_gate, d_gain, payload = call_tiled(
        top_kernel,
        2,
        (upstream_low, w["all"], mixed, gates, w["gnorm"], bc, cum),
        (None, pl.BlockSpec((D, D), lambda n: (l, n))) + (None,) * 5,
        [
            ((T, DIN), bf16, None),
            ((T, DIN), bf16, None),
            ((8, DIN), f32, None),
            ((PAIRS, PAY, T), bf16, None),
        ],
        [(2, T, D), (T, DIN), (T, DIN)],
        "top",
        5,
    )
    grad_out = dot_tn(normed, upstream_low).astype(bf16)
    if earlier is not None:
        payload, earlier = lax.optimization_barrier((payload, earlier))
        earlier = to_layers(chip_sum(*earlier)).astype(bf16)
    leaving = exchange(payload, True)
    out_total = in_chip(grad_out, 32)
    grad_out = to_layers(out_total).astype(bf16)
    ordered = (grad_out,)
    if earlier is not None:
        leaving, earlier = lax.optimization_barrier((leaving, earlier))
        ordered = (grad_out, earlier)
    d_scaled, d_bc, d_cum = call(
        inner_kernel,
        [((T, DIN), f32), ((T, 2 * STATE), f32), ((T, T), f32)],
        [(T, T), (T, T)],
        "inner",
        8,
        xs,
        bc,
        delta,
        cum,
        d_mixed,
        entering,
    )
    d_conv, d_dt, d_taps, d_heads = call(
        outer_kernel,
        [((T, CONV_CH), f32), ((T, T), f32), ((8, CONV_CH), f32), ((8, T), f32)],
        [(T + 16, CONV_CH), (T, T), (T, T), (8, T)],
        "outer",
        5,
        xbc,
        halo,
        w["taps"],
        w["heads"],
        xs,
        bc,
        delta,
        cum,
        d_mixed,
        d_scaled,
        d_bc,
        d_cum,
        entering,
        leaving,
        after=(out_total, *outputs),
    )
    halo_back = lax.ppermute(d_conv[0:8], "seq", [(i + 1, i) for i in range(15)])
    d_projected, result, d_norm = call_tiled(
        bottom_kernel,
        WIDE // TILE,
        (d_conv, halo_back, w["taps"], d_gate, d_dt, w["all"], stream, w["norm"], upstream),
        (None,) * 5 + (pl.BlockSpec((D, TILE), lambda n: (l, 4 + n)),) + (None,) * 3,
        [((T, WIDE), bf16, None), ((T, D), f32, None), ((8, D), f32, None)],
        [(T + 8, CONV_CH), (T, D)],
        "bottom",
        6,
        ordered,
    )
    grad_in = dot_tn(hidden, d_projected[:, :EINP]).astype(bf16)
    small = pack_small(d_norm[0], d_taps, d_gain[0], d_heads)
    return result, grad_in, grad_out, small, earlier


def pack_small(grad_norm, d_taps, d_gain, d_heads):
    def padded(v):
        return jnp.pad(v, ((0, 0), (0, T - v.shape[1])))

    rows = [padded(d_taps[k].reshape(64, 36)) for k in range(KW + 1)]
    rows.append(padded(grad_norm.reshape(64, 16)))
    rows.append(padded(d_gain.reshape(64, 32)))
    heads = d_heads[0:3, 0:HEADS].reshape(1, 3 * HEADS)
    rows.append(jnp.broadcast_to(padded(heads), (64, T)))
    return jnp.stack(rows, axis=1)


def turned(value, axis, steps):
    if axis == "z":
        return lax.ppermute(value, "dp", [(i, (i + steps) % 4) for i in range(4)])
    pairs = []
    for i in range(16):
        x, y = divmod(i, 4)
        if axis == "x":
            pairs.append((i, (x + steps) % 4 * 4 + y))
        else:
            pairs.append((i, x * 4 + (y + steps) % 4))
    return lax.ppermute(value, "seq", pairs)


def gathered_along(value, axis):
    seq = lax.axis_index("seq")
    me = {"z": lax.axis_index("dp"), "x": seq // 4, "y": seq % 4}[axis]
    out = jnp.zeros((4,) + value.shape, value.dtype)
    came = [value] + [turned(value, axis, steps) for steps in (1, 2, 3)]
    for steps, part in enumerate(came):
        start = ((me - steps) % 4,) + (0,) * value.ndim
        out = lax.dynamic_update_slice(out, part[None], start)
    return out


def normalised(stream):
    return stream * lax.rsqrt(jnp.mean(stream * stream, axis=-1, keepdims=True) + epsilon)


def first_projection(stream, shard, first):
    came = lax.ppermute(shard[8:16], "section", [(0, 1)])
    half = jnp.where(first, shard[0:8], came)
    for axis in ("y", "x"):
        half = gathered_along(half, axis)
    parts = normalised(stream).reshape(T, 64, 2, 8)
    parts = parts[:, :, 0, :].reshape(T, 512), parts[:, :, 1, :].reshape(T, 512)
    half, parts = lax.optimization_barrier((half, parts))
    half = gathered_along(half, "z")
    half = half.reshape(512, XBC)
    other = swap(half)
    small = jnp.where(first, half[:, XBC - T :], other[:, XBC - T :]).reshape(64, 8, T)
    gain = small[:, 5, :16].astype(f32)
    gains = gain[:, :8].reshape(1, 512), gain[:, 8:].reshape(1, 512)
    low, high = [(part * g).astype(bf16) for part, g in zip(parts, gains)]
    xbc = dot(jnp.where(first, low, high), half) + dot(jnp.where(first, high, low), other)
    return xbc.astype(bf16), small


def gathered_weights(
    stream, norm_gain, w_in, conv_w, conv_b, dt_bias, a_log, d_skip, gnorm_gain, w_out
):
    def tail(v):
        return jnp.pad(v, ((0, 0), (0, T - v.shape[1])))

    first = lax.axis_index("section") == 0
    small = jnp.concatenate(
        [tail(conv_w[0]), tail(conv_b), tail(norm_gain), tail(gnorm_gain), jnp.zeros((9, T), bf16)],
        axis=0,
    )
    mixer_part = jnp.concatenate([jnp.pad(w_in[0, :, DIN:], ((0, 0), (0, EINP - EIN))), small], axis=1)
    payload = jnp.concatenate([w_out[0, 0:16], w_out[0, 16:32], w_in[0, :, :DIN], mixer_part], axis=1)
    everything = lax.all_gather(payload, ("section", "dp", "seq"), axis=0, tiled=True)
    xbc, small_0 = first_projection(stream, mixer_part, first)
    small_1 = everything[D:, payload.shape[1] - T :].reshape(64, 16, T)
    heads = jnp.pad(jnp.concatenate([dt_bias, a_log, d_skip], axis=0), ((0, 5), (0, T - HEADS)))
    other = swap(heads)
    layers = []
    for l, part in enumerate((small_0, small_1)):
        taps = jnp.stack([part[:, k, :36].reshape(CONV_CH) for k in range(KW + 1)]).astype(f32)
        layers.append(
            {
                "layer": l,
                "all": everything,
                "xbc": xbc if l == 0 else None,
                "taps": jnp.pad(taps, ((0, 8 - KW - 1), (0, 0))),
                "norm": part[:, 5, :16].reshape(1, 1024).astype(f32),
                "gnorm": part[:, 6, :32].reshape(1, DIN).astype(f32),
                "heads": jnp.where(first == (l == 0), heads, other),
            }
        )
    return layers


def shards(
    inputs, out_grad, norm_gain, w_in, conv_w, conv_b, dt_bias, a_log, d_skip, gnorm_gain, w_out
):
    section = lax.axis_index("section")
    first = section == 0
    stream = lax.dynamic_index_in_dim(inputs, section, 0, keepdims=False)[0].astype(f32)
    layers = gathered_weights(
        stream, norm_gain, w_in, conv_w, conv_b, dt_bias, a_log, d_skip, gnorm_gain, w_out
    )
    g = lax.dynamic_index_in_dim(out_grad, section, 0, keepdims=False)[0].astype(f32)
    kept = []
    for l in range(2):
        saved, stream = forward_layer(stream, layers[l])
        kept.append(saved)
    outputs = stream.astype(bf16)
    half = outputs.shape[1] // 2

    def by_features(value):
        low, high = value[:, :half], value[:, half:]
        came = swap(jnp.where(first, high, low).astype(bf16)).astype(value.dtype)
        keep = jnp.where(first, low, high)
        return jnp.where(first, jnp.stack([keep, came]), jnp.stack([came, keep]))[:, None]

    out_part = by_features(outputs)
    g, grad_in, out_1, small_1, _ = backward_layer(
        kept[1], g, layers[1], None, (out_part,)
    )
    in_1 = chip_parts(grad_in, 16)
    g, grad_in, out_0, small_0, in_1 = backward_layer(kept[0], g, layers[0], in_1)
    total_in = in_chip(grad_in, 16)
    total_in, in_1, out_0, out_1 = lax.optimization_barrier((total_in, in_1, out_0, out_1))
    in_1 = to_owners(in_1)
    in_1, small_0, small_1 = lax.optimization_barrier((in_1, small_0, small_1))
    smalls = (small_0, small_1)
    in_halves = (to_owners(to_layers(total_in).astype(bf16)), in_1)
    outs = to_owners(jnp.concatenate([out_0, out_1], axis=1))
    out_halves = (outs[0:16], outs[16:32])
    grad_w_in = own_layer(in_halves, first)[:, :EIN]
    grad_w_out = own_layer(out_halves, first)
    small = jnp.where(first, smalls[0], smalls[1]) + swap(jnp.where(first, smalls[1], smalls[0]))
    small = to_layers_in_order(to_owners(jnp.swapaxes(small.reshape(4, 16, 8, T), 0, 1)))

    return (
        out_part,
        by_features(g),
        small[5:6, :16],
        grad_w_in[None],
        small[None, 0:KW, :36],
        small[KW : KW + 1, :36],
        small[7:8, 0:HEADS],
        small[7:8, HEADS : 2 * HEADS],
        small[7:8, 2 * HEADS : 3 * HEADS],
        small[6:7, :32],
        grad_w_out[None],
    )


def solution(mesh):
    in_specs = (
        P(None, "dp", "seq", None),
        P(None, "dp", "seq", None),
        P("section", both),
        P("section", both, None),
        P("section", None, both),
        P("section", both),
        P("section", None),
        P("section", None),
        P("section", None),
        P("section", both),
        P("section", both, None),
    )
    out_specs = (
        P(None, "dp", "seq", "section"),
        P(None, "dp", "seq", "section"),
        P("section", both),
        P("section", both, None),
        P("section", None, both),
        P("section", both),
        P("section", None),
        P("section", None),
        P("section", None),
        P("section", both),
        P("section", both, None),
    )
    return jax.shard_map(shards, mesh=mesh, in_specs=in_specs, out_specs=out_specs, check_vma=False)
```
